32 devices in a mesh: seq: 8 (over z, y), mp: 4 (over x, core).
Axes of the slice: x: 2, y: 2, z: 4, core: 2. Of those that a mesh axis runs over, the one named last changes fastest.
Arguments:
- tokens: bfloat16 [8192, 1024], P('seq'), may hold values from -6 to 6
- text_states: bfloat16 [8, 128, 1024], replicated, may hold values from -6 to 6
- item_lengths: int32 [8], replicated, may hold values from 768 to 1280, as said below
- prompt_lengths: int32 [8], replicated, may hold values from 8 to 128, as said below
- entry_gain: float32 [1024], replicated, may hold values from 0.5 to 1.5
- entry_bias: float32 [1024], replicated, may hold values from -1 to 1
- cross_gain: float32 [1024], replicated, may hold values from 0.5 to 1.5
- cross_bias: float32 [1024], replicated, may hold values from -1 to 1
- mixer_gain: float32 [1024], replicated, may hold values from 0.5 to 1.5
- mixer_bias: float32 [1024], replicated, may hold values from -1 to 1
- query_weight: bfloat16 [1024, 1024], P(None, 'mp'), may hold values from -0.1875 to 0.1875
- key_weight: bfloat16 [1024, 1024], P(None, 'mp'), may hold values from -0.1875 to 0.1875
- value_weight: bfloat16 [1024, 1024], P(None, 'mp'), may hold values from -0.1875 to 0.1875
- merge_weight: bfloat16 [1024, 1024], P('mp'), may hold values from -0.75 to 0.75
- prompt_query: bfloat16 [1024, 1024], P(None, 'mp'), may hold values from -0.1875 to 0.1875
- prompt_key: bfloat16 [1024, 1024], P(None, 'mp'), may hold values from -0.1875 to 0.1875
- prompt_value: bfloat16 [1024, 1024], P(None, 'mp'), may hold values from -0.1875 to 0.1875
- prompt_merge: bfloat16 [1024, 1024], P('mp'), may hold values from -0.5 to 0.5
- expand_weight: bfloat16 [1024, 4096], P(None, 'mp'), may hold values from -0.1875 to 0.1875
- shrink_weight: bfloat16 [4096, 1024], P('mp'), may hold values from -0.09375 to 0.09375
- output_grad: bfloat16 [8192, 1024], P('seq'), may hold values from -6 to 6
Outputs:
- layer_output: bfloat16 [8192, 1024], P('seq')
- tokens_grad: float32 [8192, 1024], P('seq')
- text_grad: float32 [8, 128, 1024], P(None, None, 'mp')
- entry_gain_grad: float32 [1024], P('seq')
- entry_bias_grad: float32 [1024], P('seq')
- cross_gain_grad: float32 [1024], P('seq')
- cross_bias_grad: float32 [1024], P('seq')
- mixer_gain_grad: float32 [1024], P('seq')
- mixer_bias_grad: float32 [1024], P('seq')
- query_weight_grad: float32 [1024, 1024], P('seq', 'mp')
- key_weight_grad: float32 [1024, 1024], P('seq', 'mp')
- value_weight_grad: float32 [1024, 1024], P('seq', 'mp')
- merge_weight_grad: float32 [1024, 1024], P('mp', 'seq')
- prompt_query_grad: float32 [1024, 1024], P('seq', 'mp')
- prompt_key_grad: float32 [1024, 1024], P(None, 'mp')
- prompt_value_grad: float32 [1024, 1024], P(None, 'mp')
- prompt_merge_grad: float32 [1024, 1024], P('mp', 'seq')
- expand_weight_grad: float32 [1024, 4096], P('seq', 'mp')
- shrink_weight_grad: float32 [4096, 1024], P('mp', 'seq')
The draws below stay inside these ranges and needn't reach their ends.
Inputs may be any that keep to these rules, and one draw needn't show every extreme that they name: `item_lengths`: the lengths sum to 8192; some item has exactly 1280 tokens and some exactly 768. `prompt_lengths`: some item has exactly 128 live text positions and some exactly 8.
All inputs are finite; a program needn't handle non-finite values.
Results may differ from the reference program's by a relative error of at most 0.028.
Values may be sent and summed in bfloat16 or wider, within the bound.
No kernel may reach another device: no remote copies, remote signals or barrier semaphores. Data moves between devices by JAX's collectives and lax.ppermute only.
A program may use at most 256 MiB of HBM per device.

```python
import math
import jax
import jax.numpy as jnp
from jax import lax

D = 1024
HEADS = 16
HD = 64
FF = 4096
TL = 128
ITEM_LEN = 1024
TOKENS = 8192
ITEMS = 8


def draw_item_lengths(key, part):
    key = jax.random.fold_in(key, 5)
    jitter_key, pick_key = jax.random.split(key)
    total_items = TOKENS // ITEM_LEN
    jitter = ITEM_LEN // 8
    shifts = jax.random.randint(jitter_key, (total_items - 1,), -jitter, jitter + 1)
    chosen = jax.random.randint(pick_key, (), 1, total_items - 2)
    places = jnp.arange(total_items - 1)
    shifts = jnp.where(places == chosen - 1, -jitter, shifts)
    shifts = jnp.where(places == chosen, jitter, shifts)
    shifts = jnp.where(places == chosen + 1, -jitter, shifts)
    boundaries = (places + 1) * ITEM_LEN + shifts
    finish = jnp.concatenate([boundaries, jnp.full((1,), TOKENS, boundaries.dtype)])
    begin = jnp.concatenate([jnp.zeros((1,), boundaries.dtype), boundaries])
    return (finish - begin).astype(jnp.int32)


def draw_prompt_lengths(key, part):
    key = jax.random.fold_in(key, 11)
    base_key, order_key = jax.random.split(key)
    lengths = jax.random.randint(base_key, (ITEMS,), 8, TL + 1)
    order = jax.random.permutation(order_key, ITEMS)
    lengths = lengths.at[order[0]].set(TL)
    lengths = lengths.at[order[1]].set(8)
    return lengths.astype(jnp.int32)


def block_scale(own_key, dims, cuts, low, high):
    level, own = 1.0, jax.random.fold_in(own_key, 6)
    for dim, shards_of in cuts:
        steps = jnp.exp(jax.random.uniform(jax.random.fold_in(own, dim), (shards_of,), jnp.float32, low / len(cuts), high / len(cuts)))
        level = level * jnp.repeat(steps, dims[dim] // shards_of).reshape([-1 if axis == dim else 1 for axis in range(len(dims))])
    return level


def scatter_about(rng, shape, scale, reach, cuts=(), held_as=jnp.bfloat16):
    values = jax.random.normal(rng, shape, jnp.float32) * scale
    if len(cuts) > 0:
        values = block_scale(rng, shape, cuts, -0.22, 0.18) * values
    return jnp.clip(values, min=-reach, max=reach).astype(held_as)


def setup_inputs(seed: int = 0) -> dict:
    arg_keys = jax.random.split(jax.random.key(seed), 22)
    tokens = scatter_about(arg_keys[0], (TOKENS, D), 1.0, 6.0, ((0, 8),))
    text_states = scatter_about(arg_keys[1], (ITEMS, TL, D), 1.0, 6.0)
    item_lengths = draw_item_lengths(jax.random.fold_in(arg_keys[21], 71), 0)
    prompt_lengths = draw_prompt_lengths(jax.random.fold_in(arg_keys[21], 71), 0)
    entry_gain = jnp.clip(1.0 + 0.1 * jax.random.normal(arg_keys[4], (D,), jnp.float32), 0.5, 1.5)
    entry_bias = scatter_about(arg_keys[5], (D,), 0.2, 1.0, (), jnp.float32)
    cross_gain = jnp.clip(1.0 + 0.1 * jax.random.normal(arg_keys[6], (D,), jnp.float32), 0.5, 1.5)
    cross_bias = scatter_about(arg_keys[7], (D,), 0.2, 1.0, (), jnp.float32)
    mixer_gain = jnp.clip(1.0 + 0.1 * jax.random.normal(arg_keys[8], (D,), jnp.float32), 0.5, 1.5)
    mixer_bias = scatter_about(arg_keys[9], (D,), 0.2, 1.0, (), jnp.float32)
    query_weight = scatter_about(arg_keys[10], (D, D), D ** -0.5, 0.1875, ((1, 4),))
    key_weight = scatter_about(arg_keys[11], (D, D), D ** -0.5, 0.1875, ((1, 4),))
    value_weight = scatter_about(arg_keys[12], (D, D), D ** -0.5, 0.1875, ((1, 4),))
    merge_weight = scatter_about(arg_keys[13], (D, D), (D // 16) ** -0.5, 0.75, ((0, 4),))
    prompt_query = scatter_about(arg_keys[14], (D, D), D ** -0.5, 0.1875, ((1, 4),))
    prompt_key = scatter_about(arg_keys[15], (D, D), D ** -0.5, 0.1875, ((1, 4),))
    prompt_value = scatter_about(arg_keys[16], (D, D), D ** -0.5, 0.1875, ((1, 4),))
    prompt_merge = scatter_about(arg_keys[17], (D, D), (D // 8) ** -0.5, 0.5, ((0, 4),))
    expand_weight = scatter_about(arg_keys[18], (D, FF), D ** -0.5, 0.1875, ((1, 4),))
    shrink_weight = scatter_about(arg_keys[19], (FF, D), FF ** -0.5, 0.09375, ((0, 4),))
    output_grad = scatter_about(arg_keys[20], (TOKENS, D), 1.0, 6.0, ((0, 8),))
    return dict(tokens=tokens, text_states=text_states, item_lengths=item_lengths, prompt_lengths=prompt_lengths, entry_gain=entry_gain, entry_bias=entry_bias, cross_gain=cross_gain, cross_bias=cross_bias, mixer_gain=mixer_gain, mixer_bias=mixer_bias, query_weight=query_weight, key_weight=key_weight, value_weight=value_weight, merge_weight=merge_weight, prompt_query=prompt_query, prompt_key=prompt_key, prompt_value=prompt_value, prompt_merge=prompt_merge, expand_weight=expand_weight, shrink_weight=shrink_weight, output_grad=output_grad)


EPS = 1e-06
NEGATIVE = -1e+30

@jax.custom_vjp
def low(v):
    return lax.optimization_barrier(v.astype(jnp.bfloat16)).astype(jnp.float32)

@jax.custom_vjp
def low_back(v):
    return v

def low_keep(v):
    return (low(v), None)

def low_pass(kept, grad):
    return (grad,)

def back_keep(v):
    return (v, None)

def back_low(kept, grad):
    return (low(grad),)
low.defvjp(low_keep, low_pass)
low_back.defvjp(back_keep, back_low)

def layer_norm(values, gain, bias):
    average = lax.optimization_barrier(jnp.mean(values, axis=-1, keepdims=True))
    centred = values - average
    spread = lax.optimization_barrier(jnp.mean(centred * centred, axis=-1, keepdims=True))
    return centred * lax.rsqrt(spread + EPS) * gain + bias

def product(left, right):
    return jnp.dot(left, right, precision=lax.Precision.HIGHEST)

def split_heads(values):
    return values.reshape(values.shape[0], HEADS, HD).transpose(1, 0, 2)

def block_softmax(query_block, key_block, value_block, allowed):
    scores = low_back(product(query_block, key_block.T) * HD ** (-0.5))
    scores = jnp.where(allowed, scores, NEGATIVE)
    maxima = lax.optimization_barrier(jnp.max(scores, axis=1, keepdims=True))
    unnorm = jnp.where(allowed, jnp.exp(scores - maxima), 0.0)
    probs = low(unnorm / lax.optimization_barrier(jnp.sum(unnorm, axis=1, keepdims=True)))
    return product(probs, value_block)

def self_attend(queries, keys, values, start_of):
    head_count, all_rows, width = queries.shape
    block_rows = math.gcd(512, all_rows)
    block_count = all_rows // block_rows
    span = ITEM_LEN + ITEM_LEN // 4
    filler = jnp.zeros((head_count, span, width), keys.dtype)
    keys_padded = jnp.concatenate([filler, keys], axis=1)
    values_padded = jnp.concatenate([filler, values], axis=1)
    query_blocks = queries.reshape(head_count * block_count, block_rows, width)
    head_ids = jnp.repeat(jnp.arange(head_count).astype(jnp.int32), block_count)
    block_ids = jnp.tile(jnp.arange(block_count).astype(jnp.int32), head_count)
    anchor = jnp.zeros((), jnp.int32)

    def single(inputs):
        query_block, head_id, block_id = inputs
        first = (block_id * block_rows).astype(jnp.int32)
        key_block = lax.dynamic_slice(keys_padded, (head_id, first, anchor), (1, span + block_rows, width))[0]
        value_block = lax.dynamic_slice(values_padded, (head_id, first, anchor), (1, span + block_rows, width))[0]
        rows = (first + jnp.arange(block_rows).astype(jnp.int32)).astype(jnp.int32)
        columns = (first - span + jnp.arange(span + block_rows).astype(jnp.int32)).astype(jnp.int32)
        row_starts = start_of[rows]
        allowed = (columns[None, :] <= rows[:, None]) & (columns[None, :] >= row_starts[:, None])
        return block_softmax(query_block, key_block, value_block, allowed)
    result = lax.map(jax.checkpoint(single), (query_blocks, head_ids, block_ids))
    return result.reshape(head_count, all_rows, width).transpose(1, 0, 2).reshape(all_rows, head_count * width)

def cross_attend(queries, keys, values, item_of, key_item, live):
    head_count, all_rows, width = queries.shape
    block_rows = math.gcd(512, all_rows)
    block_count = all_rows // block_rows
    query_blocks = queries.reshape(head_count * block_count, block_rows, width)
    head_ids = jnp.repeat(jnp.arange(head_count).astype(jnp.int32), block_count)
    block_ids = jnp.tile(jnp.arange(block_count).astype(jnp.int32), head_count)

    def single(inputs):
        query_block, head_id, block_id = inputs
        key_head = lax.dynamic_index_in_dim(keys, head_id, 0, keepdims=False)
        value_head = lax.dynamic_index_in_dim(values, head_id, 0, keepdims=False)
        rows = (block_id * block_rows + jnp.arange(block_rows).astype(jnp.int32)).astype(jnp.int32)
        allowed = (key_item[None, :] == item_of[rows][:, None]) & live[None, :]
        return block_softmax(query_block, key_head, value_head, allowed)
    result = lax.map(jax.checkpoint(single), (query_blocks, head_ids, block_ids))
    return result.reshape(head_count, all_rows, width).transpose(1, 0, 2).reshape(all_rows, head_count * width)

def reference(tokens, text_states, item_lengths, prompt_lengths, entry_gain, entry_bias, cross_gain, cross_bias, mixer_gain, mixer_bias, query_weight, key_weight, value_weight, merge_weight, prompt_query, prompt_key, prompt_value, prompt_merge, expand_weight, shrink_weight, output_grad):
    all_rows = tokens.shape[0]
    positions = jnp.arange(all_rows).astype(jnp.int32)
    item_ends = jnp.cumsum(item_lengths).astype(jnp.int32)
    item_starts = (item_ends - item_lengths).astype(jnp.int32)
    item_of = lax.optimization_barrier(jnp.sum((positions[:, None] >= item_ends[None, :]).astype(jnp.int32), axis=1)).astype(jnp.int32)
    start_of = item_starts[item_of]
    key_item = (jnp.arange(ITEMS * TL) // TL).astype(jnp.int32)
    live = (jnp.arange(TL).astype(jnp.int32)[None, :] < prompt_lengths[:, None]).reshape(-1)

    def forward(inputs, texts, gain_one, bias_one, gain_two, bias_two, gain_three, bias_three, w_query, w_key, w_value, w_merge, c_query, c_key, c_value, c_merge, w_expand, w_shrink):
        hidden_one = low(layer_norm(inputs, gain_one, bias_one))
        queries = low_back(low(product(hidden_one, w_query)))
        keys = low_back(low(product(hidden_one, w_key)))
        values = low_back(low(product(hidden_one, w_value)))
        self_out = self_attend(split_heads(queries), split_heads(keys), split_heads(values), start_of)
        self_low = low_back(low(self_out))
        after_self = inputs + low_back(product(self_low, w_merge))
        hidden_two = low(layer_norm(after_self, gain_two, bias_two))
        cross_queries = low_back(low(product(hidden_two, c_query)))
        flat_text = texts.reshape(ITEMS * TL, D)
        cross_keys = low_back(low(product(flat_text, c_key)))
        cross_values = low_back(low(product(flat_text, c_value)))
        cross_out = cross_attend(split_heads(cross_queries), split_heads(cross_keys), split_heads(cross_values), item_of, key_item, live)
        cross_low = low_back(low(cross_out))
        after_cross = after_self + low_back(product(cross_low, c_merge))
        hidden_three = low(layer_norm(after_cross, gain_three, bias_three))
        hidden_pre = low_back(product(hidden_three, w_expand))
        hidden_low = low(jax.nn.gelu(hidden_pre))
        return after_cross + low_back(product(hidden_low, w_shrink))
    arrays = (tokens.astype(jnp.float32), text_states.astype(jnp.float32), entry_gain, entry_bias, cross_gain, cross_bias, mixer_gain, mixer_bias, query_weight.astype(jnp.float32), key_weight.astype(jnp.float32), value_weight.astype(jnp.float32), merge_weight.astype(jnp.float32), prompt_query.astype(jnp.float32), prompt_key.astype(jnp.float32), prompt_value.astype(jnp.float32), prompt_merge.astype(jnp.float32), expand_weight.astype(jnp.float32), shrink_weight.astype(jnp.float32))
    result, pullback = jax.vjp(forward, *arrays)
    grads = pullback(output_grad.astype(jnp.float32))
    return (result.astype(jnp.bfloat16), grads[0], grads[1], grads[2], grads[3], grads[4], grads[5], grads[6], grads[7], grads[8], grads[9], grads[10], grads[11], grads[12], grads[13], grads[14], grads[15], grads[16], grads[17])
```

```python
import functools

import jax
import jax.numpy as jnp
from jax import lax
from jax.experimental import pallas as pl
from jax.experimental.pallas import tpu as pltpu
from jax.sharding import PartitionSpec as P

HD = 64
ITEM_LEN = 1024
EPS = 1e-06
NEGATIVE = -1e30
BF = jnp.bfloat16
F32 = jnp.float32
BLOCK = 256
SCALE = HD**-0.5
MIB = 1 << 20


def dot(left, right, ld, rd):
    return lax.dot_general(left, right, (((ld,), (rd,)), ((), ())), preferred_element_type=F32)


def nn(left, right):
    return dot(left, right, 1, 0)


def nt(left, right):
    return dot(left, right, 1, 1)


def tn(left, right):
    return dot(left, right, 0, 0)


def partner(value, step):
    count = lax.axis_size("mp")
    return lax.ppermute(value, "mp", [(rank, rank ^ step) for rank in range(count)])


def from_behind(value, axis, steps):
    count = lax.axis_size(axis)
    leading, last = (max(0, -steps), min(count, count - steps))
    return lax.ppermute(value, axis, [(source, source + steps) for source in range(leading, last)])


def whole(array):
    rank = len(array.shape)
    return pl.BlockSpec(array.shape, lambda *_: (0,) * rank)


def shaped(shape, dtype):
    return jax.ShapeDtypeStruct(shape, dtype)


def run(kernel, ids, args, outs, grid=(1,), in_specs=None, out_specs=None, scratch=(), flops=0, exps=0, vmem=40):
    in_specs = in_specs or [None] * len(args)
    out_specs = out_specs or [None] * len(outs)
    in_specs = [whole(a) if s is None else s for a, s in zip(args, in_specs)]
    out_specs = [whole(a) if s is None else s for a, s in zip(outs, out_specs)]
    moved = sum(a.size * a.dtype.itemsize for a in list(args) + list(outs))
    return pl.pallas_call(
        kernel,
        out_shape=outs,
        grid_spec=pltpu.PrefetchScalarGridSpec(
            num_scalar_prefetch=1,
            grid=grid,
            in_specs=in_specs,
            out_specs=out_specs,
            scratch_shapes=list(scratch),
        ),
        compiler_params=pltpu.CompilerParams(vmem_limit_bytes=vmem * MIB),
        cost_estimate=pl.CostEstimate(flops=flops, transcendentals=exps, bytes_accessed=moved),
    )(ids, *args)


def ln_rows(values):
    centred = values - jnp.mean(values, axis=-1, keepdims=True)
    spread = jnp.mean(centred * centred, axis=-1, keepdims=True)
    inverse = lax.rsqrt(spread + EPS)
    return centred * inverse, inverse


def ln_back(grad, gain, normed, inverse):
    scaled = grad * gain
    first = jnp.mean(scaled, axis=-1, keepdims=True)
    second = jnp.mean(scaled * normed, axis=-1, keepdims=True)
    return inverse * (scaled - first - normed * second)


def head_mask(head, heads):
    lanes = lax.broadcasted_iota(jnp.int32, (1, heads * HD), 1)
    return jnp.where(lanes // HD == head, 1.0, 0.0).astype(BF)


def by_head(rows, heads):
    return [rows * head_mask(head, heads) for head in range(heads)]


def entry_kernel(ids, tok, gain, bias, wq, wk, wv, hid, q, kv, tail):
    width = wq.shape[1]
    normed, _ = ln_rows(tok[...].astype(F32))
    hidden = (normed * gain[...] + bias[...]).astype(BF)
    hid[...] = hidden
    kv[:, :width] = nn(hidden, wk[...]).astype(BF)
    kv[:, width:] = nn(hidden, wv[...]).astype(BF)
    q[...] = (nn(hidden, wq[...]).astype(BF) * SCALE).astype(BF)

    @pl.when(pl.program_id(0) == pl.num_programs(0) - 1)
    def _():
        tail[...] = kv[...]


def prompt_kernel(ids, text, pk, pv, out):
    width = pk.shape[1]
    out[:, :width] = nn(text[0], pk[...]).astype(BF)
    out[:, width:] = nn(text[0], pv[...]).astype(BF)


def window_bias(key_base, query_base, begin):
    shape = (BLOCK, BLOCK)
    key = key_base + lax.broadcasted_iota(jnp.int32, shape, 0)
    query = query_base + lax.broadcasted_iota(jnp.int32, shape, 1)
    return jnp.where((key <= query) & (key >= begin), 0.0, NEGATIVE).astype(F32)


def attend_block(keys, values_t, queries, bias, top, total, acc):
    for head, query in enumerate(queries):
        scores = nt(keys, query) + bias
        before = top[head : head + 1, :]
        after = jnp.maximum(before, jnp.max(scores, axis=0, keepdims=True))
        fade = jnp.exp(before - after)
        unnorm = jnp.exp(scores - after)
        total[head : head + 1, :] = total[head : head + 1, :] * fade + jnp.sum(unnorm, axis=0, keepdims=True)
        acc[head] = acc[head] * fade + nn(values_t[head * HD : (head + 1) * HD, :], unnorm.astype(BF))
        top[head : head + 1, :] = after


def attend_local_kernel(ids, q, kv, begin, acc_o, top_o, total_o, vt, acc, top, total):
    step = pl.program_id(0)
    width = q.shape[1]
    heads = width // HD
    blocks = kv.shape[0] // BLOCK

    @pl.when(step == 0)
    def _():
        for b in range(blocks):
            vt[b] = kv[b * BLOCK : (b + 1) * BLOCK, width:].T

    queries = by_head(q[...], heads)
    top[...] = jnp.full_like(top, NEGATIVE)
    total[...] = jnp.zeros_like(total)
    acc[...] = jnp.zeros_like(acc)
    low = lax.shift_right_logical(jnp.maximum(ids[8 + step], 0), 8)

    @pl.loop(low, step + 1)
    def _(b):
        row = pl.multiple_of(b * BLOCK, BLOCK)
        bias = window_bias(row, step * BLOCK, begin[...])
        attend_block(kv[pl.ds(row, BLOCK), :width], vt[b], queries, bias, top, total, acc)

    acc_o[0] = acc[...]
    top_o[0] = top[...]
    total_o[0] = total[...]


def attend_remote_kernel(ids, q, kv, tail, begin, acc_i, top_i, total_i, out, low_out, lse, vt, acc, top, total):
    step = pl.program_id(0)
    width = q.shape[1]
    heads = width // HD
    blocks = kv.shape[0] // BLOCK

    @pl.when(step == 0)
    def _():
        vt[0] = tail[:, width:].T
        for b in range(blocks):
            vt[b + 1] = kv[b * BLOCK : (b + 1) * BLOCK, width:].T

    queries = by_head(q[...], heads)
    acc[...] = acc_i[0]
    top[...] = top_i[0]
    total[...] = total_i[0]
    span = (blocks + 1) * BLOCK
    low = lax.shift_right_logical(jnp.maximum(ids[8 + step] + span, 0), 8)

    def bias_of(b):
        return window_bias(b * BLOCK - span, step * BLOCK, begin[...])

    @pl.when(low == 0)
    def _():
        attend_block(tail[:, :width], vt[0], queries, bias_of(0), top, total, acc)

    @pl.loop(jnp.maximum(low, 1), blocks + 1)
    def _(b):
        row = pl.multiple_of((b - 1) * BLOCK, BLOCK)
        attend_block(kv[pl.ds(row, BLOCK), :width], vt[b], queries, bias_of(b), top, total, acc)

    lse[0] = top[...] + jnp.log(total[...])
    stacked = jnp.concatenate([acc[h] * (1.0 / total[h : h + 1, :]) for h in range(heads)], axis=0)
    rows = stacked.T
    out[0] = rows
    low_out[0] = rows.astype(BF)


def back_block(keys, values, keys_t, queries, grads, bias, lse, delta, dq):
    key_sum = value_sum = None
    for head, (query, grad) in enumerate(zip(queries, grads)):
        row = slice(head, head + 1)
        probs = jnp.exp(nt(keys, query) + bias - lse[row, :])
        score_grad = (probs * (nt(values, grad) - delta[row, :])).astype(BF)
        low_probs = probs.astype(BF)
        key_term = nn(score_grad, query)
        value_term = nn(low_probs, grad)
        key_sum = key_term if key_sum is None else key_sum + key_term
        value_sum = value_term if value_sum is None else value_sum + value_term
        dq[head] += nn(keys_t[head * HD : (head + 1) * HD, :], score_grad)
    return key_sum, value_sum


def back_remote_kernel(ids, q, kv, tail, begin, grad, out, lse, dkv_o, dtail_o, dq_o, delta_o, kt, dkv, dq):
    step = pl.program_id(0)
    width = q.shape[1]
    heads = width // HD
    blocks = kv.shape[0] // BLOCK

    @pl.when(step == 0)
    def _():
        dkv[...] = jnp.zeros_like(dkv)
        kt[0] = tail[:, :width].T
        for b in range(blocks):
            kt[b + 1] = kv[b * BLOCK : (b + 1) * BLOCK, :width].T

    products = (grad[0].astype(F32) * out[0]).T
    for head in range(heads):
        delta_o[0, head : head + 1, :] = jnp.sum(products[head * HD : (head + 1) * HD, :], axis=0, keepdims=True)
    dq[...] = jnp.zeros_like(dq)
    span = (blocks + 1) * BLOCK
    low = lax.shift_right_logical(jnp.maximum(ids[8 + step] + span, 0), 8)

    @pl.when(low <= blocks)
    def _():
        queries = by_head(q[...], heads)
        grads = by_head(grad[0], heads)

        def one(b, pair):
            bias = window_bias(b * BLOCK - span, step * BLOCK, begin[...])
            key_sum, value_sum = back_block(
                pair[:, :width], pair[:, width:], kt[b], queries, grads, bias, lse.at[0], delta_o.at[0], dq
            )
            dkv[b, :, :width] += key_sum
            dkv[b, :, width:] += value_sum

        @pl.when(low == 0)
        def _():
            one(0, tail[...])

        @pl.loop(jnp.maximum(low, 1), blocks + 1)
        def _(b):
            row = pl.multiple_of((b - 1) * BLOCK, BLOCK)
            one(b, kv[pl.ds(row, BLOCK), :])

    dq_o[0] = dq[...]

    @pl.when(step == pl.num_programs(0) - 1)
    def _():
        dtail_o[...] = dkv[0].astype(BF)
        for b in range(blocks):
            dkv_o[b * BLOCK : (b + 1) * BLOCK, :] = dkv[b + 1].astype(BF)


def back_local_kernel(ids, q, kv, begin, grad, lse, delta, dq_i, dkv_o, dq_o, kt, dkv, dq):
    step = pl.program_id(0)
    width = q.shape[1]
    heads = width // HD
    blocks = kv.shape[0] // BLOCK

    @pl.when(step == 0)
    def _():
        dkv[...] = jnp.zeros_like(dkv)
        for b in range(blocks):
            kt[b] = kv[b * BLOCK : (b + 1) * BLOCK, :width].T

    dq[...] = dq_i[0]
    queries = by_head(q[...], heads)
    grads = by_head(grad[0], heads)
    low = lax.shift_right_logical(jnp.maximum(ids[8 + step], 0), 8)

    @pl.loop(low, step + 1)
    def _(b):
        row = pl.multiple_of(b * BLOCK, BLOCK)
        pair = kv[pl.ds(row, BLOCK), :]
        bias = window_bias(row, step * BLOCK, begin[...])
        key_sum, value_sum = back_block(
            pair[:, :width], pair[:, width:], kt[b], queries, grads, bias, lse.at[0], delta.at[0], dq
        )
        dkv[b, :, :width] += key_sum
        dkv[b, :, width:] += value_sum

    stacked = jnp.concatenate([dq[h] for h in range(heads)], axis=0)
    dq_o[...] = (stacked.T * SCALE).astype(BF)

    @pl.when(step == pl.num_programs(0) - 1)
    def _():
        for b in range(blocks):
            dkv_o[b * BLOCK : (b + 1) * BLOCK, :] = dkv[b]


def cross_bias(ids, prompt_rows, rows):
    shape = (2 * prompt_rows, rows)
    key = lax.broadcasted_iota(jnp.int32, shape, 0)
    query = lax.broadcasted_iota(jnp.int32, shape, 1)
    key_slot = lax.shift_right_logical(key, prompt_rows.bit_length() - 1)
    query_slot = jnp.where(query >= ids[4], 1, 0)
    limit = jnp.where(key_slot == 1, prompt_rows + ids[6], ids[5])
    return jnp.where((key_slot == query_slot) & (key < limit), 0.0, NEGATIVE).astype(F32)


def cross_kernel(ids, tok, low, *refs):
    packs, pairs = refs[:4], refs[4:8]
    gain2, bias2, gain3, bias3 = refs[8:12]
    after_self_o, two_o, q_o, stat_o, out_o, after_o, three_o = refs[12:]
    rows = tok.shape[0]
    width = packs[0].shape[0] // 3
    heads = width // HD
    rank = ids[1]
    prompt_rows = pairs[0].shape[0] // 3
    after = tok[...].astype(F32)
    for d in range(4):
        after = after + nn(low[rank ^ d], packs[d][:width, :])
    after_self_o[...] = after
    normed, _ = ln_rows(after)
    hidden = (normed * gain2[...] + bias2[...]).astype(BF)
    two_o[...] = hidden
    bias = cross_bias(ids, prompt_rows, rows)
    first = pl.multiple_of(ids[3], prompt_rows)
    for d in range(4):
        columns = slice(d * width, (d + 1) * width)
        query_rows = (nt(hidden, packs[d][width : 2 * width, :]).astype(BF) * SCALE).astype(BF)
        q_o[:, columns] = query_rows
        keys = pairs[d][pl.ds(first, 2 * prompt_rows), :width]
        values_t = pairs[d][pl.ds(first, 2 * prompt_rows), width:].T
        parts = []
        for head, query in enumerate(by_head(query_rows, heads)):
            scores = nt(keys, query) + bias
            top = jnp.max(scores, axis=0, keepdims=True)
            unnorm = jnp.exp(scores - top)
            total = jnp.sum(unnorm, axis=0, keepdims=True)
            stat_o[d * heads + head : d * heads + head + 1, :] = top + jnp.log(total)
            part = nn(values_t[head * HD : (head + 1) * HD, :], unnorm.astype(BF))
            parts.append(part * (1.0 / total))
        out_o[:, columns] = jnp.concatenate(parts, axis=0).T.astype(BF)
    after = after_self_o[...]
    for d in range(4):
        after = after + nn(out_o[:, d * width : (d + 1) * width], packs[d][2 * width :, :])
    after_o[...] = after
    normed, _ = ln_rows(after)
    three_o[...] = (normed * gain3[...] + bias3[...]).astype(BF)


def cross_back_kernel(ids, kept, sent, crossed, og, after, after_self, q, stat, *refs):
    packs, pairs = refs[:4], refs[4:8]
    gain2, gain3 = refs[8:10]
    cog_o, cqg_o, slg_o, resid_o, shg_o, keep_o, send_o, norms_o = refs[10:]
    rows, model = after.shape
    width = packs[0].shape[0] // 3
    heads = width // HD
    rank = ids[1]
    prompt_rows = pairs[0].shape[0] // 3
    grad = kept[...].astype(F32) + sent[...].astype(F32) + crossed[...].astype(F32)
    normed, inverse = ln_rows(after[...])
    norms_o[0:1, :] = jnp.sum(grad * normed, axis=0, keepdims=True)
    norms_o[1:2, :] = jnp.sum(grad, axis=0, keepdims=True)
    resid = og[...].astype(F32) + ln_back(grad, gain3[...], normed, inverse)
    low_resid = resid.astype(BF)
    cog_o[...] = low_resid
    bias = cross_bias(ids, prompt_rows, rows)
    first = pl.multiple_of(ids[3], prompt_rows)
    keep_o[...] = jnp.zeros_like(keep_o)
    send_o[...] = jnp.zeros_like(send_o)
    for d in range(4):
        columns = slice(d * width, (d + 1) * width)
        head_grad = nt(low_resid, packs[d][2 * width :, :]).astype(BF)
        keys = pairs[d][pl.ds(first, 2 * prompt_rows), :width]
        values = pairs[d][pl.ds(first, 2 * prompt_rows), width:]
        keys_t = keys.T
        key_sum = value_sum = None
        parts = []
        for head, (query, out_grad) in enumerate(zip(by_head(q[:, columns], heads), by_head(head_grad, heads))):
            row = slice(d * heads + head, d * heads + head + 1)
            probs = jnp.exp(nt(keys, query) + bias - stat[row, :])
            prob_grad = nt(values, out_grad)
            delta = jnp.sum(probs * prob_grad, axis=0, keepdims=True)
            score_grad = (probs * (prob_grad - delta)).astype(BF)
            key_term = nn(score_grad, query)
            value_term = nn(probs.astype(BF), out_grad)
            key_sum = key_term if key_sum is None else key_sum + key_term
            value_sum = value_term if value_sum is None else value_sum + value_term
            parts.append(nn(keys_t[head * HD : (head + 1) * HD, :], score_grad))
        cqg_o[:, columns] = (jnp.concatenate(parts, axis=0).T * SCALE).astype(BF)
        target = keep_o if d % 2 == 0 else send_o
        target[d // 2, pl.ds(first, 2 * prompt_rows), :width] = key_sum.astype(BF)
        target[d // 2, pl.ds(first, 2 * prompt_rows), width:] = value_sum.astype(BF)
    two_grad = None
    for d in range(4):
        term = nn(cqg_o[:, d * width : (d + 1) * width], packs[d][width : 2 * width, :])
        two_grad = term if two_grad is None else two_grad + term
    normed, inverse = ln_rows(after_self[...])
    norms_o[2:3, :] = jnp.sum(two_grad * normed, axis=0, keepdims=True)
    norms_o[3:4, :] = jnp.sum(two_grad, axis=0, keepdims=True)
    resid = resid + ln_back(two_grad, gain2[...], normed, inverse)
    resid_o[...] = resid
    low_resid = resid.astype(BF)
    slg_o[...] = low_resid
    for d in range(4):
        shg_o[rank ^ d] = nt(low_resid, packs[d][:width, :]).astype(BF)


def feed_kernel(ids, h_a, h_b, dh_a, dh_b, expand, shrink, *refs):
    outs, accs = refs[:8], refs[8:]
    last = pl.num_programs(0) - 1
    c = 0.7978845608028654
    for side, (h, dh) in enumerate(((h_a, dh_a), (h_b, dh_b))):
        low_o, pre_o, out_o, three_o = outs[4 * side : 4 * side + 4]
        out_s, three_s = accs[2 * side : 2 * side + 2]
        v = nn(h[...], expand[...])
        square = v * v
        t = jnp.tanh(c * v * (1.0 + 0.044715 * square))
        half = 0.5 * (1.0 + t)
        low = (v * half).astype(BF)
        slope = half + 0.5 * v * (1.0 - t * t) * (c * (1.0 + 3 * 0.044715 * square))
        pre = (dh[...].astype(F32) * slope).astype(BF)
        low_o[...] = low
        pre_o[...] = pre
        out_part = nn(low, shrink[...])
        three_part = nt(pre, expand[...])

        @pl.when(pl.program_id(0) == 0)
        def _():
            out_s[...] = out_part
            three_s[...] = three_part

        @pl.when(pl.program_id(0) > 0)
        def _():
            out_s[...] += out_part
            three_s[...] += three_part

        @pl.when(pl.program_id(0) == last)
        def _():
            out_o[...] = out_s[...].astype(BF)
            three_o[...] = three_s[...].astype(BF)


def feed(ids, base, h_a, h_b, dh, expand, shrink):
    rows, model = h_a.shape
    hidden = expand.shape[1]
    chunk = 256
    row_block = lambda d: pl.BlockSpec((rows, chunk), lambda j, s: (s[1] ^ d, j))
    column = pl.BlockSpec((rows, chunk), lambda j, s: (0, j))
    full = pl.BlockSpec((rows, model), lambda j, s: (0, 0))
    return run(
        feed_kernel,
        ids,
        (h_a, h_b, dh, dh, expand, shrink),
        [shaped((rows, hidden), BF), shaped((rows, hidden), BF), shaped((rows, model), BF), shaped((rows, model), BF)] * 2,
        grid=(hidden // chunk,),
        in_specs=[
            full,
            full,
            row_block(base),
            row_block(base + 1),
            pl.BlockSpec((model, chunk), lambda j, s: (0, j)),
            pl.BlockSpec((chunk, model), lambda j, s: (j, 0)),
        ],
        out_specs=[column, column, full, full] * 2,
        scratch=[pltpu.VMEM((rows, model), F32)] * 4,
        flops=2 * 2 * 3 * rows * model * hidden,
        exps=2 * rows * hidden,
    )


def feed_weights_kernel(ids, *refs):
    threes, pres, lows = refs[:4], refs[4:8], refs[8:12]
    og, out, turned = refs[12:]
    step = pl.program_id(0)
    half = pl.num_programs(0) // 2
    rank = ids[1]
    rows = threes[0].shape[0]

    @pl.when(step == 0)
    def _():
        for d in range(4):
            turned[:, d * rows : (d + 1) * rows] = threes[d][...].T

    @pl.when(step == half)
    def _():
        for d in range(4):
            turned[:, d * rows : (d + 1) * rows] = og[pl.ds(pl.multiple_of((rank ^ d) * rows, rows), rows), :].T

    @pl.when(step < half)
    def _():
        out[...] = nn(turned[...], jnp.concatenate([p[...] for p in pres], axis=0)).astype(BF)

    @pl.when(step >= half)
    def _():
        out[...] = nn(turned[...], jnp.concatenate([p[...] for p in lows], axis=0)).astype(BF)


def feed_weights(ids, threes, pres, lows, og):
    rows, model = threes[0].shape
    hidden = pres[0].shape[1]
    chunk = 256
    half = hidden // chunk
    front = pl.BlockSpec((rows, chunk), lambda j, s: (0, jnp.minimum(j, half - 1)))
    back = pl.BlockSpec((rows, chunk), lambda j, s: (0, jnp.maximum(j - half, 0)))
    return run(
        feed_weights_kernel,
        ids,
        (*threes, *pres, *lows, og),
        [shaped((model, 2 * hidden), BF)],
        grid=(2 * half,),
        in_specs=[None] * 4 + [front] * 4 + [back] * 4 + [None],
        out_specs=[pl.BlockSpec((model, chunk), lambda j, s: (0, j))],
        scratch=[pltpu.VMEM((model, 4 * rows), BF)],
        flops=2 * 2 * 4 * rows * model * hidden,
    )[0]


def head_weights_kernel(ids, two, cqg, cog, crossed, slg, low, keep, send, turned):
    step = pl.program_id(0)
    rank = ids[1]
    width = low.shape[2]

    @pl.when(step == 0)
    def _():
        turned[0] = two[...].T
        turned[1] = cog[...].T
        turned[2] = slg[...].T

    for side, out in enumerate((keep, send)):
        columns = pl.ds(pl.multiple_of((2 * step + side) * width, width), width)
        out[0, :, :width] = nn(turned[0], cqg[:, columns]).astype(BF)
        out[0, :, width : 2 * width] = nn(turned[1], crossed[:, columns]).astype(BF)
        out[0, :, 2 * width :] = nn(turned[2], low[rank ^ (2 * step + side)]).astype(BF)


def key_sum_kernel(ids, dkv, near, far, hid, dq, wq, wk, wv, gain, bias, kvg_o, keep, send, norms):
    rows, width2 = dkv.shape
    width = width2 // 2
    quarter = rows // 4
    rank = ids[1]
    kvg_o[: rows - BLOCK, :] = (dkv[: rows - BLOCK, :] + near[: rows - BLOCK, :].astype(F32)).astype(BF)
    kvg_o[rows - BLOCK :, :] = (
        dkv[rows - BLOCK :, :] + near[rows - BLOCK :, :].astype(F32) + far[...].astype(F32)
    ).astype(BF)
    product = total = None
    for d in (1, 3, 2, 0):
        own = pl.ds(pl.multiple_of((rank ^ d) * quarter, quarter), quarter)
        part = (
            nt(dq[own, :], wq[...]) + nt(kvg_o[own, :width], wk[...]) + nt(kvg_o[own, width:], wv[...])
        )
        hidden = hid[own, :].astype(F32)
        term = jnp.sum(part * hidden, axis=0, keepdims=True)
        plain = jnp.sum(part, axis=0, keepdims=True)
        product = term if product is None else product + term
        total = plain if total is None else total + plain
        target = keep if d % 2 == 0 else send
        target[d // 2] = part.astype(BF)
    norms[0:1, :] = (product - bias[...] * total) / gain[...]
    norms[1:2, :] = total


def entry_back_kernel(ids, keep, sent, crossed, tok, gain, resid, out):
    grad = keep[0].astype(F32) + sent[0].astype(F32) + crossed[...].astype(F32)
    normed, inverse = ln_rows(tok[...].astype(F32))
    out[...] = (resid[...] + ln_back(grad, gain[...], normed, inverse)).astype(BF)


def assemble_kernel(ids, *refs):
    out = refs[4]
    for d in range(4):

        @pl.when(pl.program_id(0) == ids[1] ^ d)
        def _():
            out[...] = refs[d][...].astype(out.dtype)


def assemble(ids, pieces, dtype):
    rows, model = pieces[0].shape
    return run(
        assemble_kernel,
        ids,
        pieces,
        [shaped((4 * rows, model), dtype)],
        grid=(4,),
        out_specs=[pl.BlockSpec((rows, model), lambda i, s: (i, 0))],
    )[0]


def gather(own):
    across = partner(own, 2)
    near = partner(own, 1)
    return own, near, across, partner(across, 1)


def sum_rows(blocks):
    return jnp.sum(blocks.astype(F32), axis=0)


def body(
    tokens,
    text_states,
    item_lengths,
    prompt_lengths,
    entry_gain,
    entry_bias,
    cross_gain,
    cross_bias_,
    mixer_gain,
    mixer_bias,
    query_weight,
    key_weight,
    value_weight,
    merge_weight,
    prompt_query,
    prompt_key,
    prompt_value,
    prompt_merge,
    expand_weight,
    shrink_weight,
    output_grad,
):
    rows, model = tokens.shape
    shards = lax.axis_size("seq")
    ranks = lax.axis_size("mp")
    width = query_weight.shape[1]
    heads = width // HD
    items, prompt_rows = text_states.shape[:2]
    quarter = rows // ranks
    steps = rows // BLOCK
    hidden_units = expand_weight.shape[1]
    assert ranks == 4 and quarter == BLOCK

    rank = lax.axis_index("mp")
    offset = lax.axis_index("seq") * rows
    ends = jnp.cumsum(item_lengths)
    starts = ends - item_lengths
    positions = jnp.arange(rows, dtype=jnp.int32) + offset

    def begin_of(where):
        return jnp.max(jnp.where(starts[None, :] <= where[:, None], starts[None, :], 0), axis=1)

    begin = (begin_of(positions) - offset)[None, :]
    lows = begin_of(offset + BLOCK * jnp.arange(steps, dtype=jnp.int32)) - offset
    base = jnp.minimum(jnp.sum((ends <= offset).astype(jnp.int32)), items - 3)
    own_first = offset + rank * quarter
    own_base = jnp.minimum(jnp.sum((ends <= own_first).astype(jnp.int32)), items - 2)
    numbers = jnp.arange(items, dtype=jnp.int32)

    def at(values, index):
        return jnp.sum(jnp.where(numbers == index, values, 0))

    ids = jnp.stack(
        [
            lax.axis_index("seq"),
            rank,
            base,
            (own_base - base) * prompt_rows,
            at(ends, own_base) - own_first,
            at(prompt_lengths, own_base),
            at(prompt_lengths, own_base + 1),
            jnp.zeros_like(rank),
        ]
    )
    ids = jnp.concatenate([ids, lows]).astype(jnp.int32)

    row = lambda vector: vector.reshape(1, -1)
    own_rows = lambda columns: pl.BlockSpec((quarter, columns), lambda *g: (g[-1][1], 0))

    block_rows = lambda columns: pl.BlockSpec((BLOCK, columns), lambda i, s: (i, 0))
    hidden_one, q, kv, kv_tail = run(
        entry_kernel,
        ids,
        (tokens, row(entry_gain), row(entry_bias), query_weight, key_weight, value_weight),
        [shaped((rows, model), BF), shaped((rows, width), BF), shaped((rows, 2 * width), BF), shaped((BLOCK, 2 * width), BF)],
        grid=(steps,),
        in_specs=[block_rows(model)] + [None] * 5,
        out_specs=[block_rows(model), block_rows(width), block_rows(2 * width), None],
        flops=6 * rows * model * width,
    )
    kv_near = from_behind(kv, "seq", 1)
    kv_far = from_behind(kv_tail, "seq", 2)

    pack = jnp.concatenate([merge_weight, prompt_query.T, prompt_merge], axis=0)
    pair = run(
        prompt_kernel,
        ids,
        (text_states, prompt_key, prompt_value),
        [shaped((3 * prompt_rows, 2 * width), BF)],
        grid=(3,),
        in_specs=[pl.BlockSpec((1, prompt_rows, model), lambda i, s: (s[2] + i, 0, 0)), None, None],
        out_specs=[pl.BlockSpec((prompt_rows, 2 * width), lambda i, s: (i, 0))],
        flops=4 * 3 * prompt_rows * model * width,
    )[0]
    packs = gather(pack)
    pairs = gather(pair)
    hidden_grad = nt(output_grad, shrink_weight).astype(BF)

    state = [shaped((steps, heads, HD, BLOCK), F32), shaped((steps, heads, BLOCK), F32), shaped((steps, heads, BLOCK), F32)]
    state_specs = [
        pl.BlockSpec((1, heads, HD, BLOCK), lambda i, s: (i, 0, 0, 0)),
        pl.BlockSpec((1, heads, BLOCK), lambda i, s: (i, 0, 0)),
        pl.BlockSpec((1, heads, BLOCK), lambda i, s: (i, 0, 0)),
    ]
    state_scratch = [pltpu.VMEM((heads, HD, BLOCK), F32), pltpu.VMEM((heads, BLOCK), F32), pltpu.VMEM((heads, BLOCK), F32)]
    q_spec = block_rows(width)
    begin_spec = pl.BlockSpec((1, BLOCK), lambda i, s: (0, i))
    piece_spec = pl.BlockSpec((1, BLOCK, width), lambda i, s: (i, 0, 0))
    turned = lambda blocks: pltpu.VMEM((blocks, width, BLOCK), BF)
    pair_flops = 2 * heads * BLOCK * BLOCK * width
    acc, top, total = run(
        attend_local_kernel,
        ids,
        (q, kv, begin),
        state,
        grid=(steps,),
        in_specs=[q_spec, None, begin_spec],
        out_specs=state_specs,
        scratch=[turned(steps)] + state_scratch,
        flops=2 * pair_flops * 10,
        exps=heads * BLOCK * BLOCK * 10,
    )
    self_out, self_low, lse = run(
        attend_remote_kernel,
        ids,
        (q, kv_near, kv_far, begin, acc, top, total),
        [shaped((steps, BLOCK, width), F32), shaped((steps, BLOCK, width), BF), shaped((steps, heads, BLOCK), F32)],
        grid=(steps,),
        in_specs=[q_spec, None, None, begin_spec] + state_specs,
        out_specs=[piece_spec, piece_spec, state_specs[1]],
        scratch=[turned(steps + 1)] + state_scratch,
        flops=2 * pair_flops * 10,
        exps=heads * BLOCK * BLOCK * 10,
    )
    low_rows = lax.all_to_all(self_low, "mp", 0, 0)

    wide = lambda dtype: shaped((quarter, model), dtype)
    stat_shape = shaped((ranks * heads, quarter), F32)
    norms = (row(cross_gain), row(cross_bias_), row(mixer_gain), row(mixer_bias))
    after_self, hidden_two, cross_q, stat, cross_out, after_cross, hidden_three = run(
        cross_kernel,
        ids,
        (tokens, low_rows, *packs, *pairs, *norms),
        [wide(F32), wide(BF), wide(BF), stat_shape, wide(BF), wide(F32), wide(BF)],
        in_specs=[own_rows(model)] + [None] * 13,
        flops=6 * quarter * model * model + 4 * ranks * pair_flops,
        exps=ranks * heads * BLOCK * BLOCK,
    )

    threes = gather(hidden_three)
    low0, pre0, out0, part0, low1, pre1, out1, part1 = feed(ids, 0, threes[0], threes[1], hidden_grad, expand_weight, shrink_weight)
    low2, pre2, out2, part2, low3, pre3, out3, part3 = feed(ids, 2, threes[2], threes[3], hidden_grad, expand_weight, shrink_weight)
    sent1 = partner(part1, 1)
    across = partner((part2.astype(F32) + partner(part3, 1).astype(F32)).astype(BF), 2)

    feed_grads = feed_weights(ids, threes, (pre0, pre1, pre2, pre3), (low0, low1, low2, low3), output_grad)
    feed_sum = lax.psum_scatter(feed_grads, "seq", scatter_dimension=0, tiled=True)

    pair_out = shaped((2, 3 * prompt_rows, 2 * width), BF)
    cog, cqg, slg, resid, shg, pair_keep, pair_send, norm_grads = run(
        cross_back_kernel,
        ids,
        (part0, sent1, across, output_grad, after_cross, after_self, cross_q, stat, *packs, *pairs, norms[0], norms[2]),
        [wide(BF), wide(BF), wide(BF), wide(F32), shaped((ranks, quarter, width), BF), pair_out, pair_out, shaped((4, model), F32)],
        in_specs=[None] * 3 + [own_rows(model)] + [None] * 14,
        flops=6 * quarter * model * model + 10 * ranks * pair_flops,
        exps=ranks * heads * BLOCK * BLOCK,
        vmem=48,
    )
    self_grad = lax.all_to_all(shg, "mp", 0, 0)

    out_across = partner((out2.astype(F32) + partner(out3, 1).astype(F32)).astype(BF), 2)
    out_rows = (
        after_cross + out0.astype(F32) + partner(out1, 1).astype(F32) + out_across.astype(F32)
    ).astype(BF)
    layer_output = assemble(ids, gather(out_rows), BF)

    pieces = shaped((2, model, 3 * width), BF)
    piece_out = pl.BlockSpec((1, model, 3 * width), lambda i, s: (i, 0, 0))
    head_keep, head_send = run(
        head_weights_kernel,
        ids,
        (hidden_two, cqg, cog, cross_out, slg, low_rows),
        [pieces, pieces],
        grid=(2,),
        out_specs=[piece_out, piece_out],
        scratch=[pltpu.VMEM((3, model, quarter), BF)],
        flops=6 * quarter * model * model,
    )

    def over_ranks(keep, send):
        sent = partner(send, 1).astype(F32) + keep.astype(F32)
        return (sent[0] + partner(sent[1].astype(BF), 2).astype(F32)).astype(BF)

    def over_shards(blocks):
        return sum_rows(lax.all_to_all(blocks.reshape(shards, -1, blocks.shape[-1]), "seq", 0, 0))

    head_sum = over_shards(over_ranks(head_keep, head_send))

    pair_sum = over_ranks(pair_keep, pair_send).reshape(3, prompt_rows, 2 * width)
    placed = lax.dynamic_update_slice_in_dim(jnp.zeros((items, prompt_rows, 2 * width), BF), pair_sum, base, 0)
    own_pair = over_shards(placed.reshape(items * prompt_rows, 2 * width)).astype(BF)
    pair_grad = lax.all_gather(own_pair, "seq", axis=0, tiled=True)
    flat_text = text_states.reshape(items * prompt_rows, model)
    prompt_grads = tn(flat_text, pair_grad)
    text_part = nt(own_pair[:, :width], prompt_key) + nt(own_pair[:, width:], prompt_value)
    text_blocks = jnp.swapaxes(text_part.astype(BF).reshape(-1, ranks, width), 0, 1)
    text_own = sum_rows(lax.all_to_all(text_blocks, "mp", 0, 0)).astype(BF)
    text_grad = lax.all_gather(text_own, "seq", axis=0, tiled=True).astype(F32).reshape(items, prompt_rows, width)

    lse_spec = state_specs[1]
    stat4 = shaped((steps, heads, BLOCK), F32)
    dkv_near, dkv_far, dq_part, delta = run(
        back_remote_kernel,
        ids,
        (q, kv_near, kv_far, begin, self_grad, self_out, lse),
        [shaped((rows, 2 * width), BF), shaped((BLOCK, 2 * width), BF), state[0], stat4],
        grid=(steps,),
        in_specs=[q_spec, None, None, begin_spec, piece_spec, piece_spec, lse_spec],
        out_specs=[None, None, state_specs[0], lse_spec],
        scratch=[turned(steps + 1), pltpu.VMEM((steps + 1, BLOCK, 2 * width), F32), state_scratch[0]],
        flops=5 * pair_flops * 10,
        exps=heads * BLOCK * BLOCK * 10,
    )
    from_near = from_behind(dkv_near, "seq", -1)
    from_far = from_behind(dkv_far, "seq", -2)
    dkv, dq = run(
        back_local_kernel,
        ids,
        (q, kv, begin, self_grad, lse, delta, dq_part),
        [shaped((rows, 2 * width), F32), shaped((rows, width), BF)],
        grid=(steps,),
        in_specs=[q_spec, None, begin_spec, piece_spec, lse_spec, lse_spec, state_specs[0]],
        out_specs=[None, q_spec],
        scratch=[turned(steps), pltpu.VMEM((steps, BLOCK, 2 * width), F32), state_scratch[0]],
        flops=5 * pair_flops * 10,
        exps=heads * BLOCK * BLOCK * 10,
    )

    two_quarters = shaped((2, quarter, model), BF)
    kvg, one_keep, one_send, entry_norms = run(
        key_sum_kernel,
        ids,
        (dkv, from_near, from_far, hidden_one, dq, query_weight, key_weight, value_weight, row(entry_gain), row(entry_bias)),
        [shaped((rows, 2 * width), BF), two_quarters, two_quarters, shaped((2, model), F32)],
        flops=6 * rows * model * width,
    )
    one_sent = partner(one_send, 1)
    one_across = partner((one_keep[1].astype(F32) + one_sent[1].astype(F32)).astype(BF), 2)
    grad_rows = run(
        entry_back_kernel,
        ids,
        (one_keep, one_sent, one_across, tokens, row(entry_gain), resid),
        [wide(BF)],
        in_specs=[None] * 3 + [own_rows(model)] + [None] * 2,
    )[0]
    tokens_grad = assemble(ids, gather(grad_rows), F32)

    entry_grads = jnp.concatenate([tn(hidden_one, dq), tn(hidden_one, kvg)], axis=1).astype(BF)
    entry_sum = over_shards(entry_grads)

    norm_rows = jnp.concatenate([entry_norms, norm_grads[2:4], norm_grads[0:2], jnp.zeros((2, model), F32)])
    norm_blocks = jnp.swapaxes(norm_rows.reshape(8, shards, model // shards), 0, 1)
    norm_sum = jnp.sum(lax.all_to_all(norm_blocks, "seq", 0, 0), axis=0)
    norm_sum = norm_sum + partner(norm_sum, 1)
    norm_sum = norm_sum + partner(norm_sum, 2)

    cut = lambda array, index: array[:, index * width : (index + 1) * width]
    feed_sum = feed_sum.astype(F32)
    return (
        layer_output,
        tokens_grad,
        text_grad,
        norm_sum[0],
        norm_sum[1],
        norm_sum[2],
        norm_sum[3],
        norm_sum[4],
        norm_sum[5],
        cut(entry_sum, 0),
        cut(entry_sum, 1),
        cut(entry_sum, 2),
        cut(head_sum, 2).T,
        cut(head_sum, 0),
        prompt_grads[:, :width],
        prompt_grads[:, width:],
        cut(head_sum, 1).T,
        feed_sum[:, :hidden_units],
        feed_sum[:, hidden_units:].T,
    )


def solution(mesh):
    seq, mp, both = P("seq", None), P("mp", None), P(None, "mp")
    return jax.shard_map(
        body,
        mesh=mesh,
        in_specs=(seq,) + (P(),) * 9 + (both,) * 3 + (mp,) + (both,) * 3 + (mp, both, mp, seq),
        out_specs=(
            (seq, seq, P(None, None, "mp"))
            + (P("seq"),) * 6
            + (P("seq", "mp"),) * 3
            + (P("mp", "seq"), P("seq", "mp"), both, both, P("mp", "seq"), P("seq", "mp"), P("mp", "seq"))
        ),
        check_vma=False,
    )
```

```python
import functools

import jax
import jax.numpy as jnp
from jax import lax
from jax.experimental import pallas as pl
from jax.experimental.pallas import tpu as pltpu
from jax.sharding import PartitionSpec as P

HD = 64
ITEM_LEN = 1024
EPS = 1e-06
NEGATIVE = -1e30
BF = jnp.bfloat16
F32 = jnp.float32
BLOCK = 256
SCALE = HD**-0.5
MIB = 1 << 20


def dot(left, right, ld, rd):
    return lax.dot_general(left, right, (((ld,), (rd,)), ((), ())), preferred_element_type=F32)


def nn(left, right):
    return dot(left, right, 1, 0)


def nt(left, right):
    return dot(left, right, 1, 1)


def tn(left, right):
    return dot(left, right, 0, 0)


def partner(value, step):
    count = lax.axis_size("mp")
    return lax.ppermute(value, "mp", [(rank, rank ^ step) for rank in range(count)])


SEQ = ("far", "near")


def from_behind(value, steps):
    count = lax.axis_size("far") * lax.axis_size("near")
    leading, last = (max(0, -steps), min(count, count - steps))
    return lax.ppermute(value, SEQ, [(source, source + steps) for source in range(leading, last)])


def other_near(value):
    return lax.ppermute(value, "near", [(0, 1), (1, 0)])


def over_shards(blocks):
    far = lax.axis_size("far")
    parts = blocks.reshape(far, 2, -1, blocks.shape[-1])
    own = lax.axis_index("near")
    sent = other_near(lax.dynamic_index_in_dim(parts, 1 - own, 1, keepdims=False))
    kept = lax.dynamic_index_in_dim(parts, own, 1, keepdims=False)
    half = (kept.astype(F32) + sent.astype(F32)).astype(BF)
    return sum_rows(lax.all_to_all(half, "far", 0, 0))


def from_shards(own):
    far = lax.axis_size("far")
    mine = lax.all_to_all(jnp.broadcast_to(own[None], (far, *own.shape)), "far", 0, 0)
    other = other_near(mine)
    first = lax.axis_index("near") == 0
    both = jnp.stack([jnp.where(first, mine, other), jnp.where(first, other, mine)], axis=1)
    return both.reshape(-1, own.shape[-1])


def whole(array):
    rank = len(array.shape)
    return pl.BlockSpec(array.shape, lambda *_: (0,) * rank)


def shaped(shape, dtype):
    return jax.ShapeDtypeStruct(shape, dtype)


def run(kernel, ids, args, outs, grid=(1,), in_specs=None, out_specs=None, scratch=(), micros=1, vmem=40):
    in_specs = in_specs or [None] * len(args)
    out_specs = out_specs or [None] * len(outs)
    in_specs = [whole(a) if s is None else s for a, s in zip(args, in_specs)]
    out_specs = [whole(a) if s is None else s for a, s in zip(outs, out_specs)]
    moved = sum(a.size * a.dtype.itemsize for a in list(args) + list(outs))
    prefetch = () if ids is None else (ids,)
    return pl.pallas_call(
        functools.partial(kernel, None) if ids is None else kernel,
        out_shape=outs,
        grid_spec=pltpu.PrefetchScalarGridSpec(
            num_scalar_prefetch=len(prefetch),
            grid=grid,
            in_specs=in_specs,
            out_specs=out_specs,
            scratch_shapes=list(scratch),
        ),
        compiler_params=pltpu.CompilerParams(vmem_limit_bytes=vmem * MIB),
        cost_estimate=pl.CostEstimate(flops=int(micros * 1e6), transcendentals=0, bytes_accessed=1000),
    )(*prefetch, *args)


def after(value, *others):
    return lax.optimization_barrier((value, *others))[0]


def ln_rows(values):
    centred = values - jnp.mean(values, axis=-1, keepdims=True)
    spread = jnp.mean(centred * centred, axis=-1, keepdims=True)
    inverse = lax.rsqrt(spread + EPS)
    return centred * inverse, inverse


def ln_back(grad, gain, normed, inverse):
    scaled = grad * gain
    first = jnp.mean(scaled, axis=-1, keepdims=True)
    second = jnp.mean(scaled * normed, axis=-1, keepdims=True)
    return inverse * (scaled - first - normed * second)


def head_mask(head, heads):
    lanes = lax.broadcasted_iota(jnp.int32, (1, heads * HD), 1)
    return jnp.where(lanes // HD == head, 1.0, 0.0).astype(BF)


def by_head(rows, heads):
    return [rows * head_mask(head, heads) for head in range(heads)]


def layout_kernel(rows, lens, prompts, place, ids, begin):
    items = lens.shape[0]
    offset = place[0] * rows
    own_first = offset + place[1] * (rows // 4)
    positions = offset + lax.broadcasted_iota(jnp.int32, (1, rows), 1)
    found = jnp.zeros((1, rows), jnp.int32)
    lows = [jnp.int32(0)] * (rows // BLOCK)
    begun = base = own_base = jnp.int32(0)
    for item in range(items):
        found = jnp.where(positions >= begun, begun, found)
        lows = [jnp.where(offset + block * BLOCK >= begun, begun, low) for block, low in enumerate(lows)]
        begun = begun + lens[item]
        base = base + jnp.where(begun <= offset, 1, 0)
        own_base = own_base + jnp.where(begun <= own_first, 1, 0)
    begin[...] = found - offset
    base = jnp.minimum(base, items - 3)
    own_base = jnp.minimum(own_base, items - 2)
    begun = bound = jnp.int32(0)
    for item in range(items):
        begun = begun + lens[item]
        bound = jnp.where(own_base == item, begun, bound)
    ids[0] = place[0]
    ids[1] = place[1]
    ids[2] = base
    ids[3] = (own_base - base) * 128
    ids[4] = bound - own_first
    ids[5] = prompts[own_base]
    ids[6] = prompts[own_base + 1]
    ids[7] = 0
    for block, low in enumerate(lows):
        ids[8 + block] = low - offset


def entry_kernel(ids, tok, gain, bias, wq, wk, wv, merge, pq, pm, hid, q, kv, tail, pack):
    width = wq.shape[1]
    for part, source in enumerate((merge, pq, pm)):

        @pl.when(pl.program_id(0) == part)
        def _():
            pack[part * width : (part + 1) * width, :] = source[...].T if part == 1 else source[...]

    normed, _ = ln_rows(tok[...].astype(F32))
    hidden = (normed * gain[...] + bias[...]).astype(BF)
    hid[...] = hidden
    kv[:, :width] = nn(hidden, wk[...]).astype(BF)
    kv[:, width:] = nn(hidden, wv[...]).astype(BF)
    q[...] = (nn(hidden, wq[...]).astype(BF) * SCALE).astype(BF)

    @pl.when(pl.program_id(0) == pl.num_programs(0) - 1)
    def _():
        tail[...] = kv[...]


def prompt_kernel(ids, text, pk, pv, out):
    width = pk.shape[1]
    out[:, :width] = nn(text[0], pk[...]).astype(BF)
    out[:, width:] = nn(text[0], pv[...]).astype(BF)


def window_bias(key_base, query_base, begin):
    shape = (BLOCK, BLOCK)
    key = key_base + lax.broadcasted_iota(jnp.int32, shape, 0)
    query = query_base + lax.broadcasted_iota(jnp.int32, shape, 1)
    return jnp.where((key <= query) & (key >= begin), 0.0, NEGATIVE).astype(F32)


def attend_block(keys, values_t, queries, bias, top, total, acc):
    for head, query in enumerate(queries):
        scores = nt(keys, query) + bias
        before = top[head : head + 1, :]
        after = jnp.maximum(before, jnp.max(scores, axis=0, keepdims=True))
        fade = jnp.exp(before - after)
        unnorm = jnp.exp(scores - after)
        total[head : head + 1, :] = total[head : head + 1, :] * fade + jnp.sum(unnorm, axis=0, keepdims=True)
        acc[head] = acc[head] * fade + nn(values_t[head * HD : (head + 1) * HD, :], unnorm.astype(BF))
        top[head : head + 1, :] = after


def attend_local_kernel(ids, q, kv, begin, acc_o, top_o, total_o, vt, acc, top, total):
    step = pl.program_id(0)
    width = q.shape[1]
    heads = width // HD
    blocks = kv.shape[0] // BLOCK

    @pl.when(step == 0)
    def _():
        for b in range(blocks):
            vt[b] = kv[b * BLOCK : (b + 1) * BLOCK, width:].T

    queries = by_head(q[...], heads)
    top[...] = jnp.full_like(top, NEGATIVE)
    total[...] = jnp.zeros_like(total)
    acc[...] = jnp.zeros_like(acc)
    low = lax.shift_right_logical(jnp.maximum(ids[8 + step], 0), 8)

    @pl.loop(low, step + 1)
    def _(b):
        row = pl.multiple_of(b * BLOCK, BLOCK)
        bias = window_bias(row, step * BLOCK, begin[...])
        attend_block(kv[pl.ds(row, BLOCK), :width], vt[b], queries, bias, top, total, acc)

    acc_o[0] = acc[...]
    top_o[0] = top[...]
    total_o[0] = total[...]


def attend_remote_kernel(ids, q, kv, tail, begin, acc_i, top_i, total_i, out, low_out, lse, vt, acc, top, total):
    step = pl.program_id(0)
    width = q.shape[1]
    heads = width // HD
    blocks = kv.shape[0] // BLOCK

    @pl.when(step == 0)
    def _():
        vt[0] = tail[:, width:].T
        for b in range(blocks):
            vt[b + 1] = kv[b * BLOCK : (b + 1) * BLOCK, width:].T

    queries = by_head(q[...], heads)
    acc[...] = acc_i[0]
    top[...] = top_i[0]
    total[...] = total_i[0]
    span = (blocks + 1) * BLOCK
    low = lax.shift_right_logical(jnp.maximum(ids[8 + step] + span, 0), 8)

    def bias_of(b):
        return window_bias(b * BLOCK - span, step * BLOCK, begin[...])

    @pl.when(low == 0)
    def _():
        attend_block(tail[:, :width], vt[0], queries, bias_of(0), top, total, acc)

    @pl.loop(jnp.maximum(low, 1), blocks + 1)
    def _(b):
        row = pl.multiple_of((b - 1) * BLOCK, BLOCK)
        attend_block(kv[pl.ds(row, BLOCK), :width], vt[b], queries, bias_of(b), top, total, acc)

    lse[0] = top[...] + jnp.log(total[...])
    stacked = jnp.concatenate([acc[h] * (1.0 / total[h : h + 1, :]) for h in range(heads)], axis=0)
    rows = stacked.T
    out[0] = rows
    low_out[0] = rows.astype(BF)


def back_block(keys, values, keys_t, queries, grads, bias, lse, delta, dq):
    key_sum = value_sum = None
    for head, (query, grad) in enumerate(zip(queries, grads)):
        row = slice(head, head + 1)
        probs = jnp.exp(nt(keys, query) + bias - lse[row, :])
        score_grad = (probs * (nt(values, grad) - delta[row, :])).astype(BF)
        low_probs = probs.astype(BF)
        key_term = nn(score_grad, query)
        value_term = nn(low_probs, grad)
        key_sum = key_term if key_sum is None else key_sum + key_term
        value_sum = value_term if value_sum is None else value_sum + value_term
        dq[head] += nn(keys_t[head * HD : (head + 1) * HD, :], score_grad)
    return key_sum, value_sum


def back_remote_kernel(ids, q, kv, tail, begin, grad, out, lse, dkv_o, dtail_o, dq_o, delta_o, kt, dkv, dq):
    step = pl.program_id(0)
    width = q.shape[1]
    heads = width // HD
    blocks = kv.shape[0] // BLOCK

    @pl.when(step == 0)
    def _():
        dkv[...] = jnp.zeros_like(dkv)
        kt[0] = tail[:, :width].T
        for b in range(blocks):
            kt[b + 1] = kv[b * BLOCK : (b + 1) * BLOCK, :width].T

    products = (grad[0].astype(F32) * out[0]).T
    for head in range(heads):
        delta_o[0, head : head + 1, :] = jnp.sum(products[head * HD : (head + 1) * HD, :], axis=0, keepdims=True)
    dq[...] = jnp.zeros_like(dq)
    span = (blocks + 1) * BLOCK
    low = lax.shift_right_logical(jnp.maximum(ids[8 + step] + span, 0), 8)

    @pl.when(low <= blocks)
    def _():
        queries = by_head(q[...], heads)
        grads = by_head(grad[0], heads)

        def one(b, pair):
            bias = window_bias(b * BLOCK - span, step * BLOCK, begin[...])
            key_sum, value_sum = back_block(
                pair[:, :width], pair[:, width:], kt[b], queries, grads, bias, lse.at[0], delta_o.at[0], dq
            )
            dkv[b, :, :width] += key_sum
            dkv[b, :, width:] += value_sum

        @pl.when(low == 0)
        def _():
            one(0, tail[...])

        @pl.loop(jnp.maximum(low, 1), blocks + 1)
        def _(b):
            row = pl.multiple_of((b - 1) * BLOCK, BLOCK)
            one(b, kv[pl.ds(row, BLOCK), :])

    dq_o[0] = dq[...]

    @pl.when(step == pl.num_programs(0) - 1)
    def _():
        dtail_o[...] = dkv[0].astype(BF)
        for b in range(blocks):
            dkv_o[b * BLOCK : (b + 1) * BLOCK, :] = dkv[b + 1].astype(BF)


def back_local_kernel(ids, q, kv, begin, grad, lse, delta, dq_i, dkv_o, dq_o, kt, dkv, dq):
    step = pl.program_id(0)
    width = q.shape[1]
    heads = width // HD
    blocks = kv.shape[0] // BLOCK

    @pl.when(step == 0)
    def _():
        dkv[...] = jnp.zeros_like(dkv)
        for b in range(blocks):
            kt[b] = kv[b * BLOCK : (b + 1) * BLOCK, :width].T

    dq[...] = dq_i[0]
    queries = by_head(q[...], heads)
    grads = by_head(grad[0], heads)
    low = lax.shift_right_logical(jnp.maximum(ids[8 + step], 0), 8)

    @pl.loop(low, step + 1)
    def _(b):
        row = pl.multiple_of(b * BLOCK, BLOCK)
        pair = kv[pl.ds(row, BLOCK), :]
        bias = window_bias(row, step * BLOCK, begin[...])
        key_sum, value_sum = back_block(
            pair[:, :width], pair[:, width:], kt[b], queries, grads, bias, lse.at[0], delta.at[0], dq
        )
        dkv[b, :, :width] += key_sum
        dkv[b, :, width:] += value_sum

    stacked = jnp.concatenate([dq[h] for h in range(heads)], axis=0)
    dq_o[...] = (stacked.T * SCALE).astype(BF)

    @pl.when(step == pl.num_programs(0) - 1)
    def _():
        for b in range(blocks):
            dkv_o[b * BLOCK : (b + 1) * BLOCK, :] = dkv[b]


def cross_bias(ids, prompt_rows, rows):
    shape = (2 * prompt_rows, rows)
    key = lax.broadcasted_iota(jnp.int32, shape, 0)
    query = lax.broadcasted_iota(jnp.int32, shape, 1)
    key_slot = lax.shift_right_logical(key, prompt_rows.bit_length() - 1)
    query_slot = jnp.where(query >= ids[4], 1, 0)
    limit = jnp.where(key_slot == 1, prompt_rows + ids[6], ids[5])
    return jnp.where((key_slot == query_slot) & (key < limit), 0.0, NEGATIVE).astype(F32)


def cross_kernel(ids, tok, low, *refs):
    packs, pairs = refs[:4], refs[4:8]
    gain2, bias2, gain3, bias3 = refs[8:12]
    after_self_o, two_o, q_o, stat_o, out_o, after_o, three_o = refs[12:]
    rows = tok.shape[0]
    width = packs[0].shape[0] // 3
    heads = width // HD
    rank = ids[1]
    prompt_rows = pairs[0].shape[0] // 3
    after = tok[...].astype(F32)
    for d in range(4):
        after = after + nn(low[rank ^ d], packs[d][:width, :])
    after_self_o[...] = after
    normed, _ = ln_rows(after)
    hidden = (normed * gain2[...] + bias2[...]).astype(BF)
    two_o[...] = hidden
    bias = cross_bias(ids, prompt_rows, rows)
    first = pl.multiple_of(ids[3], prompt_rows)
    for d in range(4):
        columns = slice(d * width, (d + 1) * width)
        query_rows = (nt(hidden, packs[d][width : 2 * width, :]).astype(BF) * SCALE).astype(BF)
        q_o[:, columns] = query_rows
        keys = pairs[d][pl.ds(first, 2 * prompt_rows), :width]
        values_t = pairs[d][pl.ds(first, 2 * prompt_rows), width:].T
        parts = []
        for head, query in enumerate(by_head(query_rows, heads)):
            scores = nt(keys, query) + bias
            top = jnp.max(scores, axis=0, keepdims=True)
            unnorm = jnp.exp(scores - top)
            total = jnp.sum(unnorm, axis=0, keepdims=True)
            stat_o[d * heads + head : d * heads + head + 1, :] = top + jnp.log(total)
            part = nn(values_t[head * HD : (head + 1) * HD, :], unnorm.astype(BF))
            parts.append(part * (1.0 / total))
        out_o[:, columns] = jnp.concatenate(parts, axis=0).T.astype(BF)
    after = after_self_o[...]
    for d in range(4):
        after = after + nn(out_o[:, d * width : (d + 1) * width], packs[d][2 * width :, :])
    after_o[...] = after
    normed, _ = ln_rows(after)
    three_o[...] = (normed * gain3[...] + bias3[...]).astype(BF)


def cross_back_kernel(ids, kept, sent, crossed, og, after, after_self, q, stat, *refs):
    packs, pairs = refs[:4], refs[4:8]
    gain2, gain3 = refs[8:10]
    cog_o, cqg_o, slg_o, resid_o, shg_o, keep0_o, keep1_o, send_o, norms_o = refs[10:]
    rows, model = after.shape
    width = packs[0].shape[0] // 3
    heads = width // HD
    rank = ids[1]
    prompt_rows = pairs[0].shape[0] // 3
    grad = kept[...].astype(F32) + sent[...].astype(F32) + crossed[...].astype(F32)
    normed, inverse = ln_rows(after[...])
    norms_o[0:1, :] = jnp.sum(grad * normed, axis=0, keepdims=True)
    norms_o[1:2, :] = jnp.sum(grad, axis=0, keepdims=True)
    resid = og[...].astype(F32) + ln_back(grad, gain3[...], normed, inverse)
    low_resid = resid.astype(BF)
    cog_o[...] = low_resid
    bias = cross_bias(ids, prompt_rows, rows)
    first = pl.multiple_of(ids[3], prompt_rows)
    keep0_o[...] = jnp.zeros_like(keep0_o)
    keep1_o[...] = jnp.zeros_like(keep1_o)
    send_o[...] = jnp.zeros_like(send_o)
    for d in range(4):
        columns = slice(d * width, (d + 1) * width)
        head_grad = nt(low_resid, packs[d][2 * width :, :]).astype(BF)
        keys = pairs[d][pl.ds(first, 2 * prompt_rows), :width]
        values = pairs[d][pl.ds(first, 2 * prompt_rows), width:]
        keys_t = keys.T
        key_sum = value_sum = None
        parts = []
        for head, (query, out_grad) in enumerate(zip(by_head(q[:, columns], heads), by_head(head_grad, heads))):
            row = slice(d * heads + head, d * heads + head + 1)
            probs = jnp.exp(nt(keys, query) + bias - stat[row, :])
            prob_grad = nt(values, out_grad)
            delta = jnp.sum(probs * prob_grad, axis=0, keepdims=True)
            score_grad = (probs * (prob_grad - delta)).astype(BF)
            key_term = nn(score_grad, query)
            value_term = nn(probs.astype(BF), out_grad)
            key_sum = key_term if key_sum is None else key_sum + key_term
            value_sum = value_term if value_sum is None else value_sum + value_term
            parts.append(nn(keys_t[head * HD : (head + 1) * HD, :], score_grad))
        cqg_o[:, columns] = (jnp.concatenate(parts, axis=0).T * SCALE).astype(BF)
        target = (keep0_o, send_o.at[0], keep1_o, send_o.at[1])[d]
        target[pl.ds(first, 2 * prompt_rows), :width] = key_sum.astype(BF)
        target[pl.ds(first, 2 * prompt_rows), width:] = value_sum.astype(BF)
    two_grad = None
    for d in range(4):
        term = nn(cqg_o[:, d * width : (d + 1) * width], packs[d][width : 2 * width, :])
        two_grad = term if two_grad is None else two_grad + term
    normed, inverse = ln_rows(after_self[...])
    norms_o[2:3, :] = jnp.sum(two_grad * normed, axis=0, keepdims=True)
    norms_o[3:4, :] = jnp.sum(two_grad, axis=0, keepdims=True)
    resid = resid + ln_back(two_grad, gain2[...], normed, inverse)
    resid_o[...] = resid
    low_resid = resid.astype(BF)
    slg_o[...] = low_resid
    for d in range(4):
        shg_o[rank ^ d] = nt(low_resid, packs[d][:width, :]).astype(BF)


def feed_kernel(ids, h_a, h_b, dh_a, dh_b, expand, shrink, *refs):
    outs, accs = refs[:8], refs[8:]
    last = pl.num_programs(0) - 1
    c = 0.7978845608028654
    for side, (h, dh) in enumerate(((h_a, dh_a), (h_b, dh_b))):
        low_o, pre_o, out_o, three_o = outs[4 * side : 4 * side + 4]
        out_s, three_s = accs[2 * side : 2 * side + 2]
        v = nn(h[...], expand[...])
        square = v * v
        t = jnp.tanh(c * v * (1.0 + 0.044715 * square))
        half = 0.5 * (1.0 + t)
        low = (v * half).astype(BF)
        slope = half + 0.5 * v * (1.0 - t * t) * (c * (1.0 + 3 * 0.044715 * square))
        pre = (dh[...].astype(F32) * slope).astype(BF)
        low_o[...] = low
        pre_o[...] = pre
        out_part = nn(low, shrink[...])
        three_part = nt(pre, expand[...])

        @pl.when(pl.program_id(0) == 0)
        def _():
            out_s[...] = out_part
            three_s[...] = three_part

        @pl.when(pl.program_id(0) > 0)
        def _():
            out_s[...] += out_part
            three_s[...] += three_part

        @pl.when(pl.program_id(0) == last)
        def _():
            out_o[...] = out_s[...].astype(BF)
            three_o[...] = three_s[...].astype(BF)


def feed(ids, base, h_a, h_b, dh, expand, shrink):
    rows, model = h_a.shape
    hidden = expand.shape[1]
    chunk = 256
    row_block = lambda d: pl.BlockSpec((rows, chunk), lambda j, s: (s[1] ^ d, j))
    column = pl.BlockSpec((rows, chunk), lambda j, s: (0, j))
    full = pl.BlockSpec((rows, model), lambda j, s: (0, 0))
    return run(
        feed_kernel,
        ids,
        (h_a, h_b, dh, dh, expand, shrink),
        [shaped((rows, hidden), BF), shaped((rows, hidden), BF), shaped((rows, model), BF), shaped((rows, model), BF)] * 2,
        grid=(hidden // chunk,),
        in_specs=[
            full,
            full,
            row_block(base),
            row_block(base + 1),
            pl.BlockSpec((model, chunk), lambda j, s: (0, j)),
            pl.BlockSpec((chunk, model), lambda j, s: (j, 0)),
        ],
        out_specs=[column, column, full, full] * 2,
        scratch=[pltpu.VMEM((rows, model), F32)] * 4,
        micros=12,
    )


def feed_weights_kernel(ids, *refs):
    threes, pres, lows = refs[:4], refs[4:8], refs[8:12]
    og, out, turned = refs[12:]
    step = pl.program_id(0)
    half = pl.num_programs(0) // 2
    rank = ids[1]
    rows = threes[0].shape[0]

    @pl.when(step == 0)
    def _():
        for d in range(4):
            turned[:, d * rows : (d + 1) * rows] = threes[d][...].T

    @pl.when(step == half)
    def _():
        for d in range(4):
            turned[:, d * rows : (d + 1) * rows] = og[pl.ds(pl.multiple_of((rank ^ d) * rows, rows), rows), :].T

    @pl.when(step < half)
    def _():
        out[...] = nn(turned[...], jnp.concatenate([p[...] for p in pres], axis=0)).astype(BF)

    @pl.when(step >= half)
    def _():
        out[...] = nn(turned[...], jnp.concatenate([p[...] for p in lows], axis=0)).astype(BF)


def feed_weights(ids, threes, pres, lows, og):
    rows, model = threes[0].shape
    hidden = pres[0].shape[1]
    chunk = 256
    half = hidden // chunk
    front = pl.BlockSpec((rows, chunk), lambda j, s: (0, jnp.minimum(j, half - 1)))
    back = pl.BlockSpec((rows, chunk), lambda j, s: (0, jnp.maximum(j - half, 0)))
    return run(
        feed_weights_kernel,
        ids,
        (*threes, *pres, *lows, og),
        [shaped((model, 2 * hidden), BF)],
        grid=(2 * half,),
        in_specs=[None] * 4 + [front] * 4 + [back] * 4 + [None],
        out_specs=[pl.BlockSpec((model, chunk), lambda j, s: (0, j))],
        scratch=[pltpu.VMEM((model, 4 * rows), BF)],
        micros=9,
    )[0]


def head_weights_kernel(ids, two, cqg, cog, crossed, slg, low, keep0, keep1, send):
    rank = ids[1]
    width = low.shape[2]
    two_t, cog_t, slg_t = two[...].T, cog[...].T, slg[...].T
    for d, out in enumerate((keep0, send.at[0], keep1, send.at[1])):
        columns = slice(d * width, (d + 1) * width)
        out[:, :width] = nn(two_t, cqg[:, columns]).astype(BF)
        out[:, width : 2 * width] = nn(cog_t, crossed[:, columns]).astype(BF)
        out[:, 2 * width :] = nn(slg_t, low[rank ^ d]).astype(BF)


def key_sum_kernel(ids, dkv, near, far, hid, dq, wq, wk, wv, gain, bias, kvg_o, keep0, keep1, send, norms):
    rows, width2 = dkv.shape
    width = width2 // 2
    quarter = rows // 4
    rank = ids[1]
    kvg_o[: rows - BLOCK, :] = (dkv[: rows - BLOCK, :] + near[: rows - BLOCK, :].astype(F32)).astype(BF)
    kvg_o[rows - BLOCK :, :] = (
        dkv[rows - BLOCK :, :] + near[rows - BLOCK :, :].astype(F32) + far[...].astype(F32)
    ).astype(BF)
    product = total = None
    for d in (1, 3, 2, 0):
        own = pl.ds(pl.multiple_of((rank ^ d) * quarter, quarter), quarter)
        part = (
            nt(dq[own, :], wq[...]) + nt(kvg_o[own, :width], wk[...]) + nt(kvg_o[own, width:], wv[...])
        )
        hidden = hid[own, :].astype(F32)
        term = jnp.sum(part * hidden, axis=0, keepdims=True)
        plain = jnp.sum(part, axis=0, keepdims=True)
        product = term if product is None else product + term
        total = plain if total is None else total + plain
        (keep0, send.at[0], keep1, send.at[1])[d][...] = part.astype(BF)
    norms[0:1, :] = (product - bias[...] * total) / gain[...]
    norms[1:2, :] = total


def entry_back_kernel(ids, keep, sent, crossed, tok, gain, resid, out):
    grad = keep[...].astype(F32) + sent[0].astype(F32) + crossed[...].astype(F32)
    normed, inverse = ln_rows(tok[...].astype(F32))
    out[...] = (resid[...] + ln_back(grad, gain[...], normed, inverse)).astype(BF)


def assemble_kernel(ids, *refs):
    out = refs[4]
    for d in range(4):

        @pl.when(pl.program_id(0) == ids[1] ^ d)
        def _():
            out[...] = refs[d][...].astype(out.dtype)


def assemble(ids, pieces, dtype):
    rows, model = pieces[0].shape
    return run(
        assemble_kernel,
        ids,
        pieces,
        [shaped((4 * rows, model), dtype)],
        grid=(4,),
        out_specs=[pl.BlockSpec((rows, model), lambda i, s: (i, 0))],
        micros=4,
    )[0]


def gather(own):
    across = partner(own, 2)
    near = partner(own, 1)
    return own, near, across, partner(across, 1)


def sum_rows(blocks):
    return jnp.sum(blocks.astype(F32), axis=0)


def body(
    tokens,
    text_states,
    item_lengths,
    prompt_lengths,
    entry_gain,
    entry_bias,
    cross_gain,
    cross_bias_,
    mixer_gain,
    mixer_bias,
    query_weight,
    key_weight,
    value_weight,
    merge_weight,
    prompt_query,
    prompt_key,
    prompt_value,
    prompt_merge,
    expand_weight,
    shrink_weight,
    output_grad,
):
    rows, model = tokens.shape
    ranks = lax.axis_size("mp")
    width = query_weight.shape[1]
    heads = width // HD
    items, prompt_rows = text_states.shape[:2]
    quarter = rows // ranks
    steps = rows // BLOCK
    hidden_units = expand_weight.shape[1]
    shards = lax.axis_size("far") * lax.axis_size("near")
    assert ranks == 4 and quarter == BLOCK and prompt_rows == 128 and items % shards == 0

    place = jnp.stack([lax.axis_index(SEQ), lax.axis_index("mp")]).astype(jnp.int32)
    scalars = pl.BlockSpec(memory_space=pltpu.SMEM)
    ids, begin = pl.pallas_call(
        functools.partial(layout_kernel, rows),
        out_shape=[shaped((8 + steps,), jnp.int32), shaped((1, rows), jnp.int32)],
        in_specs=[scalars] * 3,
        out_specs=[scalars, pl.BlockSpec(memory_space=pltpu.VMEM)],
    )(item_lengths, prompt_lengths, place)
    base = ids[2]

    row = lambda vector: vector.reshape(1, -1)
    own_rows = lambda columns: pl.BlockSpec((quarter, columns), lambda *g: (g[-1][1], 0))

    block_rows = lambda columns: pl.BlockSpec((BLOCK, columns), lambda i, *s: (i, 0))
    hidden_one, q, kv, kv_tail, pack = run(
        entry_kernel,
        None,
        (tokens, row(entry_gain), row(entry_bias), query_weight, key_weight, value_weight, merge_weight, prompt_query, prompt_merge),
        [
            shaped((rows, model), BF),
            shaped((rows, width), BF),
            shaped((rows, 2 * width), BF),
            shaped((BLOCK, 2 * width), BF),
            shaped((3 * width, model), BF),
        ],
        grid=(steps,),
        in_specs=[block_rows(model)] + [None] * 8,
        out_specs=[block_rows(model), block_rows(width), block_rows(2 * width), None, None],
        micros=5,
    )
    kv_near = from_behind(kv, 1)
    kv_far = from_behind(kv_tail, 2)

    pair = run(
        prompt_kernel,
        ids,
        (after(text_states, kv), prompt_key, prompt_value),
        [shaped((3 * prompt_rows, 2 * width), BF)],
        grid=(3,),
        in_specs=[pl.BlockSpec((1, prompt_rows, model), lambda i, s: (s[2] + i, 0, 0)), None, None],
        out_specs=[pl.BlockSpec((prompt_rows, 2 * width), lambda i, s: (i, 0))],
        micros=1.5,
    )[0]
    pack_near, pack_across = partner(pack, 1), partner(pack, 2)
    pair_near, pair_across = partner(pair, 1), partner(after(pair, pack), 2)
    hidden_grad = nt(after(output_grad, kv, pack), shrink_weight).astype(BF)

    state = [shaped((steps, heads, HD, BLOCK), F32), shaped((steps, heads, BLOCK), F32), shaped((steps, heads, BLOCK), F32)]
    state_specs = [
        pl.BlockSpec((1, heads, HD, BLOCK), lambda i, s: (i, 0, 0, 0)),
        pl.BlockSpec((1, heads, BLOCK), lambda i, s: (i, 0, 0)),
        pl.BlockSpec((1, heads, BLOCK), lambda i, s: (i, 0, 0)),
    ]
    state_scratch = [pltpu.VMEM((heads, HD, BLOCK), F32), pltpu.VMEM((heads, BLOCK), F32), pltpu.VMEM((heads, BLOCK), F32)]
    q_spec = block_rows(width)
    begin_spec = pl.BlockSpec((1, BLOCK), lambda i, s: (0, i))
    piece_spec = pl.BlockSpec((1, BLOCK, width), lambda i, s: (i, 0, 0))
    turned = lambda blocks: pltpu.VMEM((blocks, width, BLOCK), BF)
    acc, top, total = run(
        attend_local_kernel,
        ids,
        (after(q, pack, pair), kv, begin),
        state,
        grid=(steps,),
        in_specs=[q_spec, None, begin_spec],
        out_specs=state_specs,
        scratch=[turned(steps)] + state_scratch,
        micros=12,
    )
    kv_near, kv_far = lax.optimization_barrier((kv_near, kv_far, acc, hidden_grad))[:2]
    self_out, self_low, lse = run(
        attend_remote_kernel,
        ids,
        (q, kv_near, kv_far, begin, acc, top, total),
        [shaped((steps, BLOCK, width), F32), shaped((steps, BLOCK, width), BF), shaped((steps, heads, BLOCK), F32)],
        grid=(steps,),
        in_specs=[q_spec, None, None, begin_spec] + state_specs,
        out_specs=[piece_spec, piece_spec, state_specs[1]],
        scratch=[turned(steps + 1)] + state_scratch,
        micros=10,
    )
    low_rows = lax.all_to_all(self_low, "mp", 0, 0)
    pack_across, pair_across = lax.optimization_barrier((pack_across, pair_across, self_low))[:2]
    packs = (pack, pack_near, pack_across, partner(pack_across, 1))
    pairs = (pair, pair_near, pair_across, partner(pair_across, 1))

    wide = lambda dtype: shaped((quarter, model), dtype)
    stat_shape = shaped((ranks * heads, quarter), F32)
    norms = (row(cross_gain), row(cross_bias_), row(mixer_gain), row(mixer_bias))
    after_self, hidden_two, cross_q, stat, cross_out, after_cross, hidden_three = run(
        cross_kernel,
        ids,
        (tokens, low_rows, *packs, *pairs, *norms),
        [wide(F32), wide(BF), wide(BF), stat_shape, wide(BF), wide(F32), wide(BF)],
        in_specs=[own_rows(model)] + [None] * 13,
        micros=11,
    )

    three_near, three_across = partner(hidden_three, 1), partner(hidden_three, 2)
    low0, pre0, out0, part0, low1, pre1, out1, part1 = feed(
        ids, 0, hidden_three, three_near, hidden_grad, expand_weight, shrink_weight
    )
    three_across = after(three_across, part1)
    threes = (hidden_three, three_near, three_across, partner(three_across, 1))
    sent1, out_sent1 = partner(part1, 1), partner(out1, 1)
    low2, pre2, out2, part2, low3, pre3, out3, part3 = feed(
        ids, 2, threes[2], threes[3], hidden_grad, expand_weight, shrink_weight
    )
    partial = (part2.astype(F32) + partner(part3, 1).astype(F32)).astype(BF)
    across = partner(partial, 2)
    out_partial = (out2.astype(F32) + partner(after(out3, partial), 1).astype(F32)).astype(BF)
    feed_grads = feed_weights(ids, threes, (pre0, pre1, pre2, pre3), (low0, low1, low2, low3), after(output_grad, partial))
    feed_sum = lax.psum_scatter(feed_grads, SEQ, scatter_dimension=0, tiled=True)
    across = after(across, feed_grads, out_partial)
    out_across = partner(after(out_partial, across), 2)

    pair_out = shaped((3 * prompt_rows, 2 * width), BF)
    cog, cqg, slg, resid, shg, pair_keep0, pair_keep1, pair_send, norm_grads = run(
        cross_back_kernel,
        ids,
        (part0, sent1, across, output_grad, after_cross, after_self, cross_q, stat, *packs, *pairs, norms[0], norms[2]),
        [wide(BF), wide(BF), wide(BF), wide(F32), shaped((ranks, quarter, width), BF)]
        + [pair_out, pair_out, shaped((2, *pair_out.shape), BF), shaped((4, model), F32)],
        in_specs=[None] * 3 + [own_rows(model)] + [None] * 14,
        micros=15,
        vmem=48,
    )
    self_grad = lax.all_to_all(shg, "mp", 0, 0)

    pieces = shaped((model, 3 * width), BF)
    head_keep0, head_keep1, head_send = run(
        head_weights_kernel,
        ids,
        (hidden_two, cqg, cog, cross_out, slg, low_rows),
        [pieces, pieces, shaped((2, *pieces.shape), BF)],
        micros=4,
    )

    def added(*terms):
        total = terms[0].astype(F32)
        for term in terms[1:]:
            total = total + term.astype(F32)
        return total.astype(BF)

    pair_sent, head_sent = partner(pair_send, 1), partner(head_send, 1)
    pair_half = added(pair_keep1, pair_sent[1])
    self_grad = after(self_grad, head_keep0, pair_half)
    pair_across = partner(after(pair_half, self_grad), 2)
    head_across = partner(after(added(head_keep1, head_sent[1]), self_grad), 2)

    lse_spec = state_specs[1]
    stat4 = shaped((steps, heads, BLOCK), F32)
    dkv_near, dkv_far, dq_part, delta = run(
        back_remote_kernel,
        ids,
        (q, kv_near, kv_far, begin, self_grad, self_out, lse),
        [shaped((rows, 2 * width), BF), shaped((BLOCK, 2 * width), BF), state[0], stat4],
        grid=(steps,),
        in_specs=[q_spec, None, None, begin_spec, piece_spec, piece_spec, lse_spec],
        out_specs=[None, None, state_specs[0], lse_spec],
        scratch=[turned(steps + 1), pltpu.VMEM((steps + 1, BLOCK, 2 * width), F32), state_scratch[0]],
        micros=10,
    )
    from_near = from_behind(dkv_near, -1)
    from_far = from_behind(dkv_far, -2)

    pair_sum = added(pair_keep0, pair_sent[0], pair_across).reshape(3, prompt_rows, 2 * width)
    placed = lax.dynamic_update_slice_in_dim(jnp.zeros((items, prompt_rows, 2 * width), BF), pair_sum, base, 0)
    placed = after(placed, dkv_near).reshape(items * prompt_rows, 2 * width)
    dq_part = after(dq_part, placed)
    own_pair = over_shards(placed).astype(BF)

    dkv, dq = run(
        back_local_kernel,
        ids,
        (q, kv, begin, self_grad, lse, delta, dq_part),
        [shaped((rows, 2 * width), F32), shaped((rows, width), BF)],
        grid=(steps,),
        in_specs=[q_spec, None, begin_spec, piece_spec, lse_spec, lse_spec, state_specs[0]],
        out_specs=[None, q_spec],
        scratch=[turned(steps), pltpu.VMEM((steps, BLOCK, 2 * width), F32), state_scratch[0]],
        micros=14,
    )
    text_part = nt(own_pair[:, :width], prompt_key) + nt(own_pair[:, width:], prompt_value)
    text_blocks = jnp.swapaxes(text_part.astype(BF).reshape(-1, ranks, width), 0, 1)
    text_own = sum_rows(lax.all_to_all(text_blocks, "mp", 0, 0)).astype(BF)

    head_rows = added(head_keep0, head_sent[0], head_across)
    out_rows = added(after_cross, out0, out_sent1, out_across)
    layer_output = assemble(ids, gather(after(out_rows, head_rows)), BF)

    from_near, from_far = lax.optimization_barrier((from_near, from_far, dq))[:2]
    quarter_out = shaped((quarter, model), BF)
    kvg, one_keep0, one_keep1, one_send, entry_norms = run(
        key_sum_kernel,
        ids,
        (dkv, from_near, from_far, hidden_one, dq, query_weight, key_weight, value_weight, row(entry_gain), row(entry_bias)),
        [shaped((rows, 2 * width), BF), quarter_out, quarter_out, shaped((2, *quarter_out.shape), BF), shaped((2, model), F32)],
        micros=3,
    )
    one_sent = partner(one_send, 1)
    one_across = partner(added(one_keep1, one_sent[1]), 2)
    head_sum = over_shards(after(head_rows, from_near, from_far))
    entry_grads = jnp.concatenate([tn(hidden_one, dq), tn(hidden_one, kvg)], axis=1).astype(BF)
    one_across = after(one_across, entry_grads)
    entry_sum = over_shards(entry_grads)
    grad_rows = run(
        entry_back_kernel,
        ids,
        (one_keep0, one_sent, one_across, tokens, row(entry_gain), resid),
        [wide(BF)],
        in_specs=[None] * 3 + [own_rows(model)] + [None] * 2,
        micros=3,
    )[0]
    tokens_grad = assemble(ids, gather(grad_rows), F32)

    prompt_all = from_shards(jnp.concatenate([own_pair, text_own], axis=1))
    prompt_grads = tn(text_states.reshape(items * prompt_rows, model), prompt_all[:, : 2 * width])
    text_grad = prompt_all[:, 2 * width :].astype(F32).reshape(items, prompt_rows, width)

    norm_rows = jnp.concatenate([after(entry_norms, one_across), norm_grads[2:4], norm_grads[0:2], jnp.zeros((2, model), F32)])
    norm_blocks = jnp.swapaxes(norm_rows.reshape(8, shards, model // shards), 0, 1)
    norm_sum = jnp.sum(lax.all_to_all(norm_blocks, SEQ, 0, 0), axis=0)
    norm_sum = norm_sum + partner(norm_sum, 1)
    norm_sum = norm_sum + partner(norm_sum, 2)

    cut = lambda array, index: array[:, index * width : (index + 1) * width]
    feed_sum = feed_sum.astype(F32)
    return (
        layer_output,
        tokens_grad,
        text_grad,
        norm_sum[0],
        norm_sum[1],
        norm_sum[2],
        norm_sum[3],
        norm_sum[4],
        norm_sum[5],
        cut(entry_sum, 0),
        cut(entry_sum, 1),
        cut(entry_sum, 2),
        cut(head_sum, 2).T,
        cut(head_sum, 0),
        prompt_grads[:, :width],
        prompt_grads[:, width:],
        cut(head_sum, 1).T,
        feed_sum[:, :hidden_units],
        feed_sum[:, hidden_units:].T,
    )


def solution(mesh):
    shards = mesh.shape["seq"]
    mesh = jax.sharding.Mesh(mesh.devices.reshape(shards // 2, 2, mesh.shape["mp"]), (*SEQ, "mp"))
    seq, mp, both = P(SEQ, None), P("mp", None), P(None, "mp")
    return jax.shard_map(
        body,
        mesh=mesh,
        in_specs=(seq,) + (P(),) * 9 + (both,) * 3 + (mp,) + (both,) * 3 + (mp, both, mp, seq),
        out_specs=(
            (seq, seq, P(None, None, "mp"))
            + (P(SEQ),) * 6
            + (P(SEQ, "mp"),) * 3
            + (P("mp", SEQ), P(SEQ, "mp"), both, both, P("mp", SEQ), P(SEQ, "mp"), P("mp", SEQ))
        ),
        check_vma=False,
    )
```

```python
import functools

import jax
import jax.numpy as jnp
from jax import lax
from jax.experimental import pallas as pl
from jax.experimental.pallas import tpu as pltpu
from jax.sharding import PartitionSpec as P

HD = 64
ITEM_LEN = 1024
EPS = 1e-06
NEGATIVE = -1e30
BF = jnp.bfloat16
F32 = jnp.float32
BLOCK = 256
SCALE = HD**-0.5
MIB = 1 << 20


def dot(left, right, ld, rd):
    return lax.dot_general(left, right, (((ld,), (rd,)), ((), ())), preferred_element_type=F32)


def nn(left, right):
    return dot(left, right, 1, 0)


def nt(left, right):
    return dot(left, right, 1, 1)


def tn(left, right):
    return dot(left, right, 0, 0)


def partner(value, step):
    count = lax.axis_size("mp")
    return lax.ppermute(value, "mp", [(rank, rank ^ step) for rank in range(count)])


SEQ = ("far", "near")


def from_behind(value, steps):
    count = lax.axis_size("far") * lax.axis_size("near")
    leading, last = (max(0, -steps), min(count, count - steps))
    return lax.ppermute(value, SEQ, [(source, source + steps) for source in range(leading, last)])


def shard_bits():
    return (lax.axis_size("far") * lax.axis_size("near")).bit_length() - 1


def across_bit(value, bit):
    return lax.ppermute(value, SEQ, [(shard, shard ^ (1 << bit)) for shard in range(1 << shard_bits())])


def own_bit(bit):
    return lax.axis_index(SEQ) // (1 << bit) % 2


def step_kernel(bit, ids, kept, sent, kept_o, send_o):
    own = lax.shift_right_logical(ids[0], bit) % 2
    kept_o[0] = (kept[own].astype(F32) + sent[own].astype(F32)).astype(BF)
    send_o[0] = (kept[1 - own].astype(F32) + sent[1 - own].astype(F32)).astype(BF)


class ShardSum:
    def __init__(self, kept, send):
        self.left = list(range(1, shard_bits()))
        self.kept, self.sent = kept, across_bit(send, 0)

    def step(self, ids, *others):
        blocks, part, columns = self.kept.shape
        half = pl.BlockSpec((1, part, columns), lambda j, s: (j, 0, 0))
        self.kept, send = run(
            functools.partial(step_kernel, self.left[0]),
            ids,
            (self.kept, after(self.sent, *others)),
            [shaped((blocks // 2, part, columns), BF)] * 2,
            grid=(blocks // 2,),
            in_specs=[pl.BlockSpec((2, part, columns), lambda j, s: (j, 0, 0))] * 2,
            out_specs=[half, half],
            micros=2,
        )
        self.sent = across_bit(send, self.left[0])
        self.left = self.left[1:]

    def last(self, ids, *others):
        while self.left:
            self.step(ids, *others)
        rows = lambda value: value.reshape(-1, value.shape[-1])
        return rows(self.kept), rows(after(self.sent, *others))


def double(value, have, bit):
    other = across_bit(value, bit)
    dim = sorted([*have, bit], reverse=True).index(bit)
    low = own_bit(bit) == 0
    return jnp.stack([jnp.where(low, value, other), jnp.where(low, other, value)], axis=dim)


def to_all(own):
    have = []
    value = own
    for bit in reversed(range(shard_bits())):
        value = double(value, have, bit)
        have.append(bit)
    return value.reshape(-1, own.shape[-1])


def added(*terms):
    total = terms[0].astype(F32)
    for term in terms[1:]:
        total = total + term.astype(F32)
    return total.astype(BF)


def whole(array):
    rank = len(array.shape)
    return pl.BlockSpec(array.shape, lambda *_: (0,) * rank)


def shaped(shape, dtype):
    return jax.ShapeDtypeStruct(shape, dtype)


def run(kernel, ids, args, outs, grid=(1,), in_specs=None, out_specs=None, scratch=(), micros=1, vmem=40):
    in_specs = in_specs or [None] * len(args)
    out_specs = out_specs or [None] * len(outs)
    in_specs = [whole(a) if s is None else s for a, s in zip(args, in_specs)]
    out_specs = [whole(a) if s is None else s for a, s in zip(outs, out_specs)]
    prefetch = () if ids is None else (ids,)
    return pl.pallas_call(
        functools.partial(kernel, None) if ids is None else kernel,
        out_shape=outs,
        grid_spec=pltpu.PrefetchScalarGridSpec(
            num_scalar_prefetch=len(prefetch),
            grid=grid,
            in_specs=in_specs,
            out_specs=out_specs,
            scratch_shapes=list(scratch),
        ),
        compiler_params=pltpu.CompilerParams(vmem_limit_bytes=vmem * MIB),
        cost_estimate=pl.CostEstimate(flops=int(micros * 0.5e9), transcendentals=0, bytes_accessed=1000),
    )(*prefetch, *args)


def after(value, *others):
    return lax.optimization_barrier((value, *others))[0]


def ln_rows(values):
    centred = values - jnp.mean(values, axis=-1, keepdims=True)
    spread = jnp.mean(centred * centred, axis=-1, keepdims=True)
    inverse = lax.rsqrt(spread + EPS)
    return centred * inverse, inverse


def ln_back(grad, gain, normed, inverse):
    scaled = grad * gain
    first = jnp.mean(scaled, axis=-1, keepdims=True)
    second = jnp.mean(scaled * normed, axis=-1, keepdims=True)
    return inverse * (scaled - first - normed * second)


def head_mask(head, heads):
    lanes = lax.broadcasted_iota(jnp.int32, (1, heads * HD), 1)
    return jnp.where(lanes // HD == head, 1.0, 0.0).astype(BF)


def by_head(rows, heads):
    return [rows * head_mask(head, heads) for head in range(heads)]


def layout_kernel(rows, lens, prompts, place, ids, begin):
    items = lens.shape[0]
    offset = place[0] * rows
    own_first = offset + place[1] * (rows // 4)
    reach = begin.shape[1]
    positions = offset + lax.broadcasted_iota(jnp.int32, (1, reach), 1)
    found = jnp.zeros((1, reach), jnp.int32)
    lows = [jnp.int32(0)] * (reach // BLOCK)
    begun = base = own_base = jnp.int32(0)
    for item in range(items):
        found = jnp.where(positions >= begun, begun, found)
        lows = [jnp.where(offset + block * BLOCK >= begun, begun, low) for block, low in enumerate(lows)]
        begun = begun + lens[item]
        base = base + jnp.where(begun <= offset, 1, 0)
        own_base = own_base + jnp.where(begun <= own_first, 1, 0)
    begin[...] = jnp.where(positions >= begun, begun, found) - offset
    lows = [jnp.where(offset + block * BLOCK >= begun, begun, low) for block, low in enumerate(lows)]
    base = jnp.minimum(base, items - 3)
    own_base = jnp.minimum(own_base, items - 2)
    begun = bound = jnp.int32(0)
    for item in range(items):
        begun = begun + lens[item]
        bound = jnp.where(own_base == item, begun, bound)
    ids[0] = place[0]
    ids[1] = place[1]
    ids[2] = base
    ids[3] = (own_base - base) * 128
    ids[4] = bound - own_first
    ids[5] = prompts[own_base]
    ids[6] = prompts[own_base + 1]
    ids[7] = 0
    for block, low in enumerate(lows):
        ids[8 + block] = low - offset


def pack_kernel(ids, merge, pq, pm, pack):
    width = pq.shape[1]
    pack[:width, :] = merge[...]
    pack[width : 2 * width, :] = pq[...].T
    pack[2 * width :, :] = pm[...]


def entry_kernel(ids, tok, gain, bias, wq, wk, wv, hid, q, kv, tail):
    width = wq.shape[1]
    normed, _ = ln_rows(tok[...].astype(F32))
    hidden = (normed * gain[...] + bias[...]).astype(BF)
    hid[...] = hidden
    kv[:, :width] = nn(hidden, wk[...]).astype(BF)
    kv[:, width:] = nn(hidden, wv[...]).astype(BF)
    q[...] = (nn(hidden, wq[...]).astype(BF) * SCALE).astype(BF)

    @pl.when(pl.program_id(0) == pl.num_programs(0) - 1)
    def _():
        tail[...] = kv[...]


def prompt_kernel(ids, text, pk, pv, out):
    width = pk.shape[1]
    out[:, :width] = nn(text[0], pk[...]).astype(BF)
    out[:, width:] = nn(text[0], pv[...]).astype(BF)


def window_bias(key_base, query_base, begin):
    shape = (BLOCK, BLOCK)
    key = key_base + lax.broadcasted_iota(jnp.int32, shape, 0)
    query = query_base + lax.broadcasted_iota(jnp.int32, shape, 1)
    return jnp.where((key <= query) & (key >= begin), 0.0, NEGATIVE).astype(F32)


def attend_block(keys, values_t, queries, bias, top, total, acc):
    for head, query in enumerate(queries):
        scores = nt(keys, query) + bias
        before = top[head : head + 1, :]
        after = jnp.maximum(before, jnp.max(scores, axis=0, keepdims=True))
        fade = jnp.exp(before - after)
        unnorm = jnp.exp(scores - after)
        total[head : head + 1, :] = total[head : head + 1, :] * fade + jnp.sum(unnorm, axis=0, keepdims=True)
        acc[head] = acc[head] * fade + nn(values_t[head * HD : (head + 1) * HD, :], unnorm.astype(BF))
        top[head : head + 1, :] = after


def attend_local_kernel(ids, q, kv, begin, acc_o, top_o, total_o, vt, acc, top, total):
    step = pl.program_id(0)
    width = q.shape[1]
    heads = width // HD
    blocks = kv.shape[0] // BLOCK

    @pl.when(step == 0)
    def _():
        for b in range(blocks):
            vt[b] = kv[b * BLOCK : (b + 1) * BLOCK, width:].T

    queries = by_head(q[...], heads)
    top[...] = jnp.full_like(top, NEGATIVE)
    total[...] = jnp.zeros_like(total)
    acc[...] = jnp.zeros_like(acc)
    low = lax.shift_right_logical(jnp.maximum(ids[8 + step], 0), 8)

    @pl.loop(low, step + 1)
    def _(b):
        row = pl.multiple_of(b * BLOCK, BLOCK)
        bias = window_bias(row, step * BLOCK, begin[...])
        attend_block(kv[pl.ds(row, BLOCK), :width], vt[b], queries, bias, top, total, acc)

    acc_o[0] = acc[...]
    top_o[0] = top[...]
    total_o[0] = total[...]


def attend_remote_kernel(ids, q, kv, tail, begin, acc_i, top_i, total_i, out, low_out, lse, ship_a, ship_b, ship0, vt, acc, top, total):
    step = pl.program_id(0)
    width = q.shape[1]
    heads = width // HD
    blocks = kv.shape[0] // BLOCK

    @pl.when(step == 0)
    def _():
        vt[0] = tail[:, width:].T
        for b in range(blocks):
            vt[b + 1] = kv[b * BLOCK : (b + 1) * BLOCK, width:].T

    queries = by_head(q[...], heads)
    acc[...] = acc_i[0]
    top[...] = top_i[0]
    total[...] = total_i[0]
    span = (blocks + 1) * BLOCK
    low = lax.shift_right_logical(jnp.maximum(ids[8 + step] + span, 0), 8)

    def bias_of(b):
        return window_bias(b * BLOCK - span, step * BLOCK, begin[...])

    @pl.when(low == 0)
    def _():
        attend_block(tail[:, :width], vt[0], queries, bias_of(0), top, total, acc)

    @pl.loop(jnp.maximum(low, 1), blocks + 1)
    def _(b):
        row = pl.multiple_of((b - 1) * BLOCK, BLOCK)
        attend_block(kv[pl.ds(row, BLOCK), :width], vt[b], queries, bias_of(b), top, total, acc)

    sums = top[...] + jnp.log(total[...])
    lse[0] = sums
    high = sums.astype(BF).astype(F32)
    both = jnp.concatenate([high, sums - high], axis=1)
    stacked = jnp.concatenate([acc[h] * (1.0 / total[h : h + 1, :]) for h in range(heads)], axis=0)
    rows = stacked.T
    out[0] = rows
    low_out[0] = rows.astype(BF)
    half = pl.num_programs(0) // 2

    def put(ship):
        ship[:BLOCK, :width] = q[...]
        ship[:BLOCK, width:] = rows.astype(BF)
        ship[BLOCK:, :] = jnp.concatenate([both, jnp.zeros((16 - heads, 2 * BLOCK), F32)], axis=0).astype(BF)

    @pl.when(step < half)
    def _():
        put(ship_a.at[0])

    @pl.when(step >= half)
    def _():
        put(ship_b.at[0])

    @pl.when(step == 0)
    def _():
        ship0[0] = ship_a[0]


def back_block(keys, values, keys_t, queries, grads, bias, lse, delta, dq, dkv):
    width = keys.shape[1]
    key_sum = value_sum = None
    for head, (query, grad) in enumerate(zip(queries, grads)):
        row = slice(head, head + 1)
        probs = jnp.exp(nt(keys, query) + bias - lse[row, :])
        score_grad = (probs * (nt(values, grad) - delta[row, :])).astype(BF)
        if dkv is not None:
            key_term = nn(score_grad, query)
            value_term = nn(probs.astype(BF), grad)
            key_sum = key_term if key_sum is None else key_sum + key_term
            value_sum = value_term if value_sum is None else value_sum + value_term
        if dq is not None:
            dq[head] += nn(keys_t[head * HD : (head + 1) * HD, :], score_grad)
    if dkv is not None:
        dkv[:, :width] += key_sum
        dkv[:, width:] += value_sum


def put_delta(delta, grad, out):
    products = (grad.astype(F32) * out.astype(F32)).T
    for head in range(delta.shape[0]):
        delta[head : head + 1, :] = jnp.sum(products[head * HD : (head + 1) * HD, :], axis=0, keepdims=True)


def back_local_kernel(ids, q, kv, begin, grad, out, lse, dkv_o, dq_o, delta_o, kt, dkv):
    step = pl.program_id(0)
    width = q.shape[1]
    heads = width // HD
    blocks = kv.shape[0] // BLOCK

    @pl.when(step == 0)
    def _():
        dkv[...] = jnp.zeros_like(dkv)
        for b in range(blocks):
            kt[b] = kv[b * BLOCK : (b + 1) * BLOCK, :width].T

    put_delta(delta_o.at[0], grad[0], out[0])
    dq_o[...] = jnp.zeros_like(dq_o)
    queries = by_head(q[...], heads)
    grads = by_head(grad[0], heads)
    low = lax.shift_right_logical(jnp.maximum(ids[8 + step], 0), 8)

    @pl.loop(low, step + 1)
    def _(b):
        row = pl.multiple_of(b * BLOCK, BLOCK)
        pair = kv[pl.ds(row, BLOCK), :]
        bias = window_bias(row, step * BLOCK, begin[...])
        back_block(
            pair[:, :width], pair[:, width:], kt[b], queries, grads, bias, lse.at[0], delta_o.at[0], dq_o.at[0], dkv.at[b]
        )

    @pl.when(step == pl.num_programs(0) - 1)
    def _():
        for b in range(blocks):
            dkv_o[b * BLOCK : (b + 1) * BLOCK, :] = dkv[b]


def back_query_kernel(ids, q, kv, tail, begin, grad, lse, delta, dq_i, dq_o, kt, dq):
    step = pl.program_id(0)
    width = q.shape[1]
    heads = width // HD
    blocks = kv.shape[0] // BLOCK

    @pl.when(step == 0)
    def _():
        kt[0] = tail[:, :width].T
        for b in range(blocks):
            kt[b + 1] = kv[b * BLOCK : (b + 1) * BLOCK, :width].T

    dq[...] = dq_i[0]
    span = (blocks + 1) * BLOCK
    low = lax.shift_right_logical(jnp.maximum(ids[8 + step] + span, 0), 8)

    @pl.when(low <= blocks)
    def _():
        queries = by_head(q[...], heads)
        grads = by_head(grad[0], heads)

        def one(b, pair):
            bias = window_bias(b * BLOCK - span, step * BLOCK, begin[...])
            back_block(pair[:, :width], pair[:, width:], kt[b], queries, grads, bias, lse.at[0], delta.at[0], dq, None)

        @pl.when(low == 0)
        def _():
            one(0, tail[...])

        @pl.loop(jnp.maximum(low, 1), blocks + 1)
        def _(b):
            row = pl.multiple_of((b - 1) * BLOCK, BLOCK)
            one(b, kv[pl.ds(row, BLOCK), :])

    stacked = jnp.concatenate([dq[h] for h in range(heads)], axis=0)
    dq_o[...] = (stacked.T * SCALE).astype(BF)


def back_key_kernel(ids, kv, begin, ship_low, ship_high, grad_n, ship_f, grad_f, dkv_i, dkv_o, delta, lse, dkv):
    step = pl.program_id(0)
    width = kv.shape[1] // 2
    heads = width // HD
    blocks = kv.shape[0] // BLOCK

    @pl.when(step == 0)
    def _():
        for b in range(blocks):
            dkv[b] = dkv_i[b * BLOCK : (b + 1) * BLOCK, :]

    low = lax.shift_right_logical(jnp.maximum(ids[8 + blocks + step], 0), 8)

    def all_keys(ship, grad):
        put_delta(delta, grad, ship[:BLOCK, width:])
        parts = ship[BLOCK:, :].astype(F32)
        lse[...] = parts[:heads, :BLOCK] + parts[:heads, BLOCK:]
        queries, grads = by_head(ship[:BLOCK, :width], heads), by_head(grad, heads)

        @pl.loop(low, blocks)
        def _(b):
            row = pl.multiple_of(b * BLOCK, BLOCK)
            pair = kv[pl.ds(row, BLOCK), :]
            bias = window_bias(row, blocks * BLOCK + step * BLOCK, begin[...])
            back_block(pair[:, :width], pair[:, width:], None, queries, grads, bias, lse, delta, None, dkv.at[b])

    @pl.when((low < blocks) & (step < blocks // 2))
    def _():
        all_keys(ship_low.at[0], grad_n[0])

    @pl.when((low < blocks) & (step >= blocks // 2) & (step < blocks))
    def _():
        all_keys(ship_high.at[0], grad_n[0])

    @pl.when((low < blocks) & (step == blocks))
    def _():
        all_keys(ship_f.at[0], grad_f[0])

    @pl.when(step == blocks)
    def _():
        for b in range(blocks):
            dkv_o[b * BLOCK : (b + 1) * BLOCK, :] = dkv[b].astype(BF)


def cross_bias(ids, prompt_rows, rows):
    shape = (2 * prompt_rows, rows)
    key = lax.broadcasted_iota(jnp.int32, shape, 0)
    query = lax.broadcasted_iota(jnp.int32, shape, 1)
    key_slot = lax.shift_right_logical(key, prompt_rows.bit_length() - 1)
    query_slot = jnp.where(query >= ids[4], 1, 0)
    limit = jnp.where(key_slot == 1, prompt_rows + ids[6], ids[5])
    return jnp.where((key_slot == query_slot) & (key < limit), 0.0, NEGATIVE).astype(F32)


def cross_kernel(ids, tok, low, *refs):
    packs, pairs = refs[:4], refs[4:8]
    gain2, bias2, gain3, bias3 = refs[8:12]
    after_self_o, two_o, q_o, stat_o, out_o, after_o, three_o = refs[12:]
    rows = tok.shape[0]
    width = packs[0].shape[0] // 3
    heads = width // HD
    rank = ids[1]
    prompt_rows = pairs[0].shape[0] // 3
    after = tok[...].astype(F32)
    for d in range(4):
        after = after + nn(low[rank ^ d], packs[d][:width, :])
    after_self_o[...] = after
    normed, _ = ln_rows(after)
    hidden = (normed * gain2[...] + bias2[...]).astype(BF)
    two_o[...] = hidden
    bias = cross_bias(ids, prompt_rows, rows)
    first = pl.multiple_of(ids[3], prompt_rows)
    for d in range(4):
        columns = slice(d * width, (d + 1) * width)
        query_rows = (nt(hidden, packs[d][width : 2 * width, :]).astype(BF) * SCALE).astype(BF)
        q_o[:, columns] = query_rows
        keys = pairs[d][pl.ds(first, 2 * prompt_rows), :width]
        values_t = pairs[d][pl.ds(first, 2 * prompt_rows), width:].T
        parts = []
        for head, query in enumerate(by_head(query_rows, heads)):
            scores = nt(keys, query) + bias
            top = jnp.max(scores, axis=0, keepdims=True)
            unnorm = jnp.exp(scores - top)
            total = jnp.sum(unnorm, axis=0, keepdims=True)
            stat_o[d * heads + head : d * heads + head + 1, :] = top + jnp.log(total)
            part = nn(values_t[head * HD : (head + 1) * HD, :], unnorm.astype(BF))
            parts.append(part * (1.0 / total))
        out_o[:, columns] = jnp.concatenate(parts, axis=0).T.astype(BF)
    after = after_self_o[...]
    for d in range(4):
        after = after + nn(out_o[:, d * width : (d + 1) * width], packs[d][2 * width :, :])
    after_o[...] = after
    normed, _ = ln_rows(after)
    three_o[...] = (normed * gain3[...] + bias3[...]).astype(BF)


def cross_back_kernel(ids, kept, sent, crossed, og, after, after_self, q, stat, *refs):
    packs, pairs = refs[:4], refs[4:8]
    gain2, gain3 = refs[8:10]
    cog_o, cqg_o, slg_o, resid_o, shg_o, keep0_o, keep1_o, send_o, norms_o = refs[10:]
    rows, model = after.shape
    width = packs[0].shape[0] // 3
    heads = width // HD
    rank = ids[1]
    prompt_rows = pairs[0].shape[0] // 3
    grad = kept[...].astype(F32) + sent[...].astype(F32) + crossed[...].astype(F32)
    normed, inverse = ln_rows(after[...])
    norms_o[0:1, :] = jnp.sum(grad * normed, axis=0, keepdims=True)
    norms_o[1:2, :] = jnp.sum(grad, axis=0, keepdims=True)
    resid = og[...].astype(F32) + ln_back(grad, gain3[...], normed, inverse)
    low_resid = resid.astype(BF)
    cog_o[...] = low_resid
    bias = cross_bias(ids, prompt_rows, rows)
    first = pl.multiple_of(ids[3], prompt_rows)
    keep0_o[...] = jnp.zeros_like(keep0_o)
    keep1_o[...] = jnp.zeros_like(keep1_o)
    send_o[...] = jnp.zeros_like(send_o)
    for d in range(4):
        columns = slice(d * width, (d + 1) * width)
        head_grad = nt(low_resid, packs[d][2 * width :, :]).astype(BF)
        keys = pairs[d][pl.ds(first, 2 * prompt_rows), :width]
        values = pairs[d][pl.ds(first, 2 * prompt_rows), width:]
        keys_t = keys.T
        key_sum = value_sum = None
        parts = []
        for head, (query, out_grad) in enumerate(zip(by_head(q[:, columns], heads), by_head(head_grad, heads))):
            row = slice(d * heads + head, d * heads + head + 1)
            probs = jnp.exp(nt(keys, query) + bias - stat[row, :])
            prob_grad = nt(values, out_grad)
            delta = jnp.sum(probs * prob_grad, axis=0, keepdims=True)
            score_grad = (probs * (prob_grad - delta)).astype(BF)
            key_term = nn(score_grad, query)
            value_term = nn(probs.astype(BF), out_grad)
            key_sum = key_term if key_sum is None else key_sum + key_term
            value_sum = value_term if value_sum is None else value_sum + value_term
            parts.append(nn(keys_t[head * HD : (head + 1) * HD, :], score_grad))
        cqg_o[:, columns] = (jnp.concatenate(parts, axis=0).T * SCALE).astype(BF)
        target = (keep0_o, send_o.at[0], keep1_o, send_o.at[1])[d]
        target[pl.ds(first, 2 * prompt_rows), :width] = key_sum.astype(BF)
        target[pl.ds(first, 2 * prompt_rows), width:] = value_sum.astype(BF)
    two_grad = None
    for d in range(4):
        term = nn(cqg_o[:, d * width : (d + 1) * width], packs[d][width : 2 * width, :])
        two_grad = term if two_grad is None else two_grad + term
    normed, inverse = ln_rows(after_self[...])
    norms_o[2:3, :] = jnp.sum(two_grad * normed, axis=0, keepdims=True)
    norms_o[3:4, :] = jnp.sum(two_grad, axis=0, keepdims=True)
    resid = resid + ln_back(two_grad, gain2[...], normed, inverse)
    resid_o[...] = resid
    low_resid = resid.astype(BF)
    slg_o[...] = low_resid
    for d in range(4):
        shg_o[rank ^ d] = nt(low_resid, packs[d][:width, :]).astype(BF)


def feed_kernel(ids, h_a, h_b, dh_a, dh_b, expand, shrink, *refs):
    outs, accs = refs[:8], refs[8:]
    last = pl.num_programs(0) - 1
    c = 0.7978845608028654
    for side, (h, dh) in enumerate(((h_a, dh_a), (h_b, dh_b))):
        low_o, pre_o, out_o, three_o = outs[4 * side : 4 * side + 4]
        out_s, three_s = accs[2 * side : 2 * side + 2]
        v = nn(h[...], expand[...])
        square = v * v
        t = jnp.tanh(c * v * (1.0 + 0.044715 * square))
        half = 0.5 * (1.0 + t)
        low = (v * half).astype(BF)
        slope = half + 0.5 * v * (1.0 - t * t) * (c * (1.0 + 3 * 0.044715 * square))
        pre = (dh[...].astype(F32) * slope).astype(BF)
        low_o[...] = low
        pre_o[...] = pre
        out_part = nn(low, shrink[...])
        three_part = nt(pre, expand[...])

        @pl.when(pl.program_id(0) == 0)
        def _():
            out_s[...] = out_part
            three_s[...] = three_part

        @pl.when(pl.program_id(0) > 0)
        def _():
            out_s[...] += out_part
            three_s[...] += three_part

        @pl.when(pl.program_id(0) == last)
        def _():
            out_o[...] = out_s[...].astype(BF)
            three_o[...] = three_s[...].astype(BF)


def feed(ids, base, h_a, h_b, dh, expand, shrink):
    rows, model = h_a.shape
    hidden = expand.shape[1]
    chunk = 256
    row_block = lambda d: pl.BlockSpec((rows, chunk), lambda j, s: (s[1] ^ d, j))
    column = pl.BlockSpec((rows, chunk), lambda j, s: (0, j))
    full = pl.BlockSpec((rows, model), lambda j, s: (0, 0))
    return run(
        feed_kernel,
        ids,
        (h_a, h_b, dh, dh, expand, shrink),
        [shaped((rows, hidden), BF), shaped((rows, hidden), BF), shaped((rows, model), BF), shaped((rows, model), BF)] * 2,
        grid=(hidden // chunk,),
        in_specs=[
            full,
            full,
            row_block(base),
            row_block(base + 1),
            pl.BlockSpec((model, chunk), lambda j, s: (0, j)),
            pl.BlockSpec((chunk, model), lambda j, s: (j, 0)),
        ],
        out_specs=[column, column, full, full] * 2,
        scratch=[pltpu.VMEM((rows, model), F32)] * 4,
        micros=12,
    )


def spread(ids, rows, kept, send):
    far, part, _ = kept.shape
    own = ids[0] % 2
    for block in range(far):
        kept[block] = rows[pl.ds(pl.multiple_of((2 * block + own) * part, part), part), :]
        send[block] = rows[pl.ds(pl.multiple_of((2 * block + 1 - own) * part, part), part), :]


def feed_weights_kernel(ids, *refs):
    threes, pres, lows = refs[:4], refs[4:8], refs[8:12]
    og, out, turned = refs[12:]
    step = pl.program_id(0)
    half = pl.num_programs(0) // 2
    rank = ids[1]
    rows = threes[0].shape[0]

    @pl.when(step == 0)
    def _():
        for d in range(4):
            turned[:, d * rows : (d + 1) * rows] = threes[d][...].T

    @pl.when(step == half)
    def _():
        for d in range(4):
            turned[:, d * rows : (d + 1) * rows] = og[pl.ds(pl.multiple_of((rank ^ d) * rows, rows), rows), :].T

    @pl.when(step < half)
    def _():
        out[...] = nn(turned[...], jnp.concatenate([p[...] for p in pres], axis=0)).astype(BF)

    @pl.when(step >= half)
    def _():
        out[...] = nn(turned[...], jnp.concatenate([p[...] for p in lows], axis=0)).astype(BF)


def feed_weights(ids, threes, pres, lows, og):
    rows, model = threes[0].shape
    hidden = pres[0].shape[1]
    chunk = 256
    half = hidden // chunk
    front = pl.BlockSpec((rows, chunk), lambda j, s: (0, jnp.minimum(j, half - 1)))
    back = pl.BlockSpec((rows, chunk), lambda j, s: (0, jnp.maximum(j - half, 0)))
    return run(
        feed_weights_kernel,
        ids,
        (*threes, *pres, *lows, og),
        [shaped((model, 2 * hidden), BF)],
        grid=(2 * half,),
        in_specs=[None] * 4 + [front] * 4 + [back] * 4 + [None],
        out_specs=[pl.BlockSpec((model, chunk), lambda j, s: (0, j))],
        scratch=[pltpu.VMEM((model, 4 * rows), BF)],
        micros=9,
        vmem=60,
    )[0]


def head_weights_kernel(ids, two, cqg, cog, crossed, slg, low, keep0, keep1, send):
    rank = ids[1]
    width = low.shape[2]
    two_t, cog_t, slg_t = two[...].T, cog[...].T, slg[...].T
    for d, out in enumerate((keep0, send.at[0], keep1, send.at[1])):
        columns = slice(d * width, (d + 1) * width)
        out[:, :width] = nn(two_t, cqg[:, columns]).astype(BF)
        out[:, width : 2 * width] = nn(cog_t, crossed[:, columns]).astype(BF)
        out[:, 2 * width :] = nn(slg_t, low[rank ^ d]).astype(BF)


def one_grad_kernel(ids, kvg, hid, dq, wq, wk, wv, gain, bias, keep0, keep1, send, norms):
    rows, width2 = kvg.shape
    width = width2 // 2
    quarter = rows // 4
    rank = ids[1]
    product = total = None
    for d in (1, 3, 2, 0):
        own = pl.ds(pl.multiple_of((rank ^ d) * quarter, quarter), quarter)
        part = (
            nt(dq[own, :], wq[...]) + nt(kvg[own, :width], wk[...]) + nt(kvg[own, width:], wv[...])
        )
        hidden = hid[own, :].astype(F32)
        term = jnp.sum(part * hidden, axis=0, keepdims=True)
        plain = jnp.sum(part, axis=0, keepdims=True)
        product = term if product is None else product + term
        total = plain if total is None else total + plain
        (keep0, send.at[0], keep1, send.at[1])[d][...] = part.astype(BF)
    norms[0:1, :] = (product - bias[...] * total) / gain[...]
    norms[1:2, :] = total


def text_kernel(ids, own, pk, pv, keep0, keep1, send):
    width = own.shape[1] // 2
    rank = ids[1]
    for d, out in enumerate((keep0, send.at[0], keep1, send.at[1])):
        columns = pl.ds(pl.multiple_of((rank ^ d) * width, width), width)
        out[...] = (nt(own[:, :width], pk[columns, :]) + nt(own[:, width:], pv[columns, :])).astype(BF)


def entry_weights_kernel(ids, hid, dq, kvg, entry_norms, norms, kept, send, rows):
    width = dq.shape[1]
    model = hid.shape[1]
    turned = hid[...].T
    rows[:, :width] = nn(turned, dq[...]).astype(BF)
    rows[:, width : 3 * width] = nn(turned, kvg[...]).astype(BF)
    sums = jnp.concatenate([entry_norms[...], norms[...], jnp.zeros((122, model), F32)], axis=0)
    rows[:, 3 * width :] = sums.T.astype(BF)
    spread(ids, rows, kept, send)


def arrived_kernel(ids, *refs):
    feed, head, entry, (expand, shrink, pq, pm, merge, wq, wk, wv, norms) = refs[:1], refs[1:2], refs[2:4], refs[4:]

    def total(terms, width, index):
        columns = slice(index * width, (index + 1) * width)
        value = terms[0][:, columns].astype(F32)
        for term in terms[1:]:
            value = value + term[:, columns].astype(F32)
        return value

    hidden, width = expand.shape[1], pq.shape[1]
    expand[...] = total(feed, hidden, 0)
    shrink[...] = total(feed, hidden, 1).T
    pq[...] = total(head, width, 0)
    pm[...] = total(head, width, 1).T
    merge[...] = total(head, width, 2).T
    wq[...] = total(entry, width, 0)
    wk[...] = total(entry, width, 1)
    wv[...] = total(entry, width, 2)
    norms[...] = total(entry, 128, 3 * width // 128).T[:8, :]


def entry_back_kernel(ids, keep, sent, crossed, tok, gain, resid, out):
    grad = keep[...].astype(F32) + sent[0].astype(F32) + crossed[...].astype(F32)
    normed, inverse = ln_rows(tok[...].astype(F32))
    out[...] = (resid[...] + ln_back(grad, gain[...], normed, inverse)).astype(BF)


def assemble_kernel(ids, *refs):
    out = refs[4]
    for d in range(4):

        @pl.when(pl.program_id(0) == ids[1] ^ d)
        def _():
            out[...] = refs[d][...].astype(out.dtype)


def assemble(ids, pieces, dtype):
    rows, model = pieces[0].shape
    return run(
        assemble_kernel,
        ids,
        pieces,
        [shaped((4 * rows, model), dtype)],
        grid=(4,),
        out_specs=[pl.BlockSpec((rows, model), lambda i, s: (i, 0))],
        micros=3,
    )[0]


def gather(own):
    across = partner(own, 2)
    near = partner(own, 1)
    return own, near, across, partner(across, 1)


def body(
    tokens,
    text_states,
    item_lengths,
    prompt_lengths,
    entry_gain,
    entry_bias,
    cross_gain,
    cross_bias_,
    mixer_gain,
    mixer_bias,
    query_weight,
    key_weight,
    value_weight,
    merge_weight,
    prompt_query,
    prompt_key,
    prompt_value,
    prompt_merge,
    expand_weight,
    shrink_weight,
    output_grad,
):
    rows, model = tokens.shape
    ranks = lax.axis_size("mp")
    width = query_weight.shape[1]
    heads = width // HD
    items, prompt_rows = text_states.shape[:2]
    quarter = rows // ranks
    steps = rows // BLOCK
    hidden_units = expand_weight.shape[1]
    shards = lax.axis_size("far") * lax.axis_size("near")
    assert ranks == 4 and quarter == BLOCK and prompt_rows == 128 and items % shards == 0

    place = jnp.stack([lax.axis_index(SEQ), lax.axis_index("mp")]).astype(jnp.int32)
    scalars = pl.BlockSpec(memory_space=pltpu.SMEM)
    ids, begin = pl.pallas_call(
        functools.partial(layout_kernel, rows),
        out_shape=[shaped((9 + 2 * steps + 7,), jnp.int32), shaped((1, 2 * rows + BLOCK), jnp.int32)],
        in_specs=[scalars] * 3,
        out_specs=[scalars, pl.BlockSpec(memory_space=pltpu.VMEM)],
    )(item_lengths, prompt_lengths, place)
    base = ids[2]

    row = lambda vector: vector.reshape(1, -1)
    own_rows = lambda columns: pl.BlockSpec((quarter, columns), lambda *g: (g[-1][1], 0))

    block_rows = lambda columns: pl.BlockSpec((BLOCK, columns), lambda i, *s: (i, 0))
    pack = run(pack_kernel, None, (merge_weight, prompt_query, prompt_merge), [shaped((3 * width, model), BF)], vmem=60)[0]
    pack_near, pack_across = partner(pack, 1), partner(pack, 2)
    hidden_one, q, kv, kv_tail = run(
        entry_kernel,
        None,
        (after(tokens, pack), row(entry_gain), row(entry_bias), query_weight, key_weight, value_weight),
        [
            shaped((rows, model), BF),
            shaped((rows, width), BF),
            shaped((rows, 2 * width), BF),
            shaped((BLOCK, 2 * width), BF),
        ],
        grid=(steps,),
        in_specs=[block_rows(model)] + [None] * 5,
        out_specs=[block_rows(model), block_rows(width), block_rows(2 * width), None],
        micros=2,
        vmem=60,
    )
    kv_near = from_behind(kv, 1)
    kv_far = from_behind(kv_tail, 2)

    pair = run(
        prompt_kernel,
        ids,
        (after(text_states, kv, pack_near), prompt_key, prompt_value),
        [shaped((3 * prompt_rows, 2 * width), BF)],
        grid=(3,),
        in_specs=[pl.BlockSpec((1, prompt_rows, model), lambda i, s: (s[2] + i, 0, 0)), None, None],
        out_specs=[pl.BlockSpec((prompt_rows, 2 * width), lambda i, s: (i, 0))],
        micros=1.5,
    )[0]
    pair_near, pair_across = partner(pair, 1), partner(pair, 2)
    hidden_grad = nt(after(output_grad, kv, pair), shrink_weight).astype(BF)

    state = [shaped((steps, heads, HD, BLOCK), F32), shaped((steps, heads, BLOCK), F32), shaped((steps, heads, BLOCK), F32)]
    state_specs = [
        pl.BlockSpec((1, heads, HD, BLOCK), lambda i, s: (i, 0, 0, 0)),
        pl.BlockSpec((1, heads, BLOCK), lambda i, s: (i, 0, 0)),
        pl.BlockSpec((1, heads, BLOCK), lambda i, s: (i, 0, 0)),
    ]
    state_scratch = [pltpu.VMEM((heads, HD, BLOCK), F32), pltpu.VMEM((heads, BLOCK), F32), pltpu.VMEM((heads, BLOCK), F32)]
    q_spec = block_rows(width)
    begin_spec = pl.BlockSpec((1, BLOCK), lambda i, s: (0, i))
    piece_spec = pl.BlockSpec((1, BLOCK, width), lambda i, s: (i, 0, 0))
    turned = lambda blocks: pltpu.VMEM((blocks, width, BLOCK), BF)
    acc, top, total = run(
        attend_local_kernel,
        ids,
        (after(q, pair_near), kv, begin),
        state,
        grid=(steps,),
        in_specs=[q_spec, None, begin_spec],
        out_specs=state_specs,
        scratch=[turned(steps)] + state_scratch,
        micros=13,
    )
    kv_near, kv_far = lax.optimization_barrier((kv_near, kv_far, acc, hidden_grad))[:2]
    def ship_spec(side):
        half = steps // 2
        index = (lambda i: jnp.maximum(i - half, 0)) if side else (lambda i: jnp.minimum(i, half - 1))
        return pl.BlockSpec((1, BLOCK + 16, 2 * width), lambda i, s: (index(jnp.minimum(i, steps - 1)), 0, 0))

    self_out, self_low, lse, ship_low, ship_high, ship_first = run(
        attend_remote_kernel,
        ids,
        (q, kv_near, kv_far, begin, acc, top, total),
        [shaped((steps, BLOCK, width), F32), shaped((steps, BLOCK, width), BF), shaped((steps, heads, BLOCK), F32)]
        + [shaped((blocks, BLOCK + 16, 2 * width), BF) for blocks in (steps // 2, steps // 2, 1)],
        grid=(steps,),
        in_specs=[q_spec, None, None, begin_spec] + state_specs,
        out_specs=[piece_spec, piece_spec, state_specs[1], ship_spec(0), ship_spec(1), None],
        scratch=[turned(steps + 1)] + state_scratch,
        micros=9,
    )
    low_rows = lax.all_to_all(self_low, "mp", 0, 0)
    pack_across, pair_across = lax.optimization_barrier((pack_across, pair_across, self_low))[:2]
    packs = (pack, pack_near, pack_across, partner(pack_across, 1))
    pairs = (pair, pair_near, pair_across, partner(pair_across, 1))

    wide = lambda dtype: shaped((quarter, model), dtype)
    stat_shape = shaped((ranks * heads, quarter), F32)
    norms = (row(cross_gain), row(cross_bias_), row(mixer_gain), row(mixer_bias))
    after_self, hidden_two, cross_q, stat, cross_out, after_cross, hidden_three = run(
        cross_kernel,
        ids,
        (tokens, low_rows, *packs, *pairs, *norms),
        [wide(F32), wide(BF), wide(BF), stat_shape, wide(BF), wide(F32), wide(BF)],
        in_specs=[own_rows(model)] + [None] * 13,
        micros=11,
    )

    ship_low, ship_high, ship_f = after((ship_low, ship_high, ship_first), hidden_three)
    ship_low, ship_f = from_behind(ship_low, -1), from_behind(ship_f, -2)

    three_near, three_across = partner(hidden_three, 1), partner(hidden_three, 2)
    low0, pre0, out0, part0, low1, pre1, out1, part1 = feed(
        ids, 0, hidden_three, three_near, hidden_grad, expand_weight, shrink_weight
    )
    three_across, ship_low, ship_f = after((three_across, ship_low, ship_f), part1)
    ship_high = from_behind(after(ship_high, ship_low), -1)
    threes = (hidden_three, three_near, three_across, partner(three_across, 1))
    sent1, out_sent1 = partner(part1, 1), partner(out1, 1)
    low2, pre2, out2, part2, low3, pre3, out3, part3 = feed(
        ids, 2, threes[2], threes[3], hidden_grad, expand_weight, shrink_weight
    )
    part3, sent1, out_sent1, ship_high = after((part3, sent1, out_sent1, ship_high), part2)
    partial = (part2.astype(F32) + partner(part3, 1).astype(F32)).astype(BF)
    across = partner(partial, 2)
    out_partial = (out2.astype(F32) + partner(after(out3, partial), 1).astype(F32)).astype(BF)
    feed_grads = feed_weights(ids, threes, after((pre0, pre1, pre2, pre3), partial), (low0, low1, low2, low3), output_grad)
    feed_sum = lax.psum_scatter(feed_grads, SEQ, scatter_dimension=0, tiled=True)
    across = after(across, feed_grads, out_partial)
    out_across = partner(after(out_partial, across), 2)

    pair_out = shaped((3 * prompt_rows, 2 * width), BF)
    cog, cqg, slg, resid, shg, pair_keep0, pair_keep1, pair_send, norm_grads = run(
        cross_back_kernel,
        ids,
        (part0, sent1, across, output_grad, after_cross, after_self, cross_q, stat, *packs, *pairs, norms[0], norms[2]),
        [wide(BF), wide(BF), wide(BF), wide(F32), shaped((ranks, quarter, width), BF)]
        + [pair_out, pair_out, shaped((2, *pair_out.shape), BF), shaped((4, model), F32)],
        in_specs=[None] * 3 + [own_rows(model)] + [None] * 14,
        micros=15,
        vmem=48,
    )
    self_grad = lax.all_to_all(shg, "mp", 0, 0)

    pair_sent = partner(pair_send, 1)
    pieces = shaped((model, 3 * width), BF)
    head_keep0, head_keep1, head_send = run(
        head_weights_kernel,
        ids,
        (hidden_two, cqg, cog, cross_out, slg, low_rows),
        [pieces, pieces, shaped((2, *pieces.shape), BF)],
        micros=5,
        vmem=60,
    )
    head_sent = partner(head_send, 1)
    head_half = added(head_keep1, head_sent[1])
    self_grad, out_across, pair_sent, head_half = after((self_grad, out_across, pair_sent, head_half), head_keep0)
    head_across = partner(head_half, 2)
    grad_n, grad_f = from_behind(self_grad, -1), from_behind(self_grad[:1], -2)
    pair_half = added(pair_keep1, pair_sent[1])
    pair_across = partner(pair_half, 2)

    lse_spec = state_specs[1]
    stat4 = shaped((steps, heads, BLOCK), F32)
    dkv, dq_part, delta = run(
        back_local_kernel,
        ids,
        (q, kv, begin, after(self_grad, pair_half), self_out, lse),
        [shaped((rows, 2 * width), F32), state[0], stat4],
        grid=(steps,),
        in_specs=[q_spec, None, begin_spec, piece_spec, piece_spec, lse_spec],
        out_specs=[None, state_specs[0], lse_spec],
        scratch=[turned(steps), pltpu.VMEM((steps, BLOCK, 2 * width), F32)],
        micros=15,
    )
    pair_across, grad_n, grad_f = after((pair_across, grad_n, grad_f), dq_part)
    pair_sum = added(pair_keep0, pair_sent[0], pair_across).reshape(3, prompt_rows, 2 * width)
    placed = lax.dynamic_update_slice_in_dim(jnp.zeros((items, prompt_rows, 2 * width), BF), pair_sum, base, 0)
    placed = placed.reshape(shards // 2, 2, -1, 2 * width)
    own = own_bit(0)
    text_sum = ShardSum(
        lax.dynamic_index_in_dim(placed, own, 1, keepdims=False), lax.dynamic_index_in_dim(placed, 1 - own, 1, keepdims=False)
    )
    dq = run(
        back_query_kernel,
        ids,
        (q, kv_near, kv_far, begin, self_grad, lse, delta, after(dq_part, text_sum.kept)),
        [shaped((rows, width), BF)],
        grid=(steps,),
        in_specs=[q_spec, None, None, begin_spec, piece_spec, lse_spec, lse_spec, state_specs[0]],
        out_specs=[q_spec],
        scratch=[turned(steps + 1), state_scratch[0]],
        micros=7,
    )[0]
    text_sum.step(ids, dq)
    far = shards // 2
    spread_out = [shaped((far, model // shards, 3 * width + 128), BF)] * 2
    grad_n, grad_f = after((grad_n, grad_f), dq, text_sum.kept)
    held = lambda i: jnp.minimum(i, steps - 1)
    near_piece = pl.BlockSpec((1, BLOCK, width), lambda i, s: (held(i), 0, 0))
    kvg = run(
        back_key_kernel,
        ids,
        (kv, begin, ship_low, ship_high, grad_n, ship_f, grad_f, dkv),
        [shaped((rows, 2 * width), BF)],
        grid=(steps + 1,),
        in_specs=[None, pl.BlockSpec((1, BLOCK), lambda i, s: (0, steps + i)), ship_spec(0), ship_spec(1), near_piece] + [None] * 3,
        scratch=[pltpu.VMEM((heads, BLOCK), F32)] * 2 + [pltpu.VMEM((steps, BLOCK, 2 * width), F32)],
        micros=8,
    )[0]

    quarter_out = shaped((quarter, model), BF)
    one_keep0, one_keep1, one_send, entry_norms = run(
        one_grad_kernel,
        ids,
        (kvg, hidden_one, dq, query_weight, key_weight, value_weight, row(entry_gain), row(entry_bias)),
        [quarter_out, quarter_out, shaped((2, *quarter_out.shape), BF), shaped((2, model), F32)],
        micros=3,
    )
    one_sent = partner(one_send, 1)
    entry_rows = run(
        entry_weights_kernel,
        ids,
        (hidden_one, after(dq, one_send), kvg, entry_norms, norm_grads),
        spread_out,
        scratch=[pltpu.VMEM((model, 3 * width + 128), BF)],
        micros=4,
    )
    entry_sum = ShardSum(*entry_rows)
    head_rows = added(head_keep0, head_sent[0], after(head_across, kvg))
    one_half = added(one_keep1, after(one_sent, entry_rows[0], head_rows)[1])
    one_across = partner(one_half, 2)
    own_pair = added(*text_sum.last(ids, one_half))
    text_out = shaped((prompt_rows * items // shards, width), BF)
    text_keep0, text_keep1, text_send = run(
        text_kernel, ids, (own_pair, prompt_key, prompt_value), [text_out, text_out, shaped((2, *text_out.shape), BF)], micros=1
    )
    text_sent = partner(text_send, 1)
    text_half = added(text_keep1, text_sent[1])
    text_across = partner(text_half, 2)
    one_across = after(one_across, text_half, head_rows, feed_sum)
    head_sum = lax.psum_scatter(after(head_rows, feed_sum), SEQ, scatter_dimension=0, tiled=True)
    grad_rows = run(
        entry_back_kernel,
        ids,
        (one_keep0, one_sent, one_across, tokens, row(entry_gain), resid),
        [wide(BF)],
        in_specs=[None] * 3 + [own_rows(model)] + [None] * 2,
        micros=2,
        vmem=60,
    )[0]
    grad_pieces = gather(grad_rows)

    text_own = added(text_keep0, text_sent[0], after(text_across, grad_rows))
    entry_sum.step(ids, grad_rows)
    prompt_all = to_all(jnp.concatenate([own_pair, text_own], axis=1))
    flat_text = text_states.reshape(items * prompt_rows, model)
    key_prompt, value_prompt = tn(flat_text, prompt_all[:, :width]), tn(flat_text, prompt_all[:, width : 2 * width])
    text_grad = prompt_all[:, 2 * width :].astype(F32).reshape(items, prompt_rows, width)

    tokens_grad = assemble(ids, grad_pieces, F32)
    out_rows = added(after_cross, out0, out_sent1, out_across)
    out_pieces = gather(after(out_rows, grad_rows))
    layer_output = assemble(ids, out_pieces, BF)

    part = model // shards
    square, turned_square = shaped((part, width), F32), shaped((width, part), F32)
    expand_grad, shrink_grad, pq_grad, pm_grad, merge_grad, wq_grad, wk_grad, wv_grad, norm_sum = run(
        arrived_kernel,
        None,
        (feed_sum, head_sum, *entry_sum.last(ids, grad_rows)),
        [shaped((part, hidden_units), F32), shaped((hidden_units, part), F32)]
        + [square, turned_square, turned_square, square, square, square, shaped((8, part), F32)],
        micros=3,
    )
    norm_sum = norm_sum + partner(norm_sum, 1)
    norm_sum = norm_sum + partner(norm_sum, 2)
    return (
        layer_output,
        tokens_grad,
        text_grad,
        norm_sum[0],
        norm_sum[1],
        norm_sum[4],
        norm_sum[5],
        norm_sum[2],
        norm_sum[3],
        wq_grad,
        wk_grad,
        wv_grad,
        merge_grad,
        pq_grad,
        key_prompt,
        value_prompt,
        pm_grad,
        expand_grad,
        shrink_grad,
    )


def solution(mesh):
    shards = mesh.shape["seq"]
    mesh = jax.sharding.Mesh(mesh.devices.reshape(shards // 2, 2, mesh.shape["mp"]), (*SEQ, "mp"))
    seq, mp, both = P(SEQ, None), P("mp", None), P(None, "mp")
    return jax.shard_map(
        body,
        mesh=mesh,
        in_specs=(seq,) + (P(),) * 9 + (both,) * 3 + (mp,) + (both,) * 3 + (mp, both, mp, seq),
        out_specs=(
            (seq, seq, P(None, None, "mp"))
            + (P(SEQ),) * 6
            + (P(SEQ, "mp"),) * 3
            + (P("mp", SEQ), P(SEQ, "mp"), both, both, P("mp", SEQ), P(SEQ, "mp"), P("mp", SEQ))
        ),
        check_vma=False,
    )
```

```python
import functools

import jax
import jax.numpy as jnp
from jax import lax
from jax.experimental import pallas as pl
from jax.experimental.pallas import tpu as pltpu
from jax.sharding import PartitionSpec as P

HD = 64
ITEM_LEN = 1024
EPS = 1e-06
NEGATIVE = -1e30
BF = jnp.bfloat16
F32 = jnp.float32
BLOCK = 256
SCALE = HD**-0.5
MIB = 1 << 20


def dot(left, right, ld, rd):
    return lax.dot_general(left, right, (((ld,), (rd,)), ((), ())), preferred_element_type=F32)


def nn(left, right):
    return dot(left, right, 1, 0)


def nt(left, right):
    return dot(left, right, 1, 1)


def tn(left, right):
    return dot(left, right, 0, 0)


def partner(value, step):
    count = lax.axis_size("mp")
    return lax.ppermute(value, "mp", [(rank, rank ^ step) for rank in range(count)])


SEQ = ("far", "near")


def from_behind(value, steps):
    count = lax.axis_size("far") * lax.axis_size("near")
    leading, last = (max(0, -steps), min(count, count - steps))
    return lax.ppermute(value, SEQ, [(source, source + steps) for source in range(leading, last)])


def shard_bits():
    return (lax.axis_size("far") * lax.axis_size("near")).bit_length() - 1


def across_bit(value, bit):
    return lax.ppermute(value, SEQ, [(shard, shard ^ (1 << bit)) for shard in range(1 << shard_bits())])


def own_bit(bit):
    return lax.axis_index(SEQ) // (1 << bit) % 2


def step_kernel(bit, ids, kept, sent, kept_o, send_o):
    own = lax.shift_right_logical(ids[0], bit) % 2
    kept_o[0] = (kept[own].astype(F32) + sent[own].astype(F32)).astype(BF)
    send_o[0] = (kept[1 - own].astype(F32) + sent[1 - own].astype(F32)).astype(BF)


class ShardSum:
    def __init__(self, kept, send):
        self.left = list(range(1, shard_bits()))
        self.kept, self.sent = kept, across_bit(send, 0)

    def step(self, ids, *others):
        blocks, part, columns = self.kept.shape
        half = pl.BlockSpec((1, part, columns), lambda j, s: (j, 0, 0))
        self.kept, send = run(
            functools.partial(step_kernel, self.left[0]),
            ids,
            (self.kept, after(self.sent, *others)),
            [shaped((blocks // 2, part, columns), BF)] * 2,
            grid=(blocks // 2,),
            in_specs=[pl.BlockSpec((2, part, columns), lambda j, s: (j, 0, 0))] * 2,
            out_specs=[half, half],
            micros=2,
        )
        self.sent = across_bit(send, self.left[0])
        self.left = self.left[1:]

    def last(self, ids, *others):
        while self.left:
            self.step(ids, *others)
        rows = lambda value: value.reshape(-1, value.shape[-1])
        return rows(self.kept), rows(after(self.sent, *others))


def double(value, have, bit):
    other = across_bit(value, bit)
    dim = sorted([*have, bit], reverse=True).index(bit)
    low = own_bit(bit) == 0
    return jnp.stack([jnp.where(low, value, other), jnp.where(low, other, value)], axis=dim)


def to_all(own):
    have = []
    value = own
    for bit in reversed(range(shard_bits())):
        value = double(value, have, bit)
        have.append(bit)
    return value.reshape(-1, own.shape[-1])


def added(*terms):
    total = terms[0].astype(F32)
    for term in terms[1:]:
        total = total + term.astype(F32)
    return total.astype(BF)


def whole(array):
    rank = len(array.shape)
    return pl.BlockSpec(array.shape, lambda *_: (0,) * rank)


def shaped(shape, dtype):
    return jax.ShapeDtypeStruct(shape, dtype)


def run(kernel, ids, args, outs, grid=(1,), in_specs=None, out_specs=None, scratch=(), micros=1, vmem=40):
    in_specs = in_specs or [None] * len(args)
    out_specs = out_specs or [None] * len(outs)
    in_specs = [whole(a) if s is None else s for a, s in zip(args, in_specs)]
    out_specs = [whole(a) if s is None else s for a, s in zip(outs, out_specs)]
    prefetch = () if ids is None else (ids,)
    return pl.pallas_call(
        functools.partial(kernel, None) if ids is None else kernel,
        out_shape=outs,
        grid_spec=pltpu.PrefetchScalarGridSpec(
            num_scalar_prefetch=len(prefetch),
            grid=grid,
            in_specs=in_specs,
            out_specs=out_specs,
            scratch_shapes=list(scratch),
        ),
        compiler_params=pltpu.CompilerParams(vmem_limit_bytes=vmem * MIB),
        cost_estimate=pl.CostEstimate(flops=int(micros * 0.5e9), transcendentals=0, bytes_accessed=1000),
    )(*prefetch, *args)


def after(value, *others):
    return lax.optimization_barrier((value, *others))[0]


def ln_rows(values):
    centred = values - jnp.mean(values, axis=-1, keepdims=True)
    spread = jnp.mean(centred * centred, axis=-1, keepdims=True)
    inverse = lax.rsqrt(spread + EPS)
    return centred * inverse, inverse


def ln_back(grad, gain, normed, inverse):
    scaled = grad * gain
    first = jnp.mean(scaled, axis=-1, keepdims=True)
    second = jnp.mean(scaled * normed, axis=-1, keepdims=True)
    return inverse * (scaled - first - normed * second)


def head_mask(head, heads):
    lanes = lax.broadcasted_iota(jnp.int32, (1, heads * HD), 1)
    return jnp.where(lanes // HD == head, 1.0, 0.0).astype(BF)


def by_head(rows, heads):
    return [rows * head_mask(head, heads) for head in range(heads)]


def layout_kernel(rows, lens, prompts, place, ids, begin):
    items = lens.shape[0]
    offset = place[0] * rows
    own_first = offset + place[1] * (rows // 4)
    reach = begin.shape[1]
    positions = offset + lax.broadcasted_iota(jnp.int32, (1, reach), 1)
    found = jnp.zeros((1, reach), jnp.int32)
    lows = [jnp.int32(0)] * (reach // BLOCK)
    begun = base = own_base = jnp.int32(0)
    for item in range(items):
        found = jnp.where(positions >= begun, begun, found)
        lows = [jnp.where(offset + block * BLOCK >= begun, begun, low) for block, low in enumerate(lows)]
        begun = begun + lens[item]
        base = base + jnp.where(begun <= offset, 1, 0)
        own_base = own_base + jnp.where(begun <= own_first, 1, 0)
    begin[...] = jnp.where(positions >= begun, begun, found) - offset
    lows = [jnp.where(offset + block * BLOCK >= begun, begun, low) for block, low in enumerate(lows)]
    base = jnp.minimum(base, items - 3)
    own_base = jnp.minimum(own_base, items - 2)
    begun = bound = jnp.int32(0)
    for item in range(items):
        begun = begun + lens[item]
        bound = jnp.where(own_base == item, begun, bound)
    ids[0] = place[0]
    ids[1] = place[1]
    ids[2] = base
    ids[3] = (own_base - base) * 128
    ids[4] = bound - own_first
    ids[5] = prompts[own_base]
    ids[6] = prompts[own_base + 1]
    ids[7] = 0
    for block, low in enumerate(lows):
        ids[8 + block] = low - offset


def pack_kernel(ids, merge, pq, pm, pack):
    width = pq.shape[1]
    pack[:width, :] = merge[...]
    pack[width : 2 * width, :] = pq[...].T
    pack[2 * width :, :] = pm[...]


def entry_kernel(ids, tok, gain, bias, wq, wk, wv, hid, q, kv, tail):
    width = wq.shape[1]
    normed, _ = ln_rows(tok[...].astype(F32))
    hidden = (normed * gain[...] + bias[...]).astype(BF)
    hid[...] = hidden
    kv[:, :width] = nn(hidden, wk[...]).astype(BF)
    kv[:, width:] = nn(hidden, wv[...]).astype(BF)
    q[...] = (nn(hidden, wq[...]).astype(BF) * SCALE).astype(BF)

    @pl.when(pl.program_id(0) == pl.num_programs(0) - 1)
    def _():
        tail[...] = kv[...]


def prompt_kernel(ids, text, pk, pv, out):
    width = pk.shape[1]
    out[:, :width] = nn(text[0], pk[...]).astype(BF)
    out[:, width:] = nn(text[0], pv[...]).astype(BF)


def window_bias(key_base, query_base, begin):
    shape = (BLOCK, BLOCK)
    key = key_base + lax.broadcasted_iota(jnp.int32, shape, 0)
    query = query_base + lax.broadcasted_iota(jnp.int32, shape, 1)
    return jnp.where((key <= query) & (key >= begin), 0.0, NEGATIVE).astype(F32)


def attend_block(keys, values_t, queries, bias, top, total, acc):
    heads = range(len(queries))
    before, sums, held = top[...], total[...], [acc[head] for head in heads]
    scores = [nt(keys, query) + bias for query in queries]
    after = [jnp.maximum(before[h : h + 1, :], jnp.max(scores[h], axis=0, keepdims=True)) for h in heads]
    unnorm = [jnp.exp(scores[h] - after[h]) for h in heads]
    fade = [jnp.exp(before[h : h + 1, :] - after[h]) for h in heads]
    parts = [nn(values_t[h * HD : (h + 1) * HD, :], unnorm[h].astype(BF)) for h in heads]
    added_up = [sums[h : h + 1, :] * fade[h] + jnp.sum(unnorm[h], axis=0, keepdims=True) for h in heads]
    for h in heads:
        acc[h] = held[h] * fade[h] + parts[h]
    top[...] = jnp.concatenate(after, axis=0)
    total[...] = jnp.concatenate(added_up, axis=0)


def attend_local_kernel(ids, q, kv, begin, acc_o, top_o, total_o, vt, acc, top, total):
    step = pl.program_id(0)
    width = q.shape[1]
    heads = width // HD
    blocks = kv.shape[0] // BLOCK

    @pl.when(step == 0)
    def _():
        for b in range(blocks):
            vt[b] = kv[b * BLOCK : (b + 1) * BLOCK, width:].T

    queries = by_head(q[...], heads)
    top[...] = jnp.full_like(top, NEGATIVE)
    total[...] = jnp.zeros_like(total)
    acc[...] = jnp.zeros_like(acc)
    low = lax.shift_right_logical(jnp.maximum(ids[8 + step], 0), 8)

    @pl.loop(low, step + 1)
    def _(b):
        row = pl.multiple_of(b * BLOCK, BLOCK)
        bias = window_bias(row, step * BLOCK, begin[...])
        attend_block(kv[pl.ds(row, BLOCK), :width], vt[b], queries, bias, top, total, acc)

    acc_o[0] = acc[...]
    top_o[0] = top[...]
    total_o[0] = total[...]


def attend_remote_kernel(ids, q, kv, tail, begin, acc_i, top_i, total_i, out, low_out, lse, ship_a, ship_b, ship0, vt, acc, top, total):
    step = pl.program_id(0)
    width = q.shape[1]
    heads = width // HD
    blocks = kv.shape[0] // BLOCK

    @pl.when(step == 0)
    def _():
        vt[0] = tail[:, width:].T
        for b in range(blocks):
            vt[b + 1] = kv[b * BLOCK : (b + 1) * BLOCK, width:].T

    queries = by_head(q[...], heads)
    acc[...] = acc_i[0]
    top[...] = top_i[0]
    total[...] = total_i[0]
    span = (blocks + 1) * BLOCK
    low = lax.shift_right_logical(jnp.maximum(ids[8 + step] + span, 0), 8)

    def bias_of(b):
        return window_bias(b * BLOCK - span, step * BLOCK, begin[...])

    @pl.when(low == 0)
    def _():
        attend_block(tail[:, :width], vt[0], queries, bias_of(0), top, total, acc)

    @pl.loop(jnp.maximum(low, 1), blocks + 1)
    def _(b):
        row = pl.multiple_of((b - 1) * BLOCK, BLOCK)
        attend_block(kv[pl.ds(row, BLOCK), :width], vt[b], queries, bias_of(b), top, total, acc)

    sums = top[...] + jnp.log(total[...])
    lse[0] = sums
    high = sums.astype(BF).astype(F32)
    both = jnp.concatenate([high, sums - high], axis=1)
    stacked = jnp.concatenate([acc[h] * (1.0 / total[h : h + 1, :]) for h in range(heads)], axis=0)
    rows = stacked.T
    out[0] = rows
    low_out[0] = rows.astype(BF)
    half = pl.num_programs(0) // 2

    def put(ship):
        ship[:BLOCK, :width] = q[...]
        ship[:BLOCK, width:] = rows.astype(BF)
        ship[BLOCK:, :] = jnp.concatenate([both, jnp.zeros((16 - heads, 2 * BLOCK), F32)], axis=0).astype(BF)

    @pl.when(step < half)
    def _():
        put(ship_a.at[0])

    @pl.when(step >= half)
    def _():
        put(ship_b.at[0])

    @pl.when(step == 0)
    def _():
        ship0[0] = ship_a[0]


def back_block(keys, values, keys_t, queries, grads, bias, lse, delta, dq, dkv):
    width = keys.shape[1]
    heads = range(len(queries))
    logs, deltas = lse[...], delta[...]
    probs = [jnp.exp(nt(keys, queries[h]) + bias - logs[h : h + 1, :]) for h in heads]
    prob_grads = [nt(values, grads[h]) for h in heads]
    score_grads = [(probs[h] * (prob_grads[h] - deltas[h : h + 1, :])).astype(BF) for h in heads]
    if dkv is not None:
        stack = lambda parts: jnp.concatenate(parts, axis=1)
        low = stack([prob.astype(BF) for prob in probs])
        dkv[:, :width] += nn(stack(score_grads), jnp.concatenate(queries, axis=0))
        dkv[:, width:] += nn(low, jnp.concatenate(grads, axis=0))
    if dq is not None:
        parts = [nn(keys_t[h * HD : (h + 1) * HD, :], score_grads[h]) for h in heads]
        for h in heads:
            dq[h] += parts[h]


def put_delta(delta, grad, out):
    products = (grad.astype(F32) * out.astype(F32)).T
    for head in range(delta.shape[0]):
        delta[head : head + 1, :] = jnp.sum(products[head * HD : (head + 1) * HD, :], axis=0, keepdims=True)


def back_local_kernel(ids, q, kv, begin, grad, out, lse, dkv_o, dq_o, delta_o, kt, dkv):
    step = pl.program_id(0)
    width = q.shape[1]
    heads = width // HD
    blocks = kv.shape[0] // BLOCK

    @pl.when(step == 0)
    def _():
        dkv[...] = jnp.zeros_like(dkv)
        for b in range(blocks):
            kt[b] = kv[b * BLOCK : (b + 1) * BLOCK, :width].T

    put_delta(delta_o.at[0], grad[0], out[0])
    dq_o[...] = jnp.zeros_like(dq_o)
    queries = by_head(q[...], heads)
    grads = by_head(grad[0], heads)
    low = lax.shift_right_logical(jnp.maximum(ids[8 + step], 0), 8)

    @pl.loop(low, step + 1)
    def _(b):
        row = pl.multiple_of(b * BLOCK, BLOCK)
        pair = kv[pl.ds(row, BLOCK), :]
        bias = window_bias(row, step * BLOCK, begin[...])
        back_block(
            pair[:, :width], pair[:, width:], kt[b], queries, grads, bias, lse.at[0], delta_o.at[0], dq_o.at[0], dkv.at[b]
        )

    @pl.when(step == pl.num_programs(0) - 1)
    def _():
        for b in range(blocks):
            dkv_o[b * BLOCK : (b + 1) * BLOCK, :] = dkv[b]


def back_query_kernel(ids, q, kv, tail, begin, grad, lse, delta, dq_i, dq_o, kt, dq):
    step = pl.program_id(0)
    width = q.shape[1]
    heads = width // HD
    blocks = kv.shape[0] // BLOCK

    @pl.when(step == 0)
    def _():
        kt[0] = tail[:, :width].T
        for b in range(blocks):
            kt[b + 1] = kv[b * BLOCK : (b + 1) * BLOCK, :width].T

    dq[...] = dq_i[0]
    span = (blocks + 1) * BLOCK
    low = lax.shift_right_logical(jnp.maximum(ids[8 + step] + span, 0), 8)

    @pl.when(low <= blocks)
    def _():
        queries = by_head(q[...], heads)
        grads = by_head(grad[0], heads)

        def one(b, pair):
            bias = window_bias(b * BLOCK - span, step * BLOCK, begin[...])
            back_block(pair[:, :width], pair[:, width:], kt[b], queries, grads, bias, lse.at[0], delta.at[0], dq, None)

        @pl.when(low == 0)
        def _():
            one(0, tail[...])

        @pl.loop(jnp.maximum(low, 1), blocks + 1)
        def _(b):
            row = pl.multiple_of((b - 1) * BLOCK, BLOCK)
            one(b, kv[pl.ds(row, BLOCK), :])

    stacked = jnp.concatenate([dq[h] for h in range(heads)], axis=0)
    dq_o[...] = (stacked.T * SCALE).astype(BF)


def back_key_kernel(ids, kv, begin, ship_low, ship_high, grad_n, ship_f, grad_f, dkv_i, dkv_o, delta, lse, dkv):
    step = pl.program_id(0)
    width = kv.shape[1] // 2
    heads = width // HD
    blocks = kv.shape[0] // BLOCK

    @pl.when(step == 0)
    def _():
        for b in range(blocks):
            dkv[b] = dkv_i[b * BLOCK : (b + 1) * BLOCK, :]

    low = lax.shift_right_logical(jnp.maximum(ids[8 + blocks + step], 0), 8)

    def all_keys(ship, grad):
        put_delta(delta, grad, ship[:BLOCK, width:])
        parts = ship[BLOCK:, :].astype(F32)
        lse[...] = parts[:heads, :BLOCK] + parts[:heads, BLOCK:]
        queries, grads = by_head(ship[:BLOCK, :width], heads), by_head(grad, heads)

        @pl.loop(low, blocks)
        def _(b):
            row = pl.multiple_of(b * BLOCK, BLOCK)
            pair = kv[pl.ds(row, BLOCK), :]
            bias = window_bias(row, blocks * BLOCK + step * BLOCK, begin[...])
            back_block(pair[:, :width], pair[:, width:], None, queries, grads, bias, lse, delta, None, dkv.at[b])

    @pl.when((low < blocks) & (step < blocks // 2))
    def _():
        all_keys(ship_low.at[0], grad_n[0])

    @pl.when((low < blocks) & (step >= blocks // 2) & (step < blocks))
    def _():
        all_keys(ship_high.at[0], grad_n[0])

    @pl.when((low < blocks) & (step == blocks))
    def _():
        all_keys(ship_f.at[0], grad_f[0])

    @pl.when(step == blocks)
    def _():
        for b in range(blocks):
            dkv_o[b * BLOCK : (b + 1) * BLOCK, :] = dkv[b].astype(BF)


def cross_bias(ids, prompt_rows, rows):
    shape = (2 * prompt_rows, rows)
    key = lax.broadcasted_iota(jnp.int32, shape, 0)
    query = lax.broadcasted_iota(jnp.int32, shape, 1)
    key_slot = lax.shift_right_logical(key, prompt_rows.bit_length() - 1)
    query_slot = jnp.where(query >= ids[4], 1, 0)
    limit = jnp.where(key_slot == 1, prompt_rows + ids[6], ids[5])
    return jnp.where((key_slot == query_slot) & (key < limit), 0.0, NEGATIVE).astype(F32)


def cross_kernel(ids, tok, low, *refs):
    packs, pairs = refs[:4], refs[4:8]
    gain2, bias2, gain3, bias3 = refs[8:12]
    after_self_o, two_o, q_o, stat_o, out_o, after_o, three_o = refs[12:]
    rows = tok.shape[0]
    width = packs[0].shape[0] // 3
    heads = width // HD
    rank = ids[1]
    prompt_rows = pairs[0].shape[0] // 3
    after = tok[...].astype(F32)
    for d in range(4):
        after = after + nn(low[rank ^ d], packs[d][:width, :])
    after_self_o[...] = after
    normed, _ = ln_rows(after)
    hidden = (normed * gain2[...] + bias2[...]).astype(BF)
    two_o[...] = hidden
    bias = cross_bias(ids, prompt_rows, rows)
    first = pl.multiple_of(ids[3], prompt_rows)
    for d in range(4):
        columns = slice(d * width, (d + 1) * width)
        query_rows = (nt(hidden, packs[d][width : 2 * width, :]).astype(BF) * SCALE).astype(BF)
        q_o[:, columns] = query_rows
        keys = pairs[d][pl.ds(first, 2 * prompt_rows), :width]
        values_t = pairs[d][pl.ds(first, 2 * prompt_rows), width:].T
        each = range(heads)
        scores = [nt(keys, query) + bias for query in by_head(query_rows, heads)]
        tops = [jnp.max(score, axis=0, keepdims=True) for score in scores]
        unnorm = [jnp.exp(scores[h] - tops[h]) for h in each]
        totals = [jnp.sum(value, axis=0, keepdims=True) for value in unnorm]
        stat_o[d * heads : (d + 1) * heads, :] = jnp.concatenate([tops[h] + jnp.log(totals[h]) for h in each], axis=0)
        parts = [nn(values_t[h * HD : (h + 1) * HD, :], unnorm[h].astype(BF)) * (1.0 / totals[h]) for h in each]
        out_o[:, columns] = jnp.concatenate(parts, axis=0).T.astype(BF)
    after = after_self_o[...]
    for d in range(4):
        after = after + nn(out_o[:, d * width : (d + 1) * width], packs[d][2 * width :, :])
    after_o[...] = after
    normed, _ = ln_rows(after)
    three_o[...] = (normed * gain3[...] + bias3[...]).astype(BF)


def cross_back_kernel(ids, kept, sent, crossed, og, after, after_self, q, stat, *refs):
    packs, pairs = refs[:4], refs[4:8]
    gain2, gain3 = refs[8:10]
    cog_o, cqg_o, slg_o, resid_o, shg_o, keep0_o, keep1_o, send_o, norms_o = refs[10:]
    rows, model = after.shape
    width = packs[0].shape[0] // 3
    heads = width // HD
    rank = ids[1]
    prompt_rows = pairs[0].shape[0] // 3
    grad = kept[...].astype(F32) + sent[...].astype(F32) + crossed[...].astype(F32)
    normed, inverse = ln_rows(after[...])
    norms_o[0:1, :] = jnp.sum(grad * normed, axis=0, keepdims=True)
    norms_o[1:2, :] = jnp.sum(grad, axis=0, keepdims=True)
    resid = og[...].astype(F32) + ln_back(grad, gain3[...], normed, inverse)
    low_resid = resid.astype(BF)
    cog_o[...] = low_resid
    bias = cross_bias(ids, prompt_rows, rows)
    first = pl.multiple_of(ids[3], prompt_rows)
    keep0_o[...] = jnp.zeros_like(keep0_o)
    keep1_o[...] = jnp.zeros_like(keep1_o)
    send_o[...] = jnp.zeros_like(send_o)
    for d in range(4):
        columns = slice(d * width, (d + 1) * width)
        head_grad = nt(low_resid, packs[d][2 * width :, :]).astype(BF)
        keys = pairs[d][pl.ds(first, 2 * prompt_rows), :width]
        values = pairs[d][pl.ds(first, 2 * prompt_rows), width:]
        keys_t = keys.T
        each = range(heads)
        queries, grads = by_head(q[:, columns], heads), by_head(head_grad, heads)
        logs = stat[d * heads : (d + 1) * heads, :]
        probs = [jnp.exp(nt(keys, queries[h]) + bias - logs[h : h + 1, :]) for h in each]
        prob_grads = [nt(values, grads[h]) for h in each]
        deltas = [jnp.sum(probs[h] * prob_grads[h], axis=0, keepdims=True) for h in each]
        score_grads = [(probs[h] * (prob_grads[h] - deltas[h])).astype(BF) for h in each]
        key_sum = nn(jnp.concatenate(score_grads, axis=1), jnp.concatenate(queries, axis=0))
        value_sum = nn(jnp.concatenate([prob.astype(BF) for prob in probs], axis=1), jnp.concatenate(grads, axis=0))
        parts = [nn(keys_t[h * HD : (h + 1) * HD, :], score_grads[h]) for h in each]
        cqg_o[:, columns] = (jnp.concatenate(parts, axis=0).T * SCALE).astype(BF)
        target = (keep0_o, send_o.at[0], keep1_o, send_o.at[1])[d]
        target[pl.ds(first, 2 * prompt_rows), :width] = key_sum.astype(BF)
        target[pl.ds(first, 2 * prompt_rows), width:] = value_sum.astype(BF)
    two_grad = None
    for d in range(4):
        term = nn(cqg_o[:, d * width : (d + 1) * width], packs[d][width : 2 * width, :])
        two_grad = term if two_grad is None else two_grad + term
    normed, inverse = ln_rows(after_self[...])
    norms_o[2:3, :] = jnp.sum(two_grad * normed, axis=0, keepdims=True)
    norms_o[3:4, :] = jnp.sum(two_grad, axis=0, keepdims=True)
    resid = resid + ln_back(two_grad, gain2[...], normed, inverse)
    resid_o[...] = resid
    low_resid = resid.astype(BF)
    slg_o[...] = low_resid
    for d in range(4):
        shg_o[rank ^ d] = nt(low_resid, packs[d][:width, :]).astype(BF)


def feed_kernel(ids, h_a, h_b, dh_a, dh_b, expand, shrink, *outs):
    c = 0.7978845608028654

    def rows(h, dh, low_o, pre_o, out_o, three_o):
        v = nn(h[...], expand[...])
        square = v * v
        t = jnp.tanh(v * (c + (c * 0.044715) * square))
        half = 0.5 * (1.0 + t)
        low = (v * half).astype(BF)
        slope = half + (v * (1.0 - t * t)) * (0.5 * c + (1.5 * c * 0.044715) * square)
        pre = (dh[...].astype(F32) * slope).astype(BF)
        low_o[...] = low
        pre_o[...] = pre
        out_o[...] = nn(low, shrink[...]).astype(BF)
        three_o[...] = nt(pre, expand[...]).astype(BF)

    half = pl.num_programs(0) // 2

    @pl.when(pl.program_id(0) < half)
    def _():
        rows(h_a, dh_a, *outs[:4])

    @pl.when(pl.program_id(0) >= half)
    def _():
        rows(h_b, dh_b, *outs[4:])


def feed(ids, base, h_a, h_b, dh, expand, shrink):
    rows, model = h_a.shape
    hidden = expand.shape[1]
    tile = 128
    tiles = rows // tile
    first, second = lambda j: jnp.minimum(j, tiles - 1), lambda j: jnp.maximum(j - tiles, 0)
    spec = lambda columns, at: pl.BlockSpec((tile, columns), lambda j, s: (at(j), 0))
    own = lambda d, at: pl.BlockSpec((tile, hidden), lambda j, s: ((s[1] ^ d) * tiles + at(j), 0))
    outs = lambda at: [spec(hidden, at), spec(hidden, at), spec(model, at), spec(model, at)]
    return run(
        feed_kernel,
        ids,
        (h_a, h_b, dh, dh, expand, shrink),
        [shaped((rows, hidden), BF), shaped((rows, hidden), BF), shaped((rows, model), BF), shaped((rows, model), BF)] * 2,
        grid=(2 * tiles,),
        in_specs=[spec(model, first), spec(model, second), own(base, first), own(base + 1, second), None, None],
        out_specs=outs(first) + outs(second),
        micros=12,
    )


def spread(ids, rows, kept, send):
    far, part, _ = kept.shape
    own = ids[0] % 2
    for block in range(far):
        kept[block] = rows[pl.ds(pl.multiple_of((2 * block + own) * part, part), part), :]
        send[block] = rows[pl.ds(pl.multiple_of((2 * block + 1 - own) * part, part), part), :]


def feed_weights_kernel(ids, *refs):
    threes, pres, lows = refs[:4], refs[4:8], refs[8:12]
    og, out, turned = refs[12:]
    step = pl.program_id(0)
    half = pl.num_programs(0) // 2
    rank = ids[1]
    rows = threes[0].shape[0]

    @pl.when(step == 0)
    def _():
        for d in range(4):
            turned[:, d * rows : (d + 1) * rows] = threes[d][...].T

    @pl.when(step == half)
    def _():
        for d in range(4):
            turned[:, d * rows : (d + 1) * rows] = og[pl.ds(pl.multiple_of((rank ^ d) * rows, rows), rows), :].T

    @pl.when(step < half)
    def _():
        out[...] = nn(turned[...], jnp.concatenate([p[...] for p in pres], axis=0)).astype(BF)

    @pl.when(step >= half)
    def _():
        out[...] = nn(turned[...], jnp.concatenate([p[...] for p in lows], axis=0)).astype(BF)


def feed_weights(ids, threes, pres, lows, og):
    rows, model = threes[0].shape
    hidden = pres[0].shape[1]
    chunk = 256
    half = hidden // chunk
    front = pl.BlockSpec((rows, chunk), lambda j, s: (0, jnp.minimum(j, half - 1)))
    back = pl.BlockSpec((rows, chunk), lambda j, s: (0, jnp.maximum(j - half, 0)))
    return run(
        feed_weights_kernel,
        ids,
        (*threes, *pres, *lows, og),
        [shaped((model, 2 * hidden), BF)],
        grid=(2 * half,),
        in_specs=[None] * 4 + [front] * 4 + [back] * 4 + [None],
        out_specs=[pl.BlockSpec((model, chunk), lambda j, s: (0, j))],
        scratch=[pltpu.VMEM((model, 4 * rows), BF)],
        micros=9,
        vmem=60,
    )[0]


def head_weights_kernel(ids, two, cqg, cog, crossed, slg, low, keep0, keep1, send):
    rank = ids[1]
    width = low.shape[2]
    two_t, cog_t, slg_t = two[...].T, cog[...].T, slg[...].T
    for d, out in enumerate((keep0, send.at[0], keep1, send.at[1])):
        columns = slice(d * width, (d + 1) * width)
        out[:, :width] = nn(two_t, cqg[:, columns]).astype(BF)
        out[:, width : 2 * width] = nn(cog_t, crossed[:, columns]).astype(BF)
        out[:, 2 * width :] = nn(slg_t, low[rank ^ d]).astype(BF)


def one_grad_kernel(ids, kvg, hid, dq, wq, wk, wv, gain, bias, keep0, keep1, send, norms):
    rows, width2 = kvg.shape
    width = width2 // 2
    quarter = rows // 4
    rank = ids[1]
    product = total = None
    for d in (1, 3, 2, 0):
        own = pl.ds(pl.multiple_of((rank ^ d) * quarter, quarter), quarter)
        part = (
            nt(dq[own, :], wq[...]) + nt(kvg[own, :width], wk[...]) + nt(kvg[own, width:], wv[...])
        )
        hidden = hid[own, :].astype(F32)
        term = jnp.sum(part * hidden, axis=0, keepdims=True)
        plain = jnp.sum(part, axis=0, keepdims=True)
        product = term if product is None else product + term
        total = plain if total is None else total + plain
        (keep0, send.at[0], keep1, send.at[1])[d][...] = part.astype(BF)
    norms[0:1, :] = (product - bias[...] * total) / gain[...]
    norms[1:2, :] = total


def text_kernel(ids, own, pk, pv, keep0, keep1, send):
    width = own.shape[1] // 2
    rank = ids[1]
    for d, out in enumerate((keep0, send.at[0], keep1, send.at[1])):
        columns = pl.ds(pl.multiple_of((rank ^ d) * width, width), width)
        out[...] = (nt(own[:, :width], pk[columns, :]) + nt(own[:, width:], pv[columns, :])).astype(BF)


def entry_weights_kernel(ids, hid, dq, kvg, entry_norms, norms, kept, send, rows):
    width = dq.shape[1]
    model = hid.shape[1]
    turned = hid[...].T
    rows[:, :width] = nn(turned, dq[...]).astype(BF)
    rows[:, width : 3 * width] = nn(turned, kvg[...]).astype(BF)
    sums = jnp.concatenate([entry_norms[...], norms[...], jnp.zeros((122, model), F32)], axis=0)
    rows[:, 3 * width :] = sums.T.astype(BF)
    spread(ids, rows, kept, send)


def arrived_kernel(ids, *refs):
    feed, head, entry, (expand, shrink, pq, pm, merge, wq, wk, wv, norms) = refs[:1], refs[1:2], refs[2:4], refs[4:]

    def total(terms, width, index):
        columns = slice(index * width, (index + 1) * width)
        value = terms[0][:, columns].astype(F32)
        for term in terms[1:]:
            value = value + term[:, columns].astype(F32)
        return value

    hidden, width = expand.shape[1], pq.shape[1]
    expand[...] = total(feed, hidden, 0)
    shrink[...] = total(feed, hidden, 1).T
    pq[...] = total(head, width, 0)
    pm[...] = total(head, width, 1).T
    merge[...] = total(head, width, 2).T
    wq[...] = total(entry, width, 0)
    wk[...] = total(entry, width, 1)
    wv[...] = total(entry, width, 2)
    norms[...] = total(entry, 128, 3 * width // 128).T[:8, :]


def entry_back_kernel(ids, keep, sent, crossed, tok, gain, resid, out):
    grad = keep[...].astype(F32) + sent[0].astype(F32) + crossed[...].astype(F32)
    normed, inverse = ln_rows(tok[...].astype(F32))
    out[...] = (resid[...] + ln_back(grad, gain[...], normed, inverse)).astype(BF)


def assemble_kernel(ids, *refs):
    out = refs[4]
    for d in range(4):

        @pl.when(pl.program_id(0) == ids[1] ^ d)
        def _():
            out[...] = refs[d][...].astype(out.dtype)


def assemble(ids, pieces, dtype):
    rows, model = pieces[0].shape
    return run(
        assemble_kernel,
        ids,
        pieces,
        [shaped((4 * rows, model), dtype)],
        grid=(4,),
        out_specs=[pl.BlockSpec((rows, model), lambda i, s: (i, 0))],
        micros=3,
    )[0]


def gather(own):
    across = partner(own, 2)
    near = partner(own, 1)
    return own, near, across, partner(across, 1)


def body(
    tokens,
    text_states,
    item_lengths,
    prompt_lengths,
    entry_gain,
    entry_bias,
    cross_gain,
    cross_bias_,
    mixer_gain,
    mixer_bias,
    query_weight,
    key_weight,
    value_weight,
    merge_weight,
    prompt_query,
    prompt_key,
    prompt_value,
    prompt_merge,
    expand_weight,
    shrink_weight,
    output_grad,
):
    rows, model = tokens.shape
    ranks = lax.axis_size("mp")
    width = query_weight.shape[1]
    heads = width // HD
    items, prompt_rows = text_states.shape[:2]
    quarter = rows // ranks
    steps = rows // BLOCK
    hidden_units = expand_weight.shape[1]
    shards = lax.axis_size("far") * lax.axis_size("near")
    assert ranks == 4 and quarter == BLOCK and prompt_rows == 128 and items % shards == 0

    place = jnp.stack([lax.axis_index(SEQ), lax.axis_index("mp")]).astype(jnp.int32)
    scalars = pl.BlockSpec(memory_space=pltpu.SMEM)
    ids, begin = pl.pallas_call(
        functools.partial(layout_kernel, rows),
        out_shape=[shaped((9 + 2 * steps + 7,), jnp.int32), shaped((1, 2 * rows + BLOCK), jnp.int32)],
        in_specs=[scalars] * 3,
        out_specs=[scalars, pl.BlockSpec(memory_space=pltpu.VMEM)],
    )(item_lengths, prompt_lengths, place)
    base = ids[2]

    row = lambda vector: vector.reshape(1, -1)
    own_rows = lambda columns: pl.BlockSpec((quarter, columns), lambda *g: (g[-1][1], 0))

    block_rows = lambda columns: pl.BlockSpec((BLOCK, columns), lambda i, *s: (i, 0))
    pack = run(pack_kernel, None, (merge_weight, prompt_query, prompt_merge), [shaped((3 * width, model), BF)], vmem=60)[0]
    pack_near, pack_across = partner(pack, 1), partner(pack, 2)
    hidden_one, q, kv, kv_tail = run(
        entry_kernel,
        None,
        (after(tokens, pack), row(entry_gain), row(entry_bias), query_weight, key_weight, value_weight),
        [
            shaped((rows, model), BF),
            shaped((rows, width), BF),
            shaped((rows, 2 * width), BF),
            shaped((BLOCK, 2 * width), BF),
        ],
        grid=(steps,),
        in_specs=[block_rows(model)] + [None] * 5,
        out_specs=[block_rows(model), block_rows(width), block_rows(2 * width), None],
        micros=2,
        vmem=60,
    )
    kv_near = from_behind(kv, 1)
    kv_far = from_behind(kv_tail, 2)

    pair = run(
        prompt_kernel,
        ids,
        (after(text_states, kv, pack_near), prompt_key, prompt_value),
        [shaped((3 * prompt_rows, 2 * width), BF)],
        grid=(3,),
        in_specs=[pl.BlockSpec((1, prompt_rows, model), lambda i, s: (s[2] + i, 0, 0)), None, None],
        out_specs=[pl.BlockSpec((prompt_rows, 2 * width), lambda i, s: (i, 0))],
        micros=1.5,
    )[0]
    pair_near, pair_across = partner(pair, 1), partner(pair, 2)
    hidden_grad = nt(after(output_grad, kv, pair), shrink_weight).astype(BF)

    state = [shaped((steps, heads, HD, BLOCK), F32), shaped((steps, heads, BLOCK), F32), shaped((steps, heads, BLOCK), F32)]
    state_specs = [
        pl.BlockSpec((1, heads, HD, BLOCK), lambda i, s: (i, 0, 0, 0)),
        pl.BlockSpec((1, heads, BLOCK), lambda i, s: (i, 0, 0)),
        pl.BlockSpec((1, heads, BLOCK), lambda i, s: (i, 0, 0)),
    ]
    state_scratch = [pltpu.VMEM((heads, HD, BLOCK), F32), pltpu.VMEM((heads, BLOCK), F32), pltpu.VMEM((heads, BLOCK), F32)]
    q_spec = block_rows(width)
    begin_spec = pl.BlockSpec((1, BLOCK), lambda i, s: (0, i))
    piece_spec = pl.BlockSpec((1, BLOCK, width), lambda i, s: (i, 0, 0))
    turned = lambda blocks: pltpu.VMEM((blocks, width, BLOCK), BF)
    acc, top, total = run(
        attend_local_kernel,
        ids,
        (after(q, pair_near), kv, begin),
        state,
        grid=(steps,),
        in_specs=[q_spec, None, begin_spec],
        out_specs=state_specs,
        scratch=[turned(steps)] + state_scratch,
        micros=13,
    )
    kv_near, kv_far = lax.optimization_barrier((kv_near, kv_far, acc, hidden_grad))[:2]
    def ship_spec(side):
        half = steps // 2
        index = (lambda i: jnp.maximum(i - half, 0)) if side else (lambda i: jnp.minimum(i, half - 1))
        return pl.BlockSpec((1, BLOCK + 16, 2 * width), lambda i, s: (index(jnp.minimum(i, steps - 1)), 0, 0))

    self_out, self_low, lse, ship_low, ship_high, ship_first = run(
        attend_remote_kernel,
        ids,
        (q, kv_near, kv_far, begin, acc, top, total),
        [shaped((steps, BLOCK, width), F32), shaped((steps, BLOCK, width), BF), shaped((steps, heads, BLOCK), F32)]
        + [shaped((blocks, BLOCK + 16, 2 * width), BF) for blocks in (steps // 2, steps // 2, 1)],
        grid=(steps,),
        in_specs=[q_spec, None, None, begin_spec] + state_specs,
        out_specs=[piece_spec, piece_spec, state_specs[1], ship_spec(0), ship_spec(1), None],
        scratch=[turned(steps + 1)] + state_scratch,
        micros=9,
    )
    low_rows = lax.all_to_all(self_low, "mp", 0, 0)
    pack_across, pair_across = lax.optimization_barrier((pack_across, pair_across, self_low))[:2]
    packs = (pack, pack_near, pack_across, partner(pack_across, 1))
    pairs = (pair, pair_near, pair_across, partner(pair_across, 1))

    wide = lambda dtype: shaped((quarter, model), dtype)
    stat_shape = shaped((ranks * heads, quarter), F32)
    norms = (row(cross_gain), row(cross_bias_), row(mixer_gain), row(mixer_bias))
    after_self, hidden_two, cross_q, stat, cross_out, after_cross, hidden_three = run(
        cross_kernel,
        ids,
        (tokens, low_rows, *packs, *pairs, *norms),
        [wide(F32), wide(BF), wide(BF), stat_shape, wide(BF), wide(F32), wide(BF)],
        in_specs=[own_rows(model)] + [None] * 13,
        micros=11,
    )

    ship_low, ship_high, ship_f = after((ship_low, ship_high, ship_first), hidden_three)
    ship_low, ship_f = from_behind(ship_low, -1), from_behind(ship_f, -2)

    three_near, three_across = partner(hidden_three, 1), partner(hidden_three, 2)
    low0, pre0, out0, part0, low1, pre1, out1, part1 = feed(
        ids, 0, hidden_three, three_near, hidden_grad, expand_weight, shrink_weight
    )
    three_across, ship_low, ship_f = after((three_across, ship_low, ship_f), part1)
    ship_high = from_behind(after(ship_high, ship_low), -1)
    threes = (hidden_three, three_near, three_across, partner(three_across, 1))
    sent1, out_sent1 = partner(part1, 1), partner(out1, 1)
    low2, pre2, out2, part2, low3, pre3, out3, part3 = feed(
        ids, 2, threes[2], threes[3], hidden_grad, expand_weight, shrink_weight
    )
    part3, sent1, out_sent1, ship_high = after((part3, sent1, out_sent1, ship_high), part2)
    partial = (part2.astype(F32) + partner(part3, 1).astype(F32)).astype(BF)
    across = partner(partial, 2)
    out_partial = (out2.astype(F32) + partner(after(out3, partial), 1).astype(F32)).astype(BF)
    feed_grads = feed_weights(ids, threes, after((pre0, pre1, pre2, pre3), partial), (low0, low1, low2, low3), output_grad)
    feed_sum = lax.psum_scatter(feed_grads, SEQ, scatter_dimension=0, tiled=True)
    across = after(across, feed_grads, out_partial)
    out_across = partner(after(out_partial, across), 2)

    pair_out = shaped((3 * prompt_rows, 2 * width), BF)
    cog, cqg, slg, resid, shg, pair_keep0, pair_keep1, pair_send, norm_grads = run(
        cross_back_kernel,
        ids,
        (part0, sent1, across, output_grad, after_cross, after_self, cross_q, stat, *packs, *pairs, norms[0], norms[2]),
        [wide(BF), wide(BF), wide(BF), wide(F32), shaped((ranks, quarter, width), BF)]
        + [pair_out, pair_out, shaped((2, *pair_out.shape), BF), shaped((4, model), F32)],
        in_specs=[None] * 3 + [own_rows(model)] + [None] * 14,
        micros=15,
        vmem=48,
    )
    self_grad = lax.all_to_all(shg, "mp", 0, 0)

    pair_sent = partner(pair_send, 1)
    pieces = shaped((model, 3 * width), BF)
    head_keep0, head_keep1, head_send = run(
        head_weights_kernel,
        ids,
        (hidden_two, cqg, cog, cross_out, slg, low_rows),
        [pieces, pieces, shaped((2, *pieces.shape), BF)],
        micros=5,
        vmem=60,
    )
    head_sent = partner(head_send, 1)
    head_half = added(head_keep1, head_sent[1])
    self_grad, out_across, pair_sent, head_half = after((self_grad, out_across, pair_sent, head_half), head_keep0)
    head_across = partner(head_half, 2)
    grad_n, grad_f = from_behind(self_grad, -1), from_behind(self_grad[:1], -2)
    pair_half = added(pair_keep1, pair_sent[1])
    pair_across = partner(pair_half, 2)

    lse_spec = state_specs[1]
    stat4 = shaped((steps, heads, BLOCK), F32)
    dkv, dq_part, delta = run(
        back_local_kernel,
        ids,
        (q, kv, begin, after(self_grad, pair_half), self_out, lse),
        [shaped((rows, 2 * width), F32), state[0], stat4],
        grid=(steps,),
        in_specs=[q_spec, None, begin_spec, piece_spec, piece_spec, lse_spec],
        out_specs=[None, state_specs[0], lse_spec],
        scratch=[turned(steps), pltpu.VMEM((steps, BLOCK, 2 * width), F32)],
        micros=15,
    )
    pair_across, grad_n, grad_f = after((pair_across, grad_n, grad_f), dq_part)
    pair_sum = added(pair_keep0, pair_sent[0], pair_across).reshape(3, prompt_rows, 2 * width)
    placed = lax.dynamic_update_slice_in_dim(jnp.zeros((items, prompt_rows, 2 * width), BF), pair_sum, base, 0)
    placed = placed.reshape(shards // 2, 2, -1, 2 * width)
    own = own_bit(0)
    text_sum = ShardSum(
        lax.dynamic_index_in_dim(placed, own, 1, keepdims=False), lax.dynamic_index_in_dim(placed, 1 - own, 1, keepdims=False)
    )
    dq = run(
        back_query_kernel,
        ids,
        (q, kv_near, kv_far, begin, self_grad, lse, delta, after(dq_part, text_sum.kept)),
        [shaped((rows, width), BF)],
        grid=(steps,),
        in_specs=[q_spec, None, None, begin_spec, piece_spec, lse_spec, lse_spec, state_specs[0]],
        out_specs=[q_spec],
        scratch=[turned(steps + 1), state_scratch[0]],
        micros=7,
    )[0]
    text_sum.step(ids, dq)
    far = shards // 2
    spread_out = [shaped((far, model // shards, 3 * width + 128), BF)] * 2
    grad_n, grad_f = after((grad_n, grad_f), dq, text_sum.kept)
    held = lambda i: jnp.minimum(i, steps - 1)
    near_piece = pl.BlockSpec((1, BLOCK, width), lambda i, s: (held(i), 0, 0))
    kvg = run(
        back_key_kernel,
        ids,
        (kv, begin, ship_low, ship_high, grad_n, ship_f, grad_f, dkv),
        [shaped((rows, 2 * width), BF)],
        grid=(steps + 1,),
        in_specs=[None, pl.BlockSpec((1, BLOCK), lambda i, s: (0, steps + i)), ship_spec(0), ship_spec(1), near_piece] + [None] * 3,
        scratch=[pltpu.VMEM((heads, BLOCK), F32)] * 2 + [pltpu.VMEM((steps, BLOCK, 2 * width), F32)],
        micros=8,
    )[0]

    quarter_out = shaped((quarter, model), BF)
    one_keep0, one_keep1, one_send, entry_norms = run(
        one_grad_kernel,
        ids,
        (kvg, hidden_one, dq, query_weight, key_weight, value_weight, row(entry_gain), row(entry_bias)),
        [quarter_out, quarter_out, shaped((2, *quarter_out.shape), BF), shaped((2, model), F32)],
        micros=3,
    )
    one_sent = partner(one_send, 1)
    entry_rows = run(
        entry_weights_kernel,
        ids,
        (hidden_one, after(dq, one_send), kvg, entry_norms, norm_grads),
        spread_out,
        scratch=[pltpu.VMEM((model, 3 * width + 128), BF)],
        micros=4,
    )
    entry_sum = ShardSum(*entry_rows)
    head_rows = added(head_keep0, head_sent[0], after(head_across, kvg))
    one_half = added(one_keep1, after(one_sent, entry_rows[0], head_rows)[1])
    one_across = partner(one_half, 2)
    own_pair = added(*text_sum.last(ids, one_half))
    text_out = shaped((prompt_rows * items // shards, width), BF)
    text_keep0, text_keep1, text_send = run(
        text_kernel, ids, (own_pair, prompt_key, prompt_value), [text_out, text_out, shaped((2, *text_out.shape), BF)], micros=1
    )
    text_sent = partner(text_send, 1)
    text_half = added(text_keep1, text_sent[1])
    text_across = partner(text_half, 2)
    one_across = after(one_across, text_half, head_rows, feed_sum)
    head_sum = lax.psum_scatter(after(head_rows, feed_sum), SEQ, scatter_dimension=0, tiled=True)
    grad_rows = run(
        entry_back_kernel,
        ids,
        (one_keep0, one_sent, one_across, tokens, row(entry_gain), resid),
        [wide(BF)],
        in_specs=[None] * 3 + [own_rows(model)] + [None] * 2,
        micros=2,
        vmem=60,
    )[0]
    grad_pieces = gather(grad_rows)

    text_own = added(text_keep0, text_sent[0], after(text_across, grad_rows))
    entry_sum.step(ids, grad_rows)
    prompt_all = to_all(jnp.concatenate([own_pair, text_own], axis=1))
    flat_text = text_states.reshape(items * prompt_rows, model)
    key_prompt, value_prompt = tn(flat_text, prompt_all[:, :width]), tn(flat_text, prompt_all[:, width : 2 * width])
    text_grad = prompt_all[:, 2 * width :].astype(F32).reshape(items, prompt_rows, width)

    tokens_grad = assemble(ids, grad_pieces, F32)
    out_rows = added(after_cross, out0, out_sent1, out_across)
    out_pieces = gather(after(out_rows, grad_rows))
    layer_output = assemble(ids, out_pieces, BF)

    part = model // shards
    square, turned_square = shaped((part, width), F32), shaped((width, part), F32)
    expand_grad, shrink_grad, pq_grad, pm_grad, merge_grad, wq_grad, wk_grad, wv_grad, norm_sum = run(
        arrived_kernel,
        None,
        (feed_sum, head_sum, *entry_sum.last(ids, grad_rows)),
        [shaped((part, hidden_units), F32), shaped((hidden_units, part), F32)]
        + [square, turned_square, turned_square, square, square, square, shaped((8, part), F32)],
        micros=3,
    )
    norm_sum = norm_sum + partner(norm_sum, 1)
    norm_sum = norm_sum + partner(norm_sum, 2)
    return (
        layer_output,
        tokens_grad,
        text_grad,
        norm_sum[0],
        norm_sum[1],
        norm_sum[4],
        norm_sum[5],
        norm_sum[2],
        norm_sum[3],
        wq_grad,
        wk_grad,
        wv_grad,
        merge_grad,
        pq_grad,
        key_prompt,
        value_prompt,
        pm_grad,
        expand_grad,
        shrink_grad,
    )


def solution(mesh):
    shards = mesh.shape["seq"]
    mesh = jax.sharding.Mesh(mesh.devices.reshape(shards // 2, 2, mesh.shape["mp"]), (*SEQ, "mp"))
    seq, mp, both = P(SEQ, None), P("mp", None), P(None, "mp")
    return jax.shard_map(
        body,
        mesh=mesh,
        in_specs=(seq,) + (P(),) * 9 + (both,) * 3 + (mp,) + (both,) * 3 + (mp, both, mp, seq),
        out_specs=(
            (seq, seq, P(None, None, "mp"))
            + (P(SEQ),) * 6
            + (P(SEQ, "mp"),) * 3
            + (P("mp", SEQ), P(SEQ, "mp"), both, both, P("mp", SEQ), P(SEQ, "mp"), P("mp", SEQ))
        ),
        check_vma=False,
    )
```

```python
import functools

import jax
import jax.numpy as jnp
from jax import lax
from jax.experimental import pallas as pl
from jax.experimental.pallas import tpu as pltpu
from jax.sharding import PartitionSpec as P

HD = 64
ITEM_LEN = 1024
EPS = 1e-06
NEGATIVE = -1e30
BF = jnp.bfloat16
F32 = jnp.float32
BLOCK = 256
SCALE = HD**-0.5
MIB = 1 << 20


def dot(left, right, ld, rd):
    return lax.dot_general(left, right, (((ld,), (rd,)), ((), ())), preferred_element_type=F32)


def nn(left, right):
    return dot(left, right, 1, 0)


def nt(left, right):
    return dot(left, right, 1, 1)


def tn(left, right):
    return dot(left, right, 0, 0)


def partner(value, step):
    count = lax.axis_size("mp")
    return lax.ppermute(value, "mp", [(rank, rank ^ step) for rank in range(count)])


SEQ = ("far", "near")


def from_behind(value, steps):
    count = lax.axis_size("far") * lax.axis_size("near")
    leading, last = (max(0, -steps), min(count, count - steps))
    return lax.ppermute(value, SEQ, [(source, source + steps) for source in range(leading, last)])


def shard_bits():
    return (lax.axis_size("far") * lax.axis_size("near")).bit_length() - 1


def across_bit(value, bit):
    return lax.ppermute(value, SEQ, [(shard, shard ^ (1 << bit)) for shard in range(1 << shard_bits())])


def own_bit(bit):
    return lax.axis_index(SEQ) // (1 << bit) % 2


def step_kernel(bit, ids, kept, sent, kept_o, send_o):
    own = lax.shift_right_logical(ids[0], bit) % 2
    kept_o[0] = (kept[own].astype(F32) + sent[own].astype(F32)).astype(BF)
    send_o[0] = (kept[1 - own].astype(F32) + sent[1 - own].astype(F32)).astype(BF)


class ShardSum:
    def __init__(self, kept, send):
        self.left = list(range(1, shard_bits()))
        self.kept, self.sent = kept, across_bit(send, 0)

    def step(self, ids, *others):
        blocks, part, columns = self.kept.shape
        half = pl.BlockSpec((1, part, columns), lambda j, s: (j, 0, 0))
        self.kept, send = run(
            functools.partial(step_kernel, self.left[0]),
            ids,
            (self.kept, after(self.sent, *others)),
            [shaped((blocks // 2, part, columns), BF)] * 2,
            grid=(blocks // 2,),
            in_specs=[pl.BlockSpec((2, part, columns), lambda j, s: (j, 0, 0))] * 2,
            out_specs=[half, half],
            micros=2,
        )
        self.sent = across_bit(send, self.left[0])
        self.left = self.left[1:]

    def last(self, ids, *others):
        while self.left:
            self.step(ids, *others)
        rows = lambda value: value.reshape(-1, value.shape[-1])
        return rows(self.kept), rows(after(self.sent, *others))


def double(value, have, bit):
    other = across_bit(value, bit)
    dim = sorted([*have, bit], reverse=True).index(bit)
    low = own_bit(bit) == 0
    return jnp.stack([jnp.where(low, value, other), jnp.where(low, other, value)], axis=dim)


def to_all(own):
    have = []
    value = own
    for bit in reversed(range(shard_bits())):
        value = double(value, have, bit)
        have.append(bit)
    return value.reshape(-1, own.shape[-1])


def added(*terms):
    total = terms[0].astype(F32)
    for term in terms[1:]:
        total = total + term.astype(F32)
    return total.astype(BF)


def whole(array):
    rank = len(array.shape)
    return pl.BlockSpec(array.shape, lambda *_: (0,) * rank)


def shaped(shape, dtype):
    return jax.ShapeDtypeStruct(shape, dtype)


def run(kernel, ids, args, outs, grid=(1,), in_specs=None, out_specs=None, scratch=(), micros=1, vmem=40):
    in_specs = in_specs or [None] * len(args)
    out_specs = out_specs or [None] * len(outs)
    in_specs = [whole(a) if s is None else s for a, s in zip(args, in_specs)]
    out_specs = [whole(a) if s is None else s for a, s in zip(outs, out_specs)]
    prefetch = () if ids is None else (ids,)
    return pl.pallas_call(
        functools.partial(kernel, None) if ids is None else kernel,
        out_shape=outs,
        grid_spec=pltpu.PrefetchScalarGridSpec(
            num_scalar_prefetch=len(prefetch),
            grid=grid,
            in_specs=in_specs,
            out_specs=out_specs,
            scratch_shapes=list(scratch),
        ),
        compiler_params=pltpu.CompilerParams(vmem_limit_bytes=vmem * MIB),
        cost_estimate=pl.CostEstimate(flops=int(micros * 0.5e9), transcendentals=0, bytes_accessed=1000),
    )(*prefetch, *args)


def after(value, *others):
    return lax.optimization_barrier((value, *others))[0]


def ln_rows(values):
    centred = values - jnp.mean(values, axis=-1, keepdims=True)
    spread = jnp.mean(centred * centred, axis=-1, keepdims=True)
    inverse = lax.rsqrt(spread + EPS)
    return centred * inverse, inverse


def ln_back(grad, gain, normed, inverse):
    scaled = grad * gain
    first = jnp.mean(scaled, axis=-1, keepdims=True)
    second = jnp.mean(scaled * normed, axis=-1, keepdims=True)
    return inverse * (scaled - first - normed * second)


def head_mask(head, heads):
    lanes = lax.broadcasted_iota(jnp.int32, (1, heads * HD), 1)
    return jnp.where(lanes // HD == head, 1.0, 0.0).astype(BF)


def by_head(rows, heads):
    return [rows * head_mask(head, heads) for head in range(heads)]


def layout_kernel(rows, lens, prompts, place, ids, begin):
    items = lens.shape[0]
    offset = place[0] * rows
    own_first = offset + place[1] * (rows // 4)
    reach = begin.shape[1]
    positions = offset + lax.broadcasted_iota(jnp.int32, (1, reach), 1)
    found = jnp.zeros((1, reach), jnp.int32)
    lows = [jnp.int32(0)] * (reach // BLOCK)
    begun = base = own_base = jnp.int32(0)
    for item in range(items):
        found = jnp.where(positions >= begun, begun, found)
        lows = [jnp.where(offset + block * BLOCK >= begun, begun, low) for block, low in enumerate(lows)]
        begun = begun + lens[item]
        base = base + jnp.where(begun <= offset, 1, 0)
        own_base = own_base + jnp.where(begun <= own_first, 1, 0)
    begin[...] = jnp.where(positions >= begun, begun, found) - offset
    lows = [jnp.where(offset + block * BLOCK >= begun, begun, low) for block, low in enumerate(lows)]
    base = jnp.minimum(base, items - 3)
    own_base = jnp.minimum(own_base, items - 2)
    begun = bound = jnp.int32(0)
    for item in range(items):
        begun = begun + lens[item]
        bound = jnp.where(own_base == item, begun, bound)
    ids[0] = place[0]
    ids[1] = place[1]
    ids[2] = base
    ids[3] = (own_base - base) * 128
    ids[4] = bound - own_first
    ids[5] = prompts[own_base]
    ids[6] = prompts[own_base + 1]
    ids[7] = 0
    for block, low in enumerate(lows):
        ids[8 + block] = low - offset


def pack_kernel(ids, merge, pq, pm, pack):
    width = pq.shape[1]
    pack[:width, :] = merge[...]
    pack[width : 2 * width, :] = pq[...].T
    pack[2 * width :, :] = pm[...]


def entry_kernel(ids, tok, gain, bias, wq, wk, wv, hid, q, kv, tail):
    width = wq.shape[1]
    normed, _ = ln_rows(tok[...].astype(F32))
    hidden = (normed * gain[...] + bias[...]).astype(BF)
    hid[...] = hidden
    kv[:, :width] = nn(hidden, wk[...]).astype(BF)
    kv[:, width:] = nn(hidden, wv[...]).astype(BF)
    q[...] = (nn(hidden, wq[...]).astype(BF) * SCALE).astype(BF)

    @pl.when(pl.program_id(0) == pl.num_programs(0) - 1)
    def _():
        tail[...] = kv[...]


def prompt_kernel(ids, text, pk, pv, out):
    width = pk.shape[1]
    out[:, :width] = nn(text[0], pk[...]).astype(BF)
    out[:, width:] = nn(text[0], pv[...]).astype(BF)


def window_bias(key_base, query_base, begin):
    shape = (BLOCK, BLOCK)
    key = key_base + lax.broadcasted_iota(jnp.int32, shape, 0)
    query = query_base + lax.broadcasted_iota(jnp.int32, shape, 1)
    return jnp.where((key <= query) & (key >= begin), 0.0, NEGATIVE).astype(F32)


def attend_block(keys, values_t, queries, bias, top, total, acc):
    heads = range(len(queries))
    before, sums, held = top[...], total[...], [acc[head] for head in heads]
    scores = [nt(keys, query) + bias for query in queries]
    after = [jnp.maximum(before[h : h + 1, :], jnp.max(scores[h], axis=0, keepdims=True)) for h in heads]
    unnorm = [jnp.exp(scores[h] - after[h]) for h in heads]
    fade = [jnp.exp(before[h : h + 1, :] - after[h]) for h in heads]
    parts = [nn(values_t[h * HD : (h + 1) * HD, :], unnorm[h].astype(BF)) for h in heads]
    added_up = [sums[h : h + 1, :] * fade[h] + jnp.sum(unnorm[h], axis=0, keepdims=True) for h in heads]
    for h in heads:
        acc[h] = held[h] * fade[h] + parts[h]
    top[...] = jnp.concatenate(after, axis=0)
    total[...] = jnp.concatenate(added_up, axis=0)


def attend_local_kernel(ids, q, kv, begin, acc_o, top_o, total_o, vt, acc, top, total):
    step = pl.program_id(0)
    width = q.shape[1]
    heads = width // HD
    blocks = kv.shape[0] // BLOCK

    @pl.when(step == 0)
    def _():
        for b in range(blocks):
            vt[b] = kv[b * BLOCK : (b + 1) * BLOCK, width:].T

    queries = by_head(q[...], heads)
    top[...] = jnp.full_like(top, NEGATIVE)
    total[...] = jnp.zeros_like(total)
    acc[...] = jnp.zeros_like(acc)
    low = lax.shift_right_logical(jnp.maximum(ids[8 + step], 0), 8)

    @pl.loop(low, step + 1)
    def _(b):
        row = pl.multiple_of(b * BLOCK, BLOCK)
        bias = window_bias(row, step * BLOCK, begin[...])
        attend_block(kv[pl.ds(row, BLOCK), :width], vt[b], queries, bias, top, total, acc)

    acc_o[0] = acc[...]
    top_o[0] = top[...]
    total_o[0] = total[...]


def attend_remote_kernel(ids, q, kv, tail, begin, acc_i, top_i, total_i, out, low_out, lse, ship_a, ship_b, ship0, vt, acc, top, total):
    step = pl.program_id(0)
    width = q.shape[1]
    heads = width // HD
    blocks = kv.shape[0] // BLOCK

    @pl.when(step == 0)
    def _():
        vt[0] = tail[:, width:].T
        for b in range(blocks):
            vt[b + 1] = kv[b * BLOCK : (b + 1) * BLOCK, width:].T

    queries = by_head(q[...], heads)
    acc[...] = acc_i[0]
    top[...] = top_i[0]
    total[...] = total_i[0]
    span = (blocks + 1) * BLOCK
    low = lax.shift_right_logical(jnp.maximum(ids[8 + step] + span, 0), 8)

    def bias_of(b):
        return window_bias(b * BLOCK - span, step * BLOCK, begin[...])

    @pl.when(low == 0)
    def _():
        attend_block(tail[:, :width], vt[0], queries, bias_of(0), top, total, acc)

    @pl.loop(jnp.maximum(low, 1), blocks + 1)
    def _(b):
        row = pl.multiple_of((b - 1) * BLOCK, BLOCK)
        attend_block(kv[pl.ds(row, BLOCK), :width], vt[b], queries, bias_of(b), top, total, acc)

    sums = top[...] + jnp.log(total[...])
    lse[0] = sums
    high = sums.astype(BF).astype(F32)
    both = jnp.concatenate([high, sums - high], axis=1)
    stacked = jnp.concatenate([acc[h] * (1.0 / total[h : h + 1, :]) for h in range(heads)], axis=0)
    rows = stacked.T
    out[0] = rows
    low_out[0] = rows.astype(BF)
    half = pl.num_programs(0) // 2

    def put(ship):
        ship[:BLOCK, :width] = q[...]
        ship[:BLOCK, width:] = rows.astype(BF)
        ship[BLOCK:, :] = jnp.concatenate([both, jnp.zeros((16 - heads, 2 * BLOCK), F32)], axis=0).astype(BF)

    @pl.when(step < half)
    def _():
        put(ship_a.at[0])

    @pl.when(step >= half)
    def _():
        put(ship_b.at[0])

    @pl.when(step == 0)
    def _():
        ship0[0] = ship_a[0]


def back_block(keys, values, keys_t, queries, grads, bias, lse, delta, dq, dkv):
    width = keys.shape[1]
    heads = range(len(queries))
    logs, deltas = lse[...], delta[...]
    probs = [jnp.exp(nt(keys, queries[h]) + bias - logs[h : h + 1, :]) for h in heads]
    prob_grads = [nt(values, grads[h]) for h in heads]
    score_grads = [(probs[h] * (prob_grads[h] - deltas[h : h + 1, :])).astype(BF) for h in heads]
    if dkv is not None:
        stack = lambda parts: jnp.concatenate(parts, axis=1)
        low = stack([prob.astype(BF) for prob in probs])
        dkv[:, :width] += nn(stack(score_grads), jnp.concatenate(queries, axis=0))
        dkv[:, width:] += nn(low, jnp.concatenate(grads, axis=0))
    if dq is not None:
        parts = [nn(keys_t[h * HD : (h + 1) * HD, :], score_grads[h]) for h in heads]
        for h in heads:
            dq[h] += parts[h]


def put_delta(delta, grad, out):
    products = (grad.astype(F32) * out.astype(F32)).T
    for head in range(delta.shape[0]):
        delta[head : head + 1, :] = jnp.sum(products[head * HD : (head + 1) * HD, :], axis=0, keepdims=True)


def back_local_kernel(ids, q, kv, begin, grad, out, lse, dkv_o, dq_o, delta_o, kt, dkv):
    step = pl.program_id(0)
    width = q.shape[1]
    heads = width // HD
    blocks = kv.shape[0] // BLOCK

    @pl.when(step == 0)
    def _():
        dkv[...] = jnp.zeros_like(dkv)
        for b in range(blocks):
            kt[b] = kv[b * BLOCK : (b + 1) * BLOCK, :width].T

    put_delta(delta_o.at[0], grad[0], out[0])
    dq_o[...] = jnp.zeros_like(dq_o)
    queries = by_head(q[...], heads)
    grads = by_head(grad[0], heads)
    low = lax.shift_right_logical(jnp.maximum(ids[8 + step], 0), 8)

    @pl.loop(low, step + 1)
    def _(b):
        row = pl.multiple_of(b * BLOCK, BLOCK)
        pair = kv[pl.ds(row, BLOCK), :]
        bias = window_bias(row, step * BLOCK, begin[...])
        back_block(
            pair[:, :width], pair[:, width:], kt[b], queries, grads, bias, lse.at[0], delta_o.at[0], dq_o.at[0], dkv.at[b]
        )

    @pl.when(step == pl.num_programs(0) - 1)
    def _():
        for b in range(blocks):
            dkv_o[b * BLOCK : (b + 1) * BLOCK, :] = dkv[b]


def back_query_kernel(ids, q, kv, tail, begin, grad, lse, delta, dq_i, dq_o, kt, dq):
    step = pl.program_id(0)
    width = q.shape[1]
    heads = width // HD
    blocks = kv.shape[0] // BLOCK

    @pl.when(step == 0)
    def _():
        kt[0] = tail[:, :width].T
        for b in range(blocks):
            kt[b + 1] = kv[b * BLOCK : (b + 1) * BLOCK, :width].T

    dq[...] = dq_i[0]
    span = (blocks + 1) * BLOCK
    low = lax.shift_right_logical(jnp.maximum(ids[8 + step] + span, 0), 8)

    @pl.when(low <= blocks)
    def _():
        queries = by_head(q[...], heads)
        grads = by_head(grad[0], heads)

        def one(b, pair):
            bias = window_bias(b * BLOCK - span, step * BLOCK, begin[...])
            back_block(pair[:, :width], pair[:, width:], kt[b], queries, grads, bias, lse.at[0], delta.at[0], dq, None)

        @pl.when(low == 0)
        def _():
            one(0, tail[...])

        @pl.loop(jnp.maximum(low, 1), blocks + 1)
        def _(b):
            row = pl.multiple_of((b - 1) * BLOCK, BLOCK)
            one(b, kv[pl.ds(row, BLOCK), :])

    stacked = jnp.concatenate([dq[h] for h in range(heads)], axis=0)
    dq_o[...] = (stacked.T * SCALE).astype(BF)


def back_key_kernel(ids, kv, begin, ship_low, ship_high, grad_n, ship_f, grad_f, dkv_i, dkv_o, delta, lse, dkv):
    step = pl.program_id(0)
    width = kv.shape[1] // 2
    heads = width // HD
    blocks = kv.shape[0] // BLOCK

    @pl.when(step == 0)
    def _():
        for b in range(blocks):
            dkv[b] = dkv_i[b * BLOCK : (b + 1) * BLOCK, :]

    low = lax.shift_right_logical(jnp.maximum(ids[8 + blocks + step], 0), 8)

    def all_keys(ship, grad):
        put_delta(delta, grad, ship[:BLOCK, width:])
        parts = ship[BLOCK:, :].astype(F32)
        lse[...] = parts[:heads, :BLOCK] + parts[:heads, BLOCK:]
        queries, grads = by_head(ship[:BLOCK, :width], heads), by_head(grad, heads)

        @pl.loop(low, blocks)
        def _(b):
            row = pl.multiple_of(b * BLOCK, BLOCK)
            pair = kv[pl.ds(row, BLOCK), :]
            bias = window_bias(row, blocks * BLOCK + step * BLOCK, begin[...])
            back_block(pair[:, :width], pair[:, width:], None, queries, grads, bias, lse, delta, None, dkv.at[b])

    @pl.when((low < blocks) & (step < blocks // 2))
    def _():
        all_keys(ship_low.at[0], grad_n[0])

    @pl.when((low < blocks) & (step >= blocks // 2) & (step < blocks))
    def _():
        all_keys(ship_high.at[0], grad_n[0])

    @pl.when((low < blocks) & (step == blocks))
    def _():
        all_keys(ship_f.at[0], grad_f[0])

    @pl.when(step == blocks)
    def _():
        for b in range(blocks):
            dkv_o[b * BLOCK : (b + 1) * BLOCK, :] = dkv[b].astype(BF)


def cross_bias(ids, prompt_rows, rows):
    shape = (2 * prompt_rows, rows)
    key = lax.broadcasted_iota(jnp.int32, shape, 0)
    query = lax.broadcasted_iota(jnp.int32, shape, 1)
    key_slot = lax.shift_right_logical(key, prompt_rows.bit_length() - 1)
    query_slot = jnp.where(query >= ids[4], 1, 0)
    limit = jnp.where(key_slot == 1, prompt_rows + ids[6], ids[5])
    return jnp.where((key_slot == query_slot) & (key < limit), 0.0, NEGATIVE).astype(F32)


def cross_kernel(ids, tok, low, *refs):
    packs, pairs = refs[:4], refs[4:8]
    gain2, bias2, gain3, bias3 = refs[8:12]
    after_self_o, two_o, q_o, stat_o, out_o, after_o, three_o = refs[12:]
    rows = tok.shape[0]
    width = packs[0].shape[0] // 3
    heads = width // HD
    rank = ids[1]
    prompt_rows = pairs[0].shape[0] // 3
    after = tok[...].astype(F32)
    for d in range(4):
        after = after + nn(low[rank ^ d], packs[d][:width, :])
    after_self_o[...] = after
    normed, _ = ln_rows(after)
    hidden = (normed * gain2[...] + bias2[...]).astype(BF)
    two_o[...] = hidden
    bias = cross_bias(ids, prompt_rows, rows)
    first = pl.multiple_of(ids[3], prompt_rows)
    for d in range(4):
        columns = slice(d * width, (d + 1) * width)
        query_rows = (nt(hidden, packs[d][width : 2 * width, :]).astype(BF) * SCALE).astype(BF)
        q_o[:, columns] = query_rows
        keys = pairs[d][pl.ds(first, 2 * prompt_rows), :width]
        values_t = pairs[d][pl.ds(first, 2 * prompt_rows), width:].T
        each = range(heads)
        scores = [nt(keys, query) + bias for query in by_head(query_rows, heads)]
        tops = [jnp.max(score, axis=0, keepdims=True) for score in scores]
        unnorm = [jnp.exp(scores[h] - tops[h]) for h in each]
        totals = [jnp.sum(value, axis=0, keepdims=True) for value in unnorm]
        stat_o[d * heads : (d + 1) * heads, :] = jnp.concatenate([tops[h] + jnp.log(totals[h]) for h in each], axis=0)
        parts = [nn(values_t[h * HD : (h + 1) * HD, :], unnorm[h].astype(BF)) * (1.0 / totals[h]) for h in each]
        out_o[:, columns] = jnp.concatenate(parts, axis=0).T.astype(BF)
    after = after_self_o[...]
    for d in range(4):
        after = after + nn(out_o[:, d * width : (d + 1) * width], packs[d][2 * width :, :])
    after_o[...] = after
    normed, _ = ln_rows(after)
    three_o[...] = (normed * gain3[...] + bias3[...]).astype(BF)


def cross_back_kernel(ids, kept, sent, crossed, og, after, after_self, q, stat, *refs):
    packs, pairs = refs[:4], refs[4:8]
    gain2, gain3 = refs[8:10]
    cog_o, cqg_o, slg_o, resid_o, shg_o, keep0_o, keep1_o, send_o, norms_o = refs[10:]
    rows, model = after.shape
    width = packs[0].shape[0] // 3
    heads = width // HD
    rank = ids[1]
    prompt_rows = pairs[0].shape[0] // 3
    grad = kept[...].astype(F32) + sent[...].astype(F32) + crossed[...].astype(F32)
    normed, inverse = ln_rows(after[...])
    norms_o[0:1, :] = jnp.sum(grad * normed, axis=0, keepdims=True)
    norms_o[1:2, :] = jnp.sum(grad, axis=0, keepdims=True)
    resid = og[...].astype(F32) + ln_back(grad, gain3[...], normed, inverse)
    low_resid = resid.astype(BF)
    cog_o[...] = low_resid
    bias = cross_bias(ids, prompt_rows, rows)
    first = pl.multiple_of(ids[3], prompt_rows)
    keep0_o[...] = jnp.zeros_like(keep0_o)
    keep1_o[...] = jnp.zeros_like(keep1_o)
    send_o[...] = jnp.zeros_like(send_o)
    for d in range(4):
        columns = slice(d * width, (d + 1) * width)
        head_grad = nt(low_resid, packs[d][2 * width :, :]).astype(BF)
        keys = pairs[d][pl.ds(first, 2 * prompt_rows), :width]
        values = pairs[d][pl.ds(first, 2 * prompt_rows), width:]
        keys_t = keys.T
        each = range(heads)
        queries, grads = by_head(q[:, columns], heads), by_head(head_grad, heads)
        logs = stat[d * heads : (d + 1) * heads, :]
        probs = [jnp.exp(nt(keys, queries[h]) + bias - logs[h : h + 1, :]) for h in each]
        prob_grads = [nt(values, grads[h]) for h in each]
        deltas = [jnp.sum(probs[h] * prob_grads[h], axis=0, keepdims=True) for h in each]
        score_grads = [(probs[h] * (prob_grads[h] - deltas[h])).astype(BF) for h in each]
        key_sum = nn(jnp.concatenate(score_grads, axis=1), jnp.concatenate(queries, axis=0))
        value_sum = nn(jnp.concatenate([prob.astype(BF) for prob in probs], axis=1), jnp.concatenate(grads, axis=0))
        parts = [nn(keys_t[h * HD : (h + 1) * HD, :], score_grads[h]) for h in each]
        cqg_o[:, columns] = (jnp.concatenate(parts, axis=0).T * SCALE).astype(BF)
        target = (keep0_o, send_o.at[0], keep1_o, send_o.at[1])[d]
        target[pl.ds(first, 2 * prompt_rows), :width] = key_sum.astype(BF)
        target[pl.ds(first, 2 * prompt_rows), width:] = value_sum.astype(BF)
    two_grad = None
    for d in range(4):
        term = nn(cqg_o[:, d * width : (d + 1) * width], packs[d][width : 2 * width, :])
        two_grad = term if two_grad is None else two_grad + term
    normed, inverse = ln_rows(after_self[...])
    norms_o[2:3, :] = jnp.sum(two_grad * normed, axis=0, keepdims=True)
    norms_o[3:4, :] = jnp.sum(two_grad, axis=0, keepdims=True)
    resid = resid + ln_back(two_grad, gain2[...], normed, inverse)
    resid_o[...] = resid
    low_resid = resid.astype(BF)
    slg_o[...] = low_resid
    for d in range(4):
        shg_o[rank ^ d] = nt(low_resid, packs[d][:width, :]).astype(BF)


def feed_kernel(ids, h_a, h_b, dh_a, dh_b, expand, shrink, *outs):
    c = 0.7978845608028654

    def rows(h, dh, low_o, pre_o, out_o, three_o):
        v = nn(h[...], expand[...])
        square = v * v
        t = jnp.tanh(v * (c + (c * 0.044715) * square))
        half = 0.5 * (1.0 + t)
        low = (v * half).astype(BF)
        slope = half + (v * (1.0 - t * t)) * (0.5 * c + (1.5 * c * 0.044715) * square)
        pre = (dh[...].astype(F32) * slope).astype(BF)
        low_o[...] = low
        pre_o[...] = pre
        out_o[...] = nn(low, shrink[...]).astype(BF)
        three_o[...] = nt(pre, expand[...]).astype(BF)

    half = pl.num_programs(0) // 2

    @pl.when(pl.program_id(0) < half)
    def _():
        rows(h_a, dh_a, *outs[:4])

    @pl.when(pl.program_id(0) >= half)
    def _():
        rows(h_b, dh_b, *outs[4:])


def feed(ids, base, h_a, h_b, dh, expand, shrink):
    rows, model = h_a.shape
    hidden = expand.shape[1]
    tile = 128
    tiles = rows // tile
    first, second = lambda j: jnp.minimum(j, tiles - 1), lambda j: jnp.maximum(j - tiles, 0)
    spec = lambda columns, at: pl.BlockSpec((tile, columns), lambda j, s: (at(j), 0))
    own = lambda d, at: pl.BlockSpec((tile, hidden), lambda j, s: ((s[1] ^ d) * tiles + at(j), 0))
    outs = lambda at: [spec(hidden, at), spec(hidden, at), spec(model, at), spec(model, at)]
    return run(
        feed_kernel,
        ids,
        (h_a, h_b, dh, dh, expand, shrink),
        [shaped((rows, hidden), BF), shaped((rows, hidden), BF), shaped((rows, model), BF), shaped((rows, model), BF)] * 2,
        grid=(2 * tiles,),
        in_specs=[spec(model, first), spec(model, second), own(base, first), own(base + 1, second), None, None],
        out_specs=outs(first) + outs(second),
        micros=12,
    )


def spread(ids, rows, kept, send):
    far, part, _ = kept.shape
    own = ids[0] % 2
    for block in range(far):
        kept[block] = rows[pl.ds(pl.multiple_of((2 * block + own) * part, part), part), :]
        send[block] = rows[pl.ds(pl.multiple_of((2 * block + 1 - own) * part, part), part), :]


def feed_weights_kernel(ids, *refs):
    threes, pres, lows = refs[:4], refs[4:8], refs[8:12]
    og, out, turned = refs[12:]
    step = pl.program_id(0)
    half = pl.num_programs(0) // 2
    rank = ids[1]
    rows = threes[0].shape[0]

    @pl.when(step == 0)
    def _():
        for d in range(4):
            turned[:, d * rows : (d + 1) * rows] = threes[d][...].T

    @pl.when(step == half)
    def _():
        for d in range(4):
            turned[:, d * rows : (d + 1) * rows] = og[pl.ds(pl.multiple_of((rank ^ d) * rows, rows), rows), :].T

    @pl.when(step < half)
    def _():
        out[...] = nn(turned[...], jnp.concatenate([p[...] for p in pres], axis=0)).astype(BF)

    @pl.when(step >= half)
    def _():
        out[...] = nn(turned[...], jnp.concatenate([p[...] for p in lows], axis=0)).astype(BF)


def feed_weights(ids, threes, pres, lows, og):
    rows, model = threes[0].shape
    hidden = pres[0].shape[1]
    chunk = 256
    half = hidden // chunk
    front = pl.BlockSpec((rows, chunk), lambda j, s: (0, jnp.minimum(j, half - 1)))
    back = pl.BlockSpec((rows, chunk), lambda j, s: (0, jnp.maximum(j - half, 0)))
    return run(
        feed_weights_kernel,
        ids,
        (*threes, *pres, *lows, og),
        [shaped((model, 2 * hidden), BF)],
        grid=(2 * half,),
        in_specs=[None] * 4 + [front] * 4 + [back] * 4 + [None],
        out_specs=[pl.BlockSpec((model, chunk), lambda j, s: (0, j))],
        scratch=[pltpu.VMEM((model, 4 * rows), BF)],
        micros=9,
        vmem=60,
    )[0]


def head_weights_kernel(ids, two, cqg, cog, crossed, slg, low, keep0, keep1, send):
    rank = ids[1]
    width = low.shape[2]
    two_t, cog_t, slg_t = two[...].T, cog[...].T, slg[...].T
    for d, out in enumerate((keep0, send.at[0], keep1, send.at[1])):
        columns = slice(d * width, (d + 1) * width)
        out[:, :width] = nn(two_t, cqg[:, columns]).astype(BF)
        out[:, width : 2 * width] = nn(cog_t, crossed[:, columns]).astype(BF)
        out[:, 2 * width :] = nn(slg_t, low[rank ^ d]).astype(BF)


def one_grad_kernel(ids, kvg, hid, dq, wq, wk, wv, gain, bias, keep0, keep1, send, norms):
    rows, width2 = kvg.shape
    width = width2 // 2
    quarter = rows // 4
    rank = ids[1]
    product = total = None
    for d in (1, 3, 2, 0):
        own = pl.ds(pl.multiple_of((rank ^ d) * quarter, quarter), quarter)
        part = (
            nt(dq[own, :], wq[...]) + nt(kvg[own, :width], wk[...]) + nt(kvg[own, width:], wv[...])
        )
        hidden = hid[own, :].astype(F32)
        term = jnp.sum(part * hidden, axis=0, keepdims=True)
        plain = jnp.sum(part, axis=0, keepdims=True)
        product = term if product is None else product + term
        total = plain if total is None else total + plain
        (keep0, send.at[0], keep1, send.at[1])[d][...] = part.astype(BF)
    norms[0:1, :] = (product - bias[...] * total) / gain[...]
    norms[1:2, :] = total


def text_kernel(ids, own, pk, pv, keep0, keep1, send):
    width = own.shape[1] // 2
    rank = ids[1]
    for d, out in enumerate((keep0, send.at[0], keep1, send.at[1])):
        columns = pl.ds(pl.multiple_of((rank ^ d) * width, width), width)
        out[...] = (nt(own[:, :width], pk[columns, :]) + nt(own[:, width:], pv[columns, :])).astype(BF)


def entry_weights_kernel(ids, hid, dq, kvg, entry_norms, norms, kept, send, rows):
    width = dq.shape[1]
    model = hid.shape[1]
    turned = hid[...].T
    rows[:, :width] = nn(turned, dq[...]).astype(BF)
    rows[:, width : 3 * width] = nn(turned, kvg[...]).astype(BF)
    sums = jnp.concatenate([entry_norms[...], norms[...], jnp.zeros((122, model), F32)], axis=0)
    rows[:, 3 * width :] = sums.T.astype(BF)
    spread(ids, rows, kept, send)


def arrived_kernel(ids, *refs):
    feed, head, entry, (expand, shrink, pq, pm, merge, wq, wk, wv, norms) = refs[:1], refs[1:2], refs[2:4], refs[4:]

    def total(terms, width, index):
        columns = slice(index * width, (index + 1) * width)
        value = terms[0][:, columns].astype(F32)
        for term in terms[1:]:
            value = value + term[:, columns].astype(F32)
        return value

    hidden, width = expand.shape[1], pq.shape[1]
    expand[...] = total(feed, hidden, 0)
    shrink[...] = total(feed, hidden, 1).T
    pq[...] = total(head, width, 0)
    pm[...] = total(head, width, 1).T
    merge[...] = total(head, width, 2).T
    wq[...] = total(entry, width, 0)
    wk[...] = total(entry, width, 1)
    wv[...] = total(entry, width, 2)
    norms[...] = total(entry, 128, 3 * width // 128).T[:8, :]


def prompt_kernel_back(ids, text, grads, key, value, text_grad):
    width = key.shape[1]

    @pl.when(pl.program_id(0) == 0)
    def _():
        key[...] = jnp.zeros_like(key)
        value[...] = jnp.zeros_like(value)

    turned = text[...].T
    key[...] += nn(turned, grads[:, :width])
    value[...] += nn(turned, grads[:, width : 2 * width])
    text_grad[...] = grads[:, 2 * width :].astype(F32)


def entry_back_kernel(ids, keep, sent, crossed, tok, gain, resid, out):
    grad = keep[...].astype(F32) + sent[0].astype(F32) + crossed[...].astype(F32)
    normed, inverse = ln_rows(tok[...].astype(F32))
    out[...] = (resid[...] + ln_back(grad, gain[...], normed, inverse)).astype(BF)


def assemble_kernel(ids, *refs):
    out = refs[4]
    for d in range(4):

        @pl.when(pl.program_id(0) == ids[1] ^ d)
        def _():
            out[...] = refs[d][...].astype(out.dtype)


def assemble(ids, pieces, dtype):
    rows, model = pieces[0].shape
    return run(
        assemble_kernel,
        ids,
        pieces,
        [shaped((4 * rows, model), dtype)],
        grid=(4,),
        out_specs=[pl.BlockSpec((rows, model), lambda i, s: (i, 0))],
        micros=3,
    )[0]


def gather(own):
    across = partner(own, 2)
    near = partner(own, 1)
    return own, near, across, partner(across, 1)


def body(
    tokens,
    text_states,
    item_lengths,
    prompt_lengths,
    entry_gain,
    entry_bias,
    cross_gain,
    cross_bias_,
    mixer_gain,
    mixer_bias,
    query_weight,
    key_weight,
    value_weight,
    merge_weight,
    prompt_query,
    prompt_key,
    prompt_value,
    prompt_merge,
    expand_weight,
    shrink_weight,
    output_grad,
):
    rows, model = tokens.shape
    ranks = lax.axis_size("mp")
    width = query_weight.shape[1]
    heads = width // HD
    items, prompt_rows = text_states.shape[:2]
    quarter = rows // ranks
    steps = rows // BLOCK
    hidden_units = expand_weight.shape[1]
    shards = lax.axis_size("far") * lax.axis_size("near")
    assert ranks == 4 and quarter == BLOCK and prompt_rows == 128 and items % shards == 0

    place = jnp.stack([lax.axis_index(SEQ), lax.axis_index("mp")]).astype(jnp.int32)
    scalars = pl.BlockSpec(memory_space=pltpu.SMEM)
    ids, begin = pl.pallas_call(
        functools.partial(layout_kernel, rows),
        out_shape=[shaped((9 + 2 * steps + 7,), jnp.int32), shaped((1, 2 * rows + BLOCK), jnp.int32)],
        in_specs=[scalars] * 3,
        out_specs=[scalars, pl.BlockSpec(memory_space=pltpu.VMEM)],
    )(item_lengths, prompt_lengths, place)
    base = ids[2]

    row = lambda vector: vector.reshape(1, -1)
    own_rows = lambda columns: pl.BlockSpec((quarter, columns), lambda *g: (g[-1][1], 0))

    block_rows = lambda columns: pl.BlockSpec((BLOCK, columns), lambda i, *s: (i, 0))
    pack = run(pack_kernel, None, (merge_weight, prompt_query, prompt_merge), [shaped((3 * width, model), BF)], vmem=60)[0]
    pack_near, pack_across = partner(pack, 1), partner(pack, 2)
    hidden_one, q, kv, kv_tail = run(
        entry_kernel,
        None,
        (after(tokens, pack), row(entry_gain), row(entry_bias), query_weight, key_weight, value_weight),
        [
            shaped((rows, model), BF),
            shaped((rows, width), BF),
            shaped((rows, 2 * width), BF),
            shaped((BLOCK, 2 * width), BF),
        ],
        grid=(steps,),
        in_specs=[block_rows(model)] + [None] * 5,
        out_specs=[block_rows(model), block_rows(width), block_rows(2 * width), None],
        micros=2,
        vmem=60,
    )
    kv_near = from_behind(kv, 1)
    kv_far = from_behind(kv_tail, 2)

    pair = run(
        prompt_kernel,
        ids,
        (after(text_states, kv, pack_near), prompt_key, prompt_value),
        [shaped((3 * prompt_rows, 2 * width), BF)],
        grid=(3,),
        in_specs=[pl.BlockSpec((1, prompt_rows, model), lambda i, s: (s[2] + i, 0, 0)), None, None],
        out_specs=[pl.BlockSpec((prompt_rows, 2 * width), lambda i, s: (i, 0))],
        micros=1.5,
    )[0]
    pair_near, pair_across = partner(pair, 1), partner(pair, 2)
    hidden_grad = nt(after(output_grad, kv, pair), shrink_weight).astype(BF)

    state = [shaped((steps, heads, HD, BLOCK), F32), shaped((steps, heads, BLOCK), F32), shaped((steps, heads, BLOCK), F32)]
    state_specs = [
        pl.BlockSpec((1, heads, HD, BLOCK), lambda i, s: (i, 0, 0, 0)),
        pl.BlockSpec((1, heads, BLOCK), lambda i, s: (i, 0, 0)),
        pl.BlockSpec((1, heads, BLOCK), lambda i, s: (i, 0, 0)),
    ]
    state_scratch = [pltpu.VMEM((heads, HD, BLOCK), F32), pltpu.VMEM((heads, BLOCK), F32), pltpu.VMEM((heads, BLOCK), F32)]
    q_spec = block_rows(width)
    begin_spec = pl.BlockSpec((1, BLOCK), lambda i, s: (0, i))
    piece_spec = pl.BlockSpec((1, BLOCK, width), lambda i, s: (i, 0, 0))
    turned = lambda blocks: pltpu.VMEM((blocks, width, BLOCK), BF)
    acc, top, total = run(
        attend_local_kernel,
        ids,
        (after(q, pair_near), kv, begin),
        state,
        grid=(steps,),
        in_specs=[q_spec, None, begin_spec],
        out_specs=state_specs,
        scratch=[turned(steps)] + state_scratch,
        micros=13,
    )
    kv_near, kv_far = lax.optimization_barrier((kv_near, kv_far, acc, hidden_grad))[:2]
    def ship_spec(side):
        half = steps // 2
        index = (lambda i: jnp.maximum(i - half, 0)) if side else (lambda i: jnp.minimum(i, half - 1))
        return pl.BlockSpec((1, BLOCK + 16, 2 * width), lambda i, s: (index(jnp.minimum(i, steps - 1)), 0, 0))

    self_out, self_low, lse, ship_low, ship_high, ship_first = run(
        attend_remote_kernel,
        ids,
        (q, kv_near, kv_far, begin, acc, top, total),
        [shaped((steps, BLOCK, width), F32), shaped((steps, BLOCK, width), BF), shaped((steps, heads, BLOCK), F32)]
        + [shaped((blocks, BLOCK + 16, 2 * width), BF) for blocks in (steps // 2, steps // 2, 1)],
        grid=(steps,),
        in_specs=[q_spec, None, None, begin_spec] + state_specs,
        out_specs=[piece_spec, piece_spec, state_specs[1], ship_spec(0), ship_spec(1), None],
        scratch=[turned(steps + 1)] + state_scratch,
        micros=9,
    )
    low_rows = lax.all_to_all(self_low, "mp", 0, 0)
    pack_across, pair_across = lax.optimization_barrier((pack_across, pair_across, self_low))[:2]
    packs = (pack, pack_near, pack_across, partner(pack_across, 1))
    pairs = (pair, pair_near, pair_across, partner(pair_across, 1))

    wide = lambda dtype: shaped((quarter, model), dtype)
    stat_shape = shaped((ranks * heads, quarter), F32)
    norms = (row(cross_gain), row(cross_bias_), row(mixer_gain), row(mixer_bias))
    after_self, hidden_two, cross_q, stat, cross_out, after_cross, hidden_three = run(
        cross_kernel,
        ids,
        (tokens, low_rows, *packs, *pairs, *norms),
        [wide(F32), wide(BF), wide(BF), stat_shape, wide(BF), wide(F32), wide(BF)],
        in_specs=[own_rows(model)] + [None] * 13,
        micros=11,
    )

    ship_low, ship_high, ship_f = after((ship_low, ship_high, ship_first), hidden_three)
    ship_low, ship_f = from_behind(ship_low, -1), from_behind(ship_f, -2)

    three_near, three_across = partner(hidden_three, 1), partner(hidden_three, 2)
    low0, pre0, out0, part0, low1, pre1, out1, part1 = feed(
        ids, 0, hidden_three, three_near, hidden_grad, expand_weight, shrink_weight
    )
    three_across, ship_low, ship_f = after((three_across, ship_low, ship_f), part1)
    threes = (hidden_three, three_near, three_across, partner(three_across, 1))
    sent1, out_sent1 = partner(part1, 1), partner(out1, 1)
    low2, pre2, out2, part2, low3, pre3, out3, part3 = feed(
        ids, 2, threes[2], threes[3], hidden_grad, expand_weight, shrink_weight
    )
    part3, sent1, out_sent1, ship_high = after((part3, sent1, out_sent1, ship_high), part2)
    ship_high = from_behind(ship_high, -1)
    partial = (part2.astype(F32) + partner(part3, 1).astype(F32)).astype(BF)
    across = partner(partial, 2)
    out_partial = (out2.astype(F32) + partner(after(out3, partial), 1).astype(F32)).astype(BF)
    feed_grads = feed_weights(ids, threes, after((pre0, pre1, pre2, pre3), partial), (low0, low1, low2, low3), output_grad)
    feed_sum = lax.psum_scatter(feed_grads, SEQ, scatter_dimension=0, tiled=True)
    across = after(across, feed_grads, out_partial)
    out_across = partner(after(out_partial, across), 2)

    pair_out = shaped((3 * prompt_rows, 2 * width), BF)
    cog, cqg, slg, resid, shg, pair_keep0, pair_keep1, pair_send, norm_grads = run(
        cross_back_kernel,
        ids,
        (part0, sent1, across, output_grad, after_cross, after_self, cross_q, stat, *packs, *pairs, norms[0], norms[2]),
        [wide(BF), wide(BF), wide(BF), wide(F32), shaped((ranks, quarter, width), BF)]
        + [pair_out, pair_out, shaped((2, *pair_out.shape), BF), shaped((4, model), F32)],
        in_specs=[None] * 3 + [own_rows(model)] + [None] * 14,
        micros=15,
        vmem=48,
    )
    self_grad = lax.all_to_all(shg, "mp", 0, 0)

    pair_sent = partner(pair_send, 1)
    pieces = shaped((model, 3 * width), BF)
    head_keep0, head_keep1, head_send = run(
        head_weights_kernel,
        ids,
        (hidden_two, cqg, cog, cross_out, slg, low_rows),
        [pieces, pieces, shaped((2, *pieces.shape), BF)],
        micros=5,
        vmem=60,
    )
    head_sent = partner(head_send, 1)
    head_half = added(head_keep1, head_sent[1])
    self_grad, out_across, pair_sent, head_half = after((self_grad, out_across, pair_sent, head_half), head_keep0)
    head_across = partner(head_half, 2)
    grad_n, grad_f = from_behind(self_grad, -1), from_behind(self_grad[:1], -2)
    pair_half = added(pair_keep1, pair_sent[1])
    pair_across = partner(pair_half, 2)

    lse_spec = state_specs[1]
    stat4 = shaped((steps, heads, BLOCK), F32)
    dkv, dq_part, delta = run(
        back_local_kernel,
        ids,
        (q, kv, begin, after(self_grad, pair_half), self_out, lse),
        [shaped((rows, 2 * width), F32), state[0], stat4],
        grid=(steps,),
        in_specs=[q_spec, None, begin_spec, piece_spec, piece_spec, lse_spec],
        out_specs=[None, state_specs[0], lse_spec],
        scratch=[turned(steps), pltpu.VMEM((steps, BLOCK, 2 * width), F32)],
        micros=15,
    )
    pair_across, grad_n, grad_f = after((pair_across, grad_n, grad_f), dq_part)
    pair_sum = added(pair_keep0, pair_sent[0], pair_across).reshape(3, prompt_rows, 2 * width)
    placed = lax.dynamic_update_slice_in_dim(jnp.zeros((items, prompt_rows, 2 * width), BF), pair_sum, base, 0)
    placed = placed.reshape(shards // 2, 2, -1, 2 * width)
    own = own_bit(0)
    text_sum = ShardSum(
        lax.dynamic_index_in_dim(placed, own, 1, keepdims=False), lax.dynamic_index_in_dim(placed, 1 - own, 1, keepdims=False)
    )
    dq = run(
        back_query_kernel,
        ids,
        (q, kv_near, kv_far, begin, self_grad, lse, delta, after(dq_part, text_sum.kept)),
        [shaped((rows, width), BF)],
        grid=(steps,),
        in_specs=[q_spec, None, None, begin_spec, piece_spec, lse_spec, lse_spec, state_specs[0]],
        out_specs=[q_spec],
        scratch=[turned(steps + 1), state_scratch[0]],
        micros=7,
    )[0]
    far = shards // 2
    spread_out = [shaped((far, model // shards, 3 * width + 128), BF)] * 2
    text_sum.step(ids, dq)
    grad_n, grad_f = after((grad_n, grad_f), dq, text_sum.kept)
    held = lambda i: jnp.minimum(i, steps - 1)
    near_piece = pl.BlockSpec((1, BLOCK, width), lambda i, s: (held(i), 0, 0))
    kvg = run(
        back_key_kernel,
        ids,
        (kv, begin, ship_low, ship_high, grad_n, ship_f, grad_f, dkv),
        [shaped((rows, 2 * width), BF)],
        grid=(steps + 1,),
        in_specs=[None, pl.BlockSpec((1, BLOCK), lambda i, s: (0, steps + i)), ship_spec(0), ship_spec(1), near_piece] + [None] * 3,
        scratch=[pltpu.VMEM((heads, BLOCK), F32)] * 2 + [pltpu.VMEM((steps, BLOCK, 2 * width), F32)],
        micros=8,
    )[0]

    quarter_out = shaped((quarter, model), BF)
    one_keep0, one_keep1, one_send, entry_norms = run(
        one_grad_kernel,
        ids,
        (kvg, hidden_one, dq, query_weight, key_weight, value_weight, row(entry_gain), row(entry_bias)),
        [quarter_out, quarter_out, shaped((2, *quarter_out.shape), BF), shaped((2, model), F32)],
        micros=3,
    )
    one_sent = partner(one_send, 1)
    entry_rows = run(
        entry_weights_kernel,
        ids,
        (hidden_one, after(dq, one_send), kvg, entry_norms, norm_grads),
        spread_out,
        scratch=[pltpu.VMEM((model, 3 * width + 128), BF)],
        micros=4,
    )
    entry_sum = ShardSum(*entry_rows)
    head_rows = added(head_keep0, head_sent[0], after(head_across, kvg))
    one_half = added(one_keep1, after(one_sent, entry_rows[0], head_rows)[1])
    one_across = partner(one_half, 2)
    own_pair = added(*text_sum.last(ids, one_half))
    text_out = shaped((prompt_rows * items // shards, width), BF)
    text_keep0, text_keep1, text_send = run(
        text_kernel, ids, (own_pair, prompt_key, prompt_value), [text_out, text_out, shaped((2, *text_out.shape), BF)], micros=1
    )
    text_sent = partner(text_send, 1)
    text_half = added(text_keep1, text_sent[1])
    text_across = partner(text_half, 2)
    one_across = after(one_across, text_half, head_rows, feed_sum)
    head_sum = lax.psum_scatter(after(head_rows, feed_sum), SEQ, scatter_dimension=0, tiled=True)
    grad_rows = run(
        entry_back_kernel,
        ids,
        (one_keep0, one_sent, one_across, tokens, row(entry_gain), resid),
        [wide(BF)],
        in_specs=[None] * 3 + [own_rows(model)] + [None] * 2,
        micros=2,
        vmem=60,
    )[0]
    grad_pieces = gather(grad_rows)

    text_own = added(text_keep0, text_sent[0], after(text_across, grad_rows))
    entry_sum.step(ids, grad_rows)
    prompt_all = to_all(jnp.concatenate([own_pair, text_own], axis=1))
    all_text = items * prompt_rows
    some = min(all_text, 1024)
    key_prompt, value_prompt, text_grad = run(
        prompt_kernel_back,
        None,
        (text_states.reshape(all_text, model), prompt_all),
        [shaped((model, width), F32), shaped((model, width), F32), shaped((all_text, width), F32)],
        grid=(all_text // some,),
        in_specs=[pl.BlockSpec((some, model), lambda i: (i, 0)), pl.BlockSpec((some, 3 * width), lambda i: (i, 0))],
        out_specs=[None, None, pl.BlockSpec((some, width), lambda i: (i, 0))],
        micros=3,
    )
    text_grad = text_grad.reshape(items, prompt_rows, width)

    tokens_grad = assemble(ids, grad_pieces, F32)
    out_rows = added(after_cross, out0, out_sent1, out_across)
    out_pieces = gather(after(out_rows, grad_rows))
    layer_output = assemble(ids, out_pieces, BF)

    part = model // shards
    square, turned_square = shaped((part, width), F32), shaped((width, part), F32)
    expand_grad, shrink_grad, pq_grad, pm_grad, merge_grad, wq_grad, wk_grad, wv_grad, norm_sum = run(
        arrived_kernel,
        None,
        (feed_sum, head_sum, *entry_sum.last(ids, grad_rows)),
        [shaped((part, hidden_units), F32), shaped((hidden_units, part), F32)]
        + [square, turned_square, turned_square, square, square, square, shaped((8, part), F32)],
        micros=3,
    )
    norm_sum = norm_sum + partner(norm_sum, 1)
    norm_sum = norm_sum + partner(norm_sum, 2)
    return (
        layer_output,
        tokens_grad,
        text_grad,
        norm_sum[0],
        norm_sum[1],
        norm_sum[4],
        norm_sum[5],
        norm_sum[2],
        norm_sum[3],
        wq_grad,
        wk_grad,
        wv_grad,
        merge_grad,
        pq_grad,
        key_prompt,
        value_prompt,
        pm_grad,
        expand_grad,
        shrink_grad,
    )


def solution(mesh):
    shards = mesh.shape["seq"]
    mesh = jax.sharding.Mesh(mesh.devices.reshape(shards // 2, 2, mesh.shape["mp"]), (*SEQ, "mp"))
    seq, mp, both = P(SEQ, None), P("mp", None), P(None, "mp")
    return jax.shard_map(
        body,
        mesh=mesh,
        in_specs=(seq,) + (P(),) * 9 + (both,) * 3 + (mp,) + (both,) * 3 + (mp, both, mp, seq),
        out_specs=(
            (seq, seq, P(None, None, "mp"))
            + (P(SEQ),) * 6
            + (P(SEQ, "mp"),) * 3
            + (P("mp", SEQ), P(SEQ, "mp"), both, both, P("mp", SEQ), P(SEQ, "mp"), P("mp", SEQ))
        ),
        check_vma=False,
    )
```

```python
import functools

import jax
import jax.numpy as jnp
from jax import lax
from jax.experimental import pallas as pl
from jax.experimental.pallas import tpu as pltpu
from jax.sharding import PartitionSpec as P

HD = 64
ITEM_LEN = 1024
EPS = 1e-06
NEGATIVE = -1e30
BF = jnp.bfloat16
F32 = jnp.float32
BLOCK = 256
SCALE = HD**-0.5
MIB = 1 << 20


def dot(left, right, ld, rd):
    return lax.dot_general(left, right, (((ld,), (rd,)), ((), ())), preferred_element_type=F32)


def nn(left, right):
    return dot(left, right, 1, 0)


def nt(left, right):
    return dot(left, right, 1, 1)


def tn(left, right):
    return dot(left, right, 0, 0)


def partner(value, step):
    count = lax.axis_size("mp")
    return lax.ppermute(value, "mp", [(rank, rank ^ step) for rank in range(count)])


SEQ = ("far", "near")


def from_behind(value, steps):
    count = lax.axis_size("far") * lax.axis_size("near")
    leading, last = (max(0, -steps), min(count, count - steps))
    return lax.ppermute(value, SEQ, [(source, source + steps) for source in range(leading, last)])


def shard_bits():
    return (lax.axis_size("far") * lax.axis_size("near")).bit_length() - 1


def across_bit(value, bit):
    return lax.ppermute(value, SEQ, [(shard, shard ^ (1 << bit)) for shard in range(1 << shard_bits())])


def own_bit(bit):
    return lax.axis_index(SEQ) // (1 << bit) % 2


def step_kernel(bit, ids, kept, sent, kept_o, send_o):
    own = lax.shift_right_logical(ids[0], bit) % 2
    kept_o[0] = (kept[own].astype(F32) + sent[own].astype(F32)).astype(BF)
    send_o[0] = (kept[1 - own].astype(F32) + sent[1 - own].astype(F32)).astype(BF)


class ShardSum:
    def __init__(self, kept, send):
        self.left = list(range(1, shard_bits()))
        self.kept, self.sent = kept, across_bit(send, 0)

    def step(self, ids, *others):
        blocks, part, columns = self.kept.shape
        half = pl.BlockSpec((1, part, columns), lambda j, s: (j, 0, 0))
        self.kept, send = run(
            functools.partial(step_kernel, self.left[0]),
            ids,
            (self.kept, after(self.sent, *others)),
            [shaped((blocks // 2, part, columns), BF)] * 2,
            grid=(blocks // 2,),
            in_specs=[pl.BlockSpec((2, part, columns), lambda j, s: (j, 0, 0))] * 2,
            out_specs=[half, half],
            micros=2,
        )
        self.sent = across_bit(send, self.left[0])
        self.left = self.left[1:]

    def last(self, ids, *others):
        while self.left:
            self.step(ids, *others)
        rows = lambda value: value.reshape(-1, value.shape[-1])
        return rows(self.kept), rows(after(self.sent, *others))


def double(value, have, bit):
    other = across_bit(value, bit)
    dim = sorted([*have, bit], reverse=True).index(bit)
    low = own_bit(bit) == 0
    return jnp.stack([jnp.where(low, value, other), jnp.where(low, other, value)], axis=dim)


def to_all(own):
    have = []
    value = own
    for bit in reversed(range(shard_bits())):
        value = double(value, have, bit)
        have.append(bit)
    return value.reshape(-1, own.shape[-1])


def added(*terms):
    total = terms[0].astype(F32)
    for term in terms[1:]:
        total = total + term.astype(F32)
    return total.astype(BF)


def whole(array):
    rank = len(array.shape)
    return pl.BlockSpec(array.shape, lambda *_: (0,) * rank)


def shaped(shape, dtype):
    return jax.ShapeDtypeStruct(shape, dtype)


def run(kernel, ids, args, outs, grid=(1,), in_specs=None, out_specs=None, scratch=(), micros=1, vmem=40):
    in_specs = in_specs or [None] * len(args)
    out_specs = out_specs or [None] * len(outs)
    in_specs = [whole(a) if s is None else s for a, s in zip(args, in_specs)]
    out_specs = [whole(a) if s is None else s for a, s in zip(outs, out_specs)]
    prefetch = () if ids is None else (ids,)
    return pl.pallas_call(
        functools.partial(kernel, None) if ids is None else kernel,
        out_shape=outs,
        grid_spec=pltpu.PrefetchScalarGridSpec(
            num_scalar_prefetch=len(prefetch),
            grid=grid,
            in_specs=in_specs,
            out_specs=out_specs,
            scratch_shapes=list(scratch),
        ),
        compiler_params=pltpu.CompilerParams(vmem_limit_bytes=vmem * MIB),
        cost_estimate=pl.CostEstimate(flops=int(micros * 0.5e9), transcendentals=0, bytes_accessed=1000),
    )(*prefetch, *args)


def after(value, *others):
    return lax.optimization_barrier((value, *others))[0]


def ln_rows(values):
    centred = values - jnp.mean(values, axis=-1, keepdims=True)
    spread = jnp.mean(centred * centred, axis=-1, keepdims=True)
    inverse = lax.rsqrt(spread + EPS)
    return centred * inverse, inverse


def ln_back(grad, gain, normed, inverse):
    scaled = grad * gain
    first = jnp.mean(scaled, axis=-1, keepdims=True)
    second = jnp.mean(scaled * normed, axis=-1, keepdims=True)
    return inverse * (scaled - first - normed * second)


def head_mask(head, heads):
    lanes = lax.broadcasted_iota(jnp.int32, (1, heads * HD), 1)
    return jnp.where(lanes // HD == head, 1.0, 0.0).astype(BF)


def by_head(rows, heads):
    return [rows * head_mask(head, heads) for head in range(heads)]


def layout_kernel(rows, lens, prompts, place, ids, begin):
    items = lens.shape[0]
    offset = place[0] * rows
    own_first = offset + place[1] * (rows // 4)
    reach = begin.shape[1]
    positions = offset + lax.broadcasted_iota(jnp.int32, (1, reach), 1)
    found = jnp.zeros((1, reach), jnp.int32)
    lows = [jnp.int32(0)] * (reach // BLOCK)
    begun = base = own_base = jnp.int32(0)
    for item in range(items):
        found = jnp.where(positions >= begun, begun, found)
        lows = [jnp.where(offset + block * BLOCK >= begun, begun, low) for block, low in enumerate(lows)]
        begun = begun + lens[item]
        base = base + jnp.where(begun <= offset, 1, 0)
        own_base = own_base + jnp.where(begun <= own_first, 1, 0)
    begin[...] = jnp.where(positions >= begun, begun, found) - offset
    lows = [jnp.where(offset + block * BLOCK >= begun, begun, low) for block, low in enumerate(lows)]
    base = jnp.minimum(base, items - 3)
    own_base = jnp.minimum(own_base, items - 2)
    begun = bound = jnp.int32(0)
    for item in range(items):
        begun = begun + lens[item]
        bound = jnp.where(own_base == item, begun, bound)
    ids[0] = place[0]
    ids[1] = place[1]
    ids[2] = base
    ids[3] = (own_base - base) * 128
    ids[4] = bound - own_first
    ids[5] = prompts[own_base]
    ids[6] = prompts[own_base + 1]
    ids[7] = 0
    for block, low in enumerate(lows):
        ids[8 + block] = low - offset


def pack_kernel(ids, merge, pq, pm, pack):
    width = pq.shape[1]
    pack[:width, :] = merge[...]
    pack[width : 2 * width, :] = pq[...].T
    pack[2 * width :, :] = pm[...]


def entry_kernel(ids, tok, gain, bias, wq, wk, wv, hid, q, kv, tail):
    width = wq.shape[1]
    normed, _ = ln_rows(tok[...].astype(F32))
    hidden = (normed * gain[...] + bias[...]).astype(BF)
    hid[...] = hidden
    kv[:, :width] = nn(hidden, wk[...]).astype(BF)
    kv[:, width:] = nn(hidden, wv[...]).astype(BF)
    q[...] = (nn(hidden, wq[...]).astype(BF) * SCALE).astype(BF)

    @pl.when(pl.program_id(0) == pl.num_programs(0) - 1)
    def _():
        tail[...] = kv[...]


def prompt_kernel(ids, text, pk, pv, out):
    width = pk.shape[1]
    out[:, :width] = nn(text[0], pk[...]).astype(BF)
    out[:, width:] = nn(text[0], pv[...]).astype(BF)


def window_bias(key_base, query_base, begin):
    shape = (BLOCK, BLOCK)
    key = key_base + lax.broadcasted_iota(jnp.int32, shape, 0)
    query = query_base + lax.broadcasted_iota(jnp.int32, shape, 1)
    return jnp.where((key <= query) & (key >= begin), 0.0, NEGATIVE).astype(F32)


def attend_block(keys, values_t, queries, bias, top, total, acc):
    heads = range(len(queries))
    before, sums, held = top[...], total[...], [acc[head] for head in heads]
    scores = [nt(keys, query) + bias for query in queries]
    after = [jnp.maximum(before[h : h + 1, :], jnp.max(scores[h], axis=0, keepdims=True)) for h in heads]
    unnorm = [jnp.exp(scores[h] - after[h]) for h in heads]
    fade = [jnp.exp(before[h : h + 1, :] - after[h]) for h in heads]
    parts = [nn(values_t[h * HD : (h + 1) * HD, :], unnorm[h].astype(BF)) for h in heads]
    added_up = [sums[h : h + 1, :] * fade[h] + jnp.sum(unnorm[h], axis=0, keepdims=True) for h in heads]
    for h in heads:
        acc[h] = held[h] * fade[h] + parts[h]
    top[...] = jnp.concatenate(after, axis=0)
    total[...] = jnp.concatenate(added_up, axis=0)


def attend_local_kernel(ids, q, kv, begin, acc_o, top_o, total_o, vt, acc, top, total):
    step = pl.program_id(0)
    width = q.shape[1]
    heads = width // HD
    blocks = kv.shape[0] // BLOCK

    @pl.when(step == 0)
    def _():
        for b in range(blocks):
            vt[b] = kv[b * BLOCK : (b + 1) * BLOCK, width:].T

    queries = by_head(q[...], heads)
    top[...] = jnp.full_like(top, NEGATIVE)
    total[...] = jnp.zeros_like(total)
    acc[...] = jnp.zeros_like(acc)
    low = lax.shift_right_logical(jnp.maximum(ids[8 + step], 0), 8)

    @pl.loop(low, step + 1)
    def _(b):
        row = pl.multiple_of(b * BLOCK, BLOCK)
        bias = window_bias(row, step * BLOCK, begin[...])
        attend_block(kv[pl.ds(row, BLOCK), :width], vt[b], queries, bias, top, total, acc)

    acc_o[0] = acc[...]
    top_o[0] = top[...]
    total_o[0] = total[...]


def attend_remote_kernel(ids, q, kv, tail, begin, acc_i, top_i, total_i, out, low_out, lse, ship_a, ship_b, ship0, vt, acc, top, total):
    step = pl.program_id(0)
    width = q.shape[1]
    heads = width // HD
    blocks = kv.shape[0] // BLOCK

    @pl.when(step == 0)
    def _():
        vt[0] = tail[:, width:].T
        for b in range(blocks):
            vt[b + 1] = kv[b * BLOCK : (b + 1) * BLOCK, width:].T

    queries = by_head(q[...], heads)
    acc[...] = acc_i[0]
    top[...] = top_i[0]
    total[...] = total_i[0]
    span = (blocks + 1) * BLOCK
    low = lax.shift_right_logical(jnp.maximum(ids[8 + step] + span, 0), 8)

    def bias_of(b):
        return window_bias(b * BLOCK - span, step * BLOCK, begin[...])

    @pl.when(low == 0)
    def _():
        attend_block(tail[:, :width], vt[0], queries, bias_of(0), top, total, acc)

    @pl.loop(jnp.maximum(low, 1), blocks + 1)
    def _(b):
        row = pl.multiple_of((b - 1) * BLOCK, BLOCK)
        attend_block(kv[pl.ds(row, BLOCK), :width], vt[b], queries, bias_of(b), top, total, acc)

    sums = top[...] + jnp.log(total[...])
    lse[0] = sums
    high = sums.astype(BF).astype(F32)
    both = jnp.concatenate([high, sums - high], axis=1)
    stacked = jnp.concatenate([acc[h] * (1.0 / total[h : h + 1, :]) for h in range(heads)], axis=0)
    rows = stacked.T
    out[0] = rows
    low_out[0] = rows.astype(BF)
    half = pl.num_programs(0) // 2

    def put(ship):
        ship[:BLOCK, :width] = q[...]
        ship[:BLOCK, width:] = rows.astype(BF)
        ship[BLOCK:, :] = jnp.concatenate([both, jnp.zeros((16 - heads, 2 * BLOCK), F32)], axis=0).astype(BF)

    @pl.when(step < half)
    def _():
        put(ship_a.at[0])

    @pl.when(step >= half)
    def _():
        put(ship_b.at[0])

    @pl.when(step == 0)
    def _():
        ship0[0] = ship_a[0]


def back_block(keys, values, keys_t, queries, grads, bias, lse, delta, dq, dkv):
    width = keys.shape[1]
    heads = range(len(queries))
    logs, deltas = lse[...], delta[...]
    probs = [jnp.exp(nt(keys, queries[h]) + bias - logs[h : h + 1, :]) for h in heads]
    prob_grads = [nt(values, grads[h]) for h in heads]
    score_grads = [(probs[h] * (prob_grads[h] - deltas[h : h + 1, :])).astype(BF) for h in heads]
    if dkv is not None:
        stack = lambda parts: jnp.concatenate(parts, axis=1)
        low = stack([prob.astype(BF) for prob in probs])
        dkv[:, :width] += nn(stack(score_grads), jnp.concatenate(queries, axis=0))
        dkv[:, width:] += nn(low, jnp.concatenate(grads, axis=0))
    if dq is not None:
        parts = [nn(keys_t[h * HD : (h + 1) * HD, :], score_grads[h]) for h in heads]
        for h in heads:
            dq[h] += parts[h]


def put_delta(delta, grad, out):
    products = (grad.astype(F32) * out.astype(F32)).T
    for head in range(delta.shape[0]):
        delta[head : head + 1, :] = jnp.sum(products[head * HD : (head + 1) * HD, :], axis=0, keepdims=True)


def back_local_kernel(ids, q, kv, begin, grad, out, lse, dkv_o, dq_o, delta_o, kt, dkv):
    step = pl.program_id(0)
    width = q.shape[1]
    heads = width // HD
    blocks = kv.shape[0] // BLOCK

    @pl.when(step == 0)
    def _():
        dkv[...] = jnp.zeros_like(dkv)
        for b in range(blocks):
            kt[b] = kv[b * BLOCK : (b + 1) * BLOCK, :width].T

    put_delta(delta_o.at[0], grad[0], out[0])
    dq_o[...] = jnp.zeros_like(dq_o)
    queries = by_head(q[...], heads)
    grads = by_head(grad[0], heads)
    low = lax.shift_right_logical(jnp.maximum(ids[8 + step], 0), 8)

    @pl.loop(low, step + 1)
    def _(b):
        row = pl.multiple_of(b * BLOCK, BLOCK)
        pair = kv[pl.ds(row, BLOCK), :]
        bias = window_bias(row, step * BLOCK, begin[...])
        back_block(
            pair[:, :width], pair[:, width:], kt[b], queries, grads, bias, lse.at[0], delta_o.at[0], dq_o.at[0], dkv.at[b]
        )

    @pl.when(step == pl.num_programs(0) - 1)
    def _():
        for b in range(blocks):
            dkv_o[b * BLOCK : (b + 1) * BLOCK, :] = dkv[b]


def back_query_kernel(ids, q, kv, tail, begin, grad, lse, delta, dq_i, dq_o, kt, dq):
    step = pl.program_id(0)
    width = q.shape[1]
    heads = width // HD
    blocks = kv.shape[0] // BLOCK

    @pl.when(step == 0)
    def _():
        kt[0] = tail[:, :width].T
        for b in range(blocks):
            kt[b + 1] = kv[b * BLOCK : (b + 1) * BLOCK, :width].T

    dq[...] = dq_i[0]
    span = (blocks + 1) * BLOCK
    low = lax.shift_right_logical(jnp.maximum(ids[8 + step] + span, 0), 8)

    @pl.when(low <= blocks)
    def _():
        queries = by_head(q[...], heads)
        grads = by_head(grad[0], heads)

        def one(b, pair):
            bias = window_bias(b * BLOCK - span, step * BLOCK, begin[...])
            back_block(pair[:, :width], pair[:, width:], kt[b], queries, grads, bias, lse.at[0], delta.at[0], dq, None)

        @pl.when(low == 0)
        def _():
            one(0, tail[...])

        @pl.loop(jnp.maximum(low, 1), blocks + 1)
        def _(b):
            row = pl.multiple_of((b - 1) * BLOCK, BLOCK)
            one(b, kv[pl.ds(row, BLOCK), :])

    stacked = jnp.concatenate([dq[h] for h in range(heads)], axis=0)
    dq_o[...] = (stacked.T * SCALE).astype(BF)


def back_key_kernel(ids, kv, begin, ship_low, ship_high, grad_n, ship_f, grad_f, dkv_i, dkv_o, delta, lse, dkv):
    step = pl.program_id(0)
    width = kv.shape[1] // 2
    heads = width // HD
    blocks = kv.shape[0] // BLOCK

    @pl.when(step == 0)
    def _():
        for b in range(blocks):
            dkv[b] = dkv_i[b * BLOCK : (b + 1) * BLOCK, :]

    low = lax.shift_right_logical(jnp.maximum(ids[8 + blocks + step], 0), 8)

    def all_keys(ship, grad):
        put_delta(delta, grad, ship[:BLOCK, width:])
        parts = ship[BLOCK:, :].astype(F32)
        lse[...] = parts[:heads, :BLOCK] + parts[:heads, BLOCK:]
        queries, grads = by_head(ship[:BLOCK, :width], heads), by_head(grad, heads)

        @pl.loop(low, blocks)
        def _(b):
            row = pl.multiple_of(b * BLOCK, BLOCK)
            pair = kv[pl.ds(row, BLOCK), :]
            bias = window_bias(row, blocks * BLOCK + step * BLOCK, begin[...])
            back_block(pair[:, :width], pair[:, width:], None, queries, grads, bias, lse, delta, None, dkv.at[b])

    @pl.when((low < blocks) & (step < blocks // 2))
    def _():
        all_keys(ship_low.at[0], grad_n[0])

    @pl.when((low < blocks) & (step >= blocks // 2) & (step < blocks))
    def _():
        all_keys(ship_high.at[0], grad_n[0])

    @pl.when((low < blocks) & (step == blocks))
    def _():
        all_keys(ship_f.at[0], grad_f[0])

    @pl.when(step == blocks)
    def _():
        for b in range(blocks):
            dkv_o[b * BLOCK : (b + 1) * BLOCK, :] = dkv[b].astype(BF)


def cross_bias(ids, prompt_rows, rows):
    shape = (2 * prompt_rows, rows)
    key = lax.broadcasted_iota(jnp.int32, shape, 0)
    query = lax.broadcasted_iota(jnp.int32, shape, 1)
    key_slot = lax.shift_right_logical(key, prompt_rows.bit_length() - 1)
    query_slot = jnp.where(query >= ids[4], 1, 0)
    limit = jnp.where(key_slot == 1, prompt_rows + ids[6], ids[5])
    return jnp.where((key_slot == query_slot) & (key < limit), 0.0, NEGATIVE).astype(F32)


def cross_kernel(ids, tok, low, *refs):
    packs, pairs = refs[:4], refs[4:8]
    gain2, bias2, gain3, bias3 = refs[8:12]
    after_self_o, two_o, q_o, stat_o, out_o, after_o, three_o = refs[12:]
    rows = tok.shape[0]
    width = packs[0].shape[0] // 3
    heads = width // HD
    rank = ids[1]
    prompt_rows = pairs[0].shape[0] // 3
    after = tok[...].astype(F32)
    for d in range(4):
        after = after + nn(low[rank ^ d], packs[d][:width, :])
    after_self_o[...] = after
    normed, _ = ln_rows(after)
    hidden = (normed * gain2[...] + bias2[...]).astype(BF)
    two_o[...] = hidden
    bias = cross_bias(ids, prompt_rows, rows)
    first = pl.multiple_of(ids[3], prompt_rows)
    for d in range(4):
        columns = slice(d * width, (d + 1) * width)
        query_rows = (nt(hidden, packs[d][width : 2 * width, :]).astype(BF) * SCALE).astype(BF)
        q_o[:, columns] = query_rows
        keys = pairs[d][pl.ds(first, 2 * prompt_rows), :width]
        values_t = pairs[d][pl.ds(first, 2 * prompt_rows), width:].T
        each = range(heads)
        scores = [nt(keys, query) + bias for query in by_head(query_rows, heads)]
        tops = [jnp.max(score, axis=0, keepdims=True) for score in scores]
        unnorm = [jnp.exp(scores[h] - tops[h]) for h in each]
        totals = [jnp.sum(value, axis=0, keepdims=True) for value in unnorm]
        stat_o[d * heads : (d + 1) * heads, :] = jnp.concatenate([tops[h] + jnp.log(totals[h]) for h in each], axis=0)
        parts = [nn(values_t[h * HD : (h + 1) * HD, :], unnorm[h].astype(BF)) * (1.0 / totals[h]) for h in each]
        out_o[:, columns] = jnp.concatenate(parts, axis=0).T.astype(BF)
    after = after_self_o[...]
    for d in range(4):
        after = after + nn(out_o[:, d * width : (d + 1) * width], packs[d][2 * width :, :])
    after_o[...] = after
    normed, _ = ln_rows(after)
    three_o[...] = (normed * gain3[...] + bias3[...]).astype(BF)


def cross_back_kernel(ids, kept, sent, crossed, og, after, after_self, q, stat, *refs):
    packs, pairs = refs[:4], refs[4:8]
    gain2, gain3 = refs[8:10]
    cog_o, cqg_o, slg_o, resid_o, shg_o, keep0_o, keep1_o, send_o, norms_o = refs[10:]
    rows, model = after.shape
    width = packs[0].shape[0] // 3
    heads = width // HD
    rank = ids[1]
    prompt_rows = pairs[0].shape[0] // 3
    grad = kept[...].astype(F32) + sent[...].astype(F32) + crossed[...].astype(F32)
    normed, inverse = ln_rows(after[...])
    norms_o[0:1, :] = jnp.sum(grad * normed, axis=0, keepdims=True)
    norms_o[1:2, :] = jnp.sum(grad, axis=0, keepdims=True)
    resid = og[...].astype(F32) + ln_back(grad, gain3[...], normed, inverse)
    low_resid = resid.astype(BF)
    cog_o[...] = low_resid
    bias = cross_bias(ids, prompt_rows, rows)
    first = pl.multiple_of(ids[3], prompt_rows)
    keep0_o[...] = jnp.zeros_like(keep0_o)
    keep1_o[...] = jnp.zeros_like(keep1_o)
    send_o[...] = jnp.zeros_like(send_o)
    for d in range(4):
        columns = slice(d * width, (d + 1) * width)
        head_grad = nt(low_resid, packs[d][2 * width :, :]).astype(BF)
        keys = pairs[d][pl.ds(first, 2 * prompt_rows), :width]
        values = pairs[d][pl.ds(first, 2 * prompt_rows), width:]
        keys_t = keys.T
        each = range(heads)
        queries, grads = by_head(q[:, columns], heads), by_head(head_grad, heads)
        logs = stat[d * heads : (d + 1) * heads, :]
        probs = [jnp.exp(nt(keys, queries[h]) + bias - logs[h : h + 1, :]) for h in each]
        prob_grads = [nt(values, grads[h]) for h in each]
        deltas = [jnp.sum(probs[h] * prob_grads[h], axis=0, keepdims=True) for h in each]
        score_grads = [(probs[h] * (prob_grads[h] - deltas[h])).astype(BF) for h in each]
        key_sum = nn(jnp.concatenate(score_grads, axis=1), jnp.concatenate(queries, axis=0))
        value_sum = nn(jnp.concatenate([prob.astype(BF) for prob in probs], axis=1), jnp.concatenate(grads, axis=0))
        parts = [nn(keys_t[h * HD : (h + 1) * HD, :], score_grads[h]) for h in each]
        cqg_o[:, columns] = (jnp.concatenate(parts, axis=0).T * SCALE).astype(BF)
        target = (keep0_o, send_o.at[0], keep1_o, send_o.at[1])[d]
        target[pl.ds(first, 2 * prompt_rows), :width] = key_sum.astype(BF)
        target[pl.ds(first, 2 * prompt_rows), width:] = value_sum.astype(BF)
    two_grad = None
    for d in range(4):
        term = nn(cqg_o[:, d * width : (d + 1) * width], packs[d][width : 2 * width, :])
        two_grad = term if two_grad is None else two_grad + term
    normed, inverse = ln_rows(after_self[...])
    norms_o[2:3, :] = jnp.sum(two_grad * normed, axis=0, keepdims=True)
    norms_o[3:4, :] = jnp.sum(two_grad, axis=0, keepdims=True)
    resid = resid + ln_back(two_grad, gain2[...], normed, inverse)
    resid_o[...] = resid
    low_resid = resid.astype(BF)
    slg_o[...] = low_resid
    for d in range(4):
        shg_o[rank ^ d] = nt(low_resid, packs[d][:width, :]).astype(BF)


def feed_kernel(ids, h_a, h_b, dh_a, dh_b, expand, shrink, *outs):
    c = 0.7978845608028654

    def rows(h, dh, low_o, pre_o, out_o, three_o):
        v = nn(h[...], expand[...])
        square = v * v
        t = jnp.tanh(v * (c + (c * 0.044715) * square))
        half = 0.5 * (1.0 + t)
        low = (v * half).astype(BF)
        slope = half + (v * (1.0 - t * t)) * (0.5 * c + (1.5 * c * 0.044715) * square)
        pre = (dh[...].astype(F32) * slope).astype(BF)
        low_o[...] = low
        pre_o[...] = pre
        out_o[...] = nn(low, shrink[...]).astype(BF)
        three_o[...] = nt(pre, expand[...]).astype(BF)

    half = pl.num_programs(0) // 2

    @pl.when(pl.program_id(0) < half)
    def _():
        rows(h_a, dh_a, *outs[:4])

    @pl.when(pl.program_id(0) >= half)
    def _():
        rows(h_b, dh_b, *outs[4:])


def feed(ids, base, h_a, h_b, dh, expand, shrink):
    rows, model = h_a.shape
    hidden = expand.shape[1]
    tile = 128
    tiles = rows // tile
    first, second = lambda j: jnp.minimum(j, tiles - 1), lambda j: jnp.maximum(j - tiles, 0)
    spec = lambda columns, at: pl.BlockSpec((tile, columns), lambda j, s: (at(j), 0))
    own = lambda d, at: pl.BlockSpec((tile, hidden), lambda j, s: ((s[1] ^ d) * tiles + at(j), 0))
    outs = lambda at: [spec(hidden, at), spec(hidden, at), spec(model, at), spec(model, at)]
    return run(
        feed_kernel,
        ids,
        (h_a, h_b, dh, dh, expand, shrink),
        [shaped((rows, hidden), BF), shaped((rows, hidden), BF), shaped((rows, model), BF), shaped((rows, model), BF)] * 2,
        grid=(2 * tiles,),
        in_specs=[spec(model, first), spec(model, second), own(base, first), own(base + 1, second), None, None],
        out_specs=outs(first) + outs(second),
        micros=12,
    )


def spread(ids, rows, kept, send):
    far, part, _ = kept.shape
    own = ids[0] % 2
    for block in range(far):
        kept[block] = rows[pl.ds(pl.multiple_of((2 * block + own) * part, part), part), :]
        send[block] = rows[pl.ds(pl.multiple_of((2 * block + 1 - own) * part, part), part), :]


def feed_weights_kernel(ids, *refs):
    threes, pres, lows = refs[:4], refs[4:8], refs[8:12]
    og, out, turned = refs[12:]
    step = pl.program_id(0)
    half = pl.num_programs(0) // 2
    rank = ids[1]
    rows = threes[0].shape[0]

    @pl.when(step == 0)
    def _():
        for d in range(4):
            turned[:, d * rows : (d + 1) * rows] = threes[d][...].T

    @pl.when(step == half)
    def _():
        for d in range(4):
            turned[:, d * rows : (d + 1) * rows] = og[pl.ds(pl.multiple_of((rank ^ d) * rows, rows), rows), :].T

    @pl.when(step < half)
    def _():
        out[...] = nn(turned[...], jnp.concatenate([p[...] for p in pres], axis=0)).astype(BF)

    @pl.when(step >= half)
    def _():
        out[...] = nn(turned[...], jnp.concatenate([p[...] for p in lows], axis=0)).astype(BF)


def feed_weights(ids, threes, pres, lows, og):
    rows, model = threes[0].shape
    hidden = pres[0].shape[1]
    chunk = 256
    half = hidden // chunk
    front = pl.BlockSpec((rows, chunk), lambda j, s: (0, jnp.minimum(j, half - 1)))
    back = pl.BlockSpec((rows, chunk), lambda j, s: (0, jnp.maximum(j - half, 0)))
    return run(
        feed_weights_kernel,
        ids,
        (*threes, *pres, *lows, og),
        [shaped((model, 2 * hidden), BF)],
        grid=(2 * half,),
        in_specs=[None] * 4 + [front] * 4 + [back] * 4 + [None],
        out_specs=[pl.BlockSpec((model, chunk), lambda j, s: (0, j))],
        scratch=[pltpu.VMEM((model, 4 * rows), BF)],
        micros=9,
        vmem=60,
    )[0]


def head_weights_kernel(ids, two, cqg, cog, crossed, slg, low, keep0, keep1, send):
    rank = ids[1]
    width = low.shape[2]
    two_t, cog_t, slg_t = two[...].T, cog[...].T, slg[...].T
    for d, out in enumerate((keep0, send.at[0], keep1, send.at[1])):
        columns = slice(d * width, (d + 1) * width)
        out[:, :width] = nn(two_t, cqg[:, columns]).astype(BF)
        out[:, width : 2 * width] = nn(cog_t, crossed[:, columns]).astype(BF)
        out[:, 2 * width :] = nn(slg_t, low[rank ^ d]).astype(BF)


def one_grad_kernel(ids, kvg, hid, dq, wq, wk, wv, gain, bias, keep0, keep1, send, norms):
    rows, width2 = kvg.shape
    width = width2 // 2
    quarter = rows // 4
    rank = ids[1]
    product = total = None
    for d in (1, 3, 2, 0):
        own = pl.ds(pl.multiple_of((rank ^ d) * quarter, quarter), quarter)
        part = (
            nt(dq[own, :], wq[...]) + nt(kvg[own, :width], wk[...]) + nt(kvg[own, width:], wv[...])
        )
        hidden = hid[own, :].astype(F32)
        term = jnp.sum(part * hidden, axis=0, keepdims=True)
        plain = jnp.sum(part, axis=0, keepdims=True)
        product = term if product is None else product + term
        total = plain if total is None else total + plain
        (keep0, send.at[0], keep1, send.at[1])[d][...] = part.astype(BF)
    norms[0:1, :] = (product - bias[...] * total) / gain[...]
    norms[1:2, :] = total


def text_kernel(ids, own, pk, pv, keep0, keep1, send):
    width = own.shape[1] // 2
    rank = ids[1]
    for d, out in enumerate((keep0, send.at[0], keep1, send.at[1])):
        columns = pl.ds(pl.multiple_of((rank ^ d) * width, width), width)
        out[...] = (nt(own[:, :width], pk[columns, :]) + nt(own[:, width:], pv[columns, :])).astype(BF)


def entry_weights_kernel(ids, hid, dq, kvg, entry_norms, norms, kept, send, rows):
    width = dq.shape[1]
    model = hid.shape[1]
    turned = hid[...].T
    rows[:, :width] = nn(turned, dq[...]).astype(BF)
    rows[:, width : 3 * width] = nn(turned, kvg[...]).astype(BF)
    sums = jnp.concatenate([entry_norms[...], norms[...], jnp.zeros((122, model), F32)], axis=0)
    rows[:, 3 * width :] = sums.T.astype(BF)
    spread(ids, rows, kept, send)


def arrived_kernel(ids, *refs):
    feed, head, entry, (expand, shrink, pq, pm, merge, wq, wk, wv, norms) = refs[:1], refs[1:2], refs[2:4], refs[4:]

    def total(terms, width, index):
        columns = slice(index * width, (index + 1) * width)
        value = terms[0][:, columns].astype(F32)
        for term in terms[1:]:
            value = value + term[:, columns].astype(F32)
        return value

    hidden, width = expand.shape[1], pq.shape[1]
    expand[...] = total(feed, hidden, 0)
    shrink[...] = total(feed, hidden, 1).T
    pq[...] = total(head, width, 0)
    pm[...] = total(head, width, 1).T
    merge[...] = total(head, width, 2).T
    wq[...] = total(entry, width, 0)
    wk[...] = total(entry, width, 1)
    wv[...] = total(entry, width, 2)
    norms[...] = total(entry, 128, 3 * width // 128).T[:8, :]


def prompt_kernel_back(ids, text, grads, key, value, text_grad):
    width = key.shape[1]

    @pl.when(pl.program_id(0) == 0)
    def _():
        key[...] = jnp.zeros_like(key)
        value[...] = jnp.zeros_like(value)

    turned = text[...].T
    key[...] += nn(turned, grads[:, :width])
    value[...] += nn(turned, grads[:, width : 2 * width])
    text_grad[...] = grads[:, 2 * width :].astype(F32)


def entry_back_kernel(ids, keep, sent, crossed, tok, gain, resid, out):
    grad = keep[...].astype(F32) + sent[0].astype(F32) + crossed[...].astype(F32)
    normed, inverse = ln_rows(tok[...].astype(F32))
    out[...] = (resid[...] + ln_back(grad, gain[...], normed, inverse)).astype(BF)


def assemble_kernel(ids, *refs):
    out = refs[4]
    for d in range(4):

        @pl.when(pl.program_id(0) == ids[1] ^ d)
        def _():
            out[...] = refs[d][...].astype(out.dtype)


def assemble(ids, pieces, dtype):
    rows, model = pieces[0].shape
    return run(
        assemble_kernel,
        ids,
        pieces,
        [shaped((4 * rows, model), dtype)],
        grid=(4,),
        out_specs=[pl.BlockSpec((rows, model), lambda i, s: (i, 0))],
        micros=3,
    )[0]


def gather(own):
    across = partner(own, 2)
    near = partner(own, 1)
    return own, near, across, partner(across, 1)


def body(
    tokens,
    text_states,
    item_lengths,
    prompt_lengths,
    entry_gain,
    entry_bias,
    cross_gain,
    cross_bias_,
    mixer_gain,
    mixer_bias,
    query_weight,
    key_weight,
    value_weight,
    merge_weight,
    prompt_query,
    prompt_key,
    prompt_value,
    prompt_merge,
    expand_weight,
    shrink_weight,
    output_grad,
):
    rows, model = tokens.shape
    ranks = lax.axis_size("mp")
    width = query_weight.shape[1]
    heads = width // HD
    items, prompt_rows = text_states.shape[:2]
    quarter = rows // ranks
    steps = rows // BLOCK
    hidden_units = expand_weight.shape[1]
    shards = lax.axis_size("far") * lax.axis_size("near")
    assert ranks == 4 and quarter == BLOCK and prompt_rows == 128 and items % shards == 0

    place = jnp.stack([lax.axis_index(SEQ), lax.axis_index("mp")]).astype(jnp.int32)
    scalars = pl.BlockSpec(memory_space=pltpu.SMEM)
    ids, begin = pl.pallas_call(
        functools.partial(layout_kernel, rows),
        out_shape=[shaped((9 + 2 * steps + 7,), jnp.int32), shaped((1, 2 * rows + BLOCK), jnp.int32)],
        in_specs=[scalars] * 3,
        out_specs=[scalars, pl.BlockSpec(memory_space=pltpu.VMEM)],
    )(item_lengths, prompt_lengths, place)
    base = ids[2]

    row = lambda vector: vector.reshape(1, -1)
    own_rows = lambda columns: pl.BlockSpec((quarter, columns), lambda *g: (g[-1][1], 0))

    block_rows = lambda columns: pl.BlockSpec((BLOCK, columns), lambda i, *s: (i, 0))
    pack = run(pack_kernel, None, (merge_weight, prompt_query, prompt_merge), [shaped((3 * width, model), BF)], vmem=60)[0]
    pack_near, pack_across = partner(pack, 1), partner(pack, 2)
    hidden_one, q, kv, kv_tail = run(
        entry_kernel,
        None,
        (after(tokens, pack), row(entry_gain), row(entry_bias), query_weight, key_weight, value_weight),
        [
            shaped((rows, model), BF),
            shaped((rows, width), BF),
            shaped((rows, 2 * width), BF),
            shaped((BLOCK, 2 * width), BF),
        ],
        grid=(steps,),
        in_specs=[block_rows(model)] + [None] * 5,
        out_specs=[block_rows(model), block_rows(width), block_rows(2 * width), None],
        micros=2,
        vmem=60,
    )
    kv_near = from_behind(kv, 1)
    kv_far = from_behind(kv_tail, 2)

    pair = run(
        prompt_kernel,
        ids,
        (after(text_states, kv, pack_near), prompt_key, prompt_value),
        [shaped((3 * prompt_rows, 2 * width), BF)],
        grid=(3,),
        in_specs=[pl.BlockSpec((1, prompt_rows, model), lambda i, s: (s[2] + i, 0, 0)), None, None],
        out_specs=[pl.BlockSpec((prompt_rows, 2 * width), lambda i, s: (i, 0))],
        micros=1.5,
    )[0]
    pair_near, pair_across = partner(pair, 1), partner(pair, 2)
    hidden_grad = nt(after(output_grad, kv, pair), shrink_weight).astype(BF)

    state = [shaped((steps, heads, HD, BLOCK), F32), shaped((steps, heads, BLOCK), F32), shaped((steps, heads, BLOCK), F32)]
    state_specs = [
        pl.BlockSpec((1, heads, HD, BLOCK), lambda i, s: (i, 0, 0, 0)),
        pl.BlockSpec((1, heads, BLOCK), lambda i, s: (i, 0, 0)),
        pl.BlockSpec((1, heads, BLOCK), lambda i, s: (i, 0, 0)),
    ]
    state_scratch = [pltpu.VMEM((heads, HD, BLOCK), F32), pltpu.VMEM((heads, BLOCK), F32), pltpu.VMEM((heads, BLOCK), F32)]
    q_spec = block_rows(width)
    begin_spec = pl.BlockSpec((1, BLOCK), lambda i, s: (0, i))
    piece_spec = pl.BlockSpec((1, BLOCK, width), lambda i, s: (i, 0, 0))
    turned = lambda blocks: pltpu.VMEM((blocks, width, BLOCK), BF)
    acc, top, total = run(
        attend_local_kernel,
        ids,
        (after(q, pair_near), kv, begin),
        state,
        grid=(steps,),
        in_specs=[q_spec, None, begin_spec],
        out_specs=state_specs,
        scratch=[turned(steps)] + state_scratch,
        micros=13,
    )
    kv_near, kv_far = lax.optimization_barrier((kv_near, kv_far, acc, hidden_grad))[:2]
    def ship_spec(side):
        half = steps // 2
        index = (lambda i: jnp.maximum(i - half, 0)) if side else (lambda i: jnp.minimum(i, half - 1))
        return pl.BlockSpec((1, BLOCK + 16, 2 * width), lambda i, s: (index(jnp.minimum(i, steps - 1)), 0, 0))

    self_out, self_low, lse, ship_low, ship_high, ship_first = run(
        attend_remote_kernel,
        ids,
        (q, kv_near, kv_far, begin, acc, top, total),
        [shaped((steps, BLOCK, width), F32), shaped((steps, BLOCK, width), BF), shaped((steps, heads, BLOCK), F32)]
        + [shaped((blocks, BLOCK + 16, 2 * width), BF) for blocks in (steps // 2, steps // 2, 1)],
        grid=(steps,),
        in_specs=[q_spec, None, None, begin_spec] + state_specs,
        out_specs=[piece_spec, piece_spec, state_specs[1], ship_spec(0), ship_spec(1), None],
        scratch=[turned(steps + 1)] + state_scratch,
        micros=9,
    )
    low_rows = lax.all_to_all(self_low, "mp", 0, 0)
    pack_across, pair_across = lax.optimization_barrier((pack_across, pair_across, self_low))[:2]
    packs = (pack, pack_near, pack_across, partner(pack_across, 1))
    pairs = (pair, pair_near, pair_across, partner(pair_across, 1))

    wide = lambda dtype: shaped((quarter, model), dtype)
    stat_shape = shaped((ranks * heads, quarter), F32)
    norms = (row(cross_gain), row(cross_bias_), row(mixer_gain), row(mixer_bias))
    after_self, hidden_two, cross_q, stat, cross_out, after_cross, hidden_three = run(
        cross_kernel,
        ids,
        (tokens, low_rows, *packs, *pairs, *norms),
        [wide(F32), wide(BF), wide(BF), stat_shape, wide(BF), wide(F32), wide(BF)],
        in_specs=[own_rows(model)] + [None] * 13,
        micros=11,
    )

    ship_low, ship_high, ship_f = after((ship_low, ship_high, ship_first), hidden_three)
    ship_low, ship_f = from_behind(ship_low, -1), from_behind(ship_f, -2)

    three_near, three_across = partner(hidden_three, 1), partner(hidden_three, 2)
    low0, pre0, out0, part0, low1, pre1, out1, part1 = feed(
        ids, 0, hidden_three, three_near, hidden_grad, expand_weight, shrink_weight
    )
    three_across, ship_low, ship_f = after((three_across, ship_low, ship_f), part1)
    threes = (hidden_three, three_near, three_across, partner(three_across, 1))
    sent1, out_sent1 = partner(part1, 1), partner(out1, 1)
    low2, pre2, out2, part2, low3, pre3, out3, part3 = feed(
        ids, 2, threes[2], threes[3], hidden_grad, expand_weight, shrink_weight
    )
    part3, sent1, out_sent1, ship_high = after((part3, sent1, out_sent1, ship_high), part2)
    ship_high = from_behind(ship_high, -1)
    partial = (part2.astype(F32) + partner(part3, 1).astype(F32)).astype(BF)
    across = partner(partial, 2)
    out_partial = (out2.astype(F32) + partner(after(out3, partial), 1).astype(F32)).astype(BF)
    feed_grads = feed_weights(ids, threes, after((pre0, pre1, pre2, pre3), partial), (low0, low1, low2, low3), output_grad)
    feed_sum = lax.psum_scatter(feed_grads, SEQ, scatter_dimension=0, tiled=True)
    across, ship_high = after((across, ship_high), feed_grads, out_partial)
    out_across = partner(after(out_partial, across), 2)

    pair_out = shaped((3 * prompt_rows, 2 * width), BF)
    cog, cqg, slg, resid, shg, pair_keep0, pair_keep1, pair_send, norm_grads = run(
        cross_back_kernel,
        ids,
        (part0, sent1, across, output_grad, after_cross, after_self, cross_q, stat, *packs, *pairs, norms[0], norms[2]),
        [wide(BF), wide(BF), wide(BF), wide(F32), shaped((ranks, quarter, width), BF)]
        + [pair_out, pair_out, shaped((2, *pair_out.shape), BF), shaped((4, model), F32)],
        in_specs=[None] * 3 + [own_rows(model)] + [None] * 14,
        micros=15,
        vmem=48,
    )
    self_grad = lax.all_to_all(shg, "mp", 0, 0)

    pair_sent = partner(pair_send, 1)
    pieces = shaped((model, 3 * width), BF)
    head_keep0, head_keep1, head_send = run(
        head_weights_kernel,
        ids,
        (hidden_two, cqg, cog, cross_out, slg, low_rows),
        [pieces, pieces, shaped((2, *pieces.shape), BF)],
        micros=5,
        vmem=60,
    )
    head_sent = partner(head_send, 1)
    head_half = added(head_keep1, head_sent[1])
    self_grad, out_across, pair_sent, head_half = after((self_grad, out_across, pair_sent, head_half), head_keep0)
    head_across = partner(head_half, 2)
    grad_n, grad_f = from_behind(self_grad, -1), from_behind(self_grad[:1], -2)
    pair_half = added(pair_keep1, pair_sent[1])
    pair_across = partner(pair_half, 2)

    lse_spec = state_specs[1]
    stat4 = shaped((steps, heads, BLOCK), F32)
    dkv, dq_part, delta = run(
        back_local_kernel,
        ids,
        (q, kv, begin, after(self_grad, pair_half), self_out, lse),
        [shaped((rows, 2 * width), F32), state[0], stat4],
        grid=(steps,),
        in_specs=[q_spec, None, begin_spec, piece_spec, piece_spec, lse_spec],
        out_specs=[None, state_specs[0], lse_spec],
        scratch=[turned(steps), pltpu.VMEM((steps, BLOCK, 2 * width), F32)],
        micros=15,
    )
    pair_across, grad_n, grad_f = after((pair_across, grad_n, grad_f), dq_part)
    pair_sum = added(pair_keep0, pair_sent[0], pair_across).reshape(3, prompt_rows, 2 * width)
    placed = lax.dynamic_update_slice_in_dim(jnp.zeros((items, prompt_rows, 2 * width), BF), pair_sum, base, 0)
    placed = placed.reshape(shards // 2, 2, -1, 2 * width)
    own = own_bit(0)
    text_sum = ShardSum(
        lax.dynamic_index_in_dim(placed, own, 1, keepdims=False), lax.dynamic_index_in_dim(placed, 1 - own, 1, keepdims=False)
    )
    dq = run(
        back_query_kernel,
        ids,
        (q, kv_near, kv_far, begin, self_grad, lse, delta, after(dq_part, text_sum.kept)),
        [shaped((rows, width), BF)],
        grid=(steps,),
        in_specs=[q_spec, None, None, begin_spec, piece_spec, lse_spec, lse_spec, state_specs[0]],
        out_specs=[q_spec],
        scratch=[turned(steps + 1), state_scratch[0]],
        micros=7,
    )[0]
    far = shards // 2
    spread_out = [shaped((far, model // shards, 3 * width + 128), BF)] * 2
    text_sum.step(ids, dq)
    grad_n, grad_f = after((grad_n, grad_f), dq, text_sum.kept)
    held = lambda i: jnp.minimum(i, steps - 1)
    near_piece = pl.BlockSpec((1, BLOCK, width), lambda i, s: (held(i), 0, 0))
    kvg = run(
        back_key_kernel,
        ids,
        (kv, begin, ship_low, ship_high, grad_n, ship_f, grad_f, dkv),
        [shaped((rows, 2 * width), BF)],
        grid=(steps + 1,),
        in_specs=[None, pl.BlockSpec((1, BLOCK), lambda i, s: (0, steps + i)), ship_spec(0), ship_spec(1), near_piece] + [None] * 3,
        scratch=[pltpu.VMEM((heads, BLOCK), F32)] * 2 + [pltpu.VMEM((steps, BLOCK, 2 * width), F32)],
        micros=8,
    )[0]

    quarter_out = shaped((quarter, model), BF)
    one_keep0, one_keep1, one_send, entry_norms = run(
        one_grad_kernel,
        ids,
        (kvg, hidden_one, dq, query_weight, key_weight, value_weight, row(entry_gain), row(entry_bias)),
        [quarter_out, quarter_out, shaped((2, *quarter_out.shape), BF), shaped((2, model), F32)],
        micros=3,
    )
    one_sent = partner(one_send, 1)
    entry_rows = run(
        entry_weights_kernel,
        ids,
        (hidden_one, after(dq, one_send), kvg, entry_norms, norm_grads),
        spread_out,
        scratch=[pltpu.VMEM((model, 3 * width + 128), BF)],
        micros=4,
    )
    entry_sum = ShardSum(*entry_rows)
    head_rows = added(head_keep0, head_sent[0], after(head_across, kvg))
    one_half = added(one_keep1, after(one_sent, entry_rows[0], head_rows)[1])
    one_across = partner(one_half, 2)
    own_pair = added(*text_sum.last(ids, one_half))
    text_out = shaped((prompt_rows * items // shards, width), BF)
    text_keep0, text_keep1, text_send = run(
        text_kernel, ids, (own_pair, prompt_key, prompt_value), [text_out, text_out, shaped((2, *text_out.shape), BF)], micros=1
    )
    text_sent = partner(text_send, 1)
    text_half = added(text_keep1, text_sent[1])
    text_across = partner(text_half, 2)
    one_across = after(one_across, text_half, head_rows, feed_sum)
    head_sum = lax.psum_scatter(after(head_rows, feed_sum), SEQ, scatter_dimension=0, tiled=True)
    grad_rows = run(
        entry_back_kernel,
        ids,
        (one_keep0, one_sent, one_across, tokens, row(entry_gain), resid),
        [wide(BF)],
        in_specs=[None] * 3 + [own_rows(model)] + [None] * 2,
        micros=2,
        vmem=60,
    )[0]
    grad_pieces = gather(grad_rows)

    text_own = added(text_keep0, text_sent[0], after(text_across, grad_rows))
    entry_sum.step(ids, grad_rows)
    prompt_all = to_all(jnp.concatenate([own_pair, text_own], axis=1))
    all_text = items * prompt_rows
    some = min(all_text, 1024)
    key_prompt, value_prompt, text_grad = run(
        prompt_kernel_back,
        None,
        (text_states.reshape(all_text, model), prompt_all),
        [shaped((model, width), F32), shaped((model, width), F32), shaped((all_text, width), F32)],
        grid=(all_text // some,),
        in_specs=[pl.BlockSpec((some, model), lambda i: (i, 0)), pl.BlockSpec((some, 3 * width), lambda i: (i, 0))],
        out_specs=[None, None, pl.BlockSpec((some, width), lambda i: (i, 0))],
        micros=3,
    )
    text_grad = text_grad.reshape(items, prompt_rows, width)

    tokens_grad = assemble(ids, grad_pieces, F32)
    out_rows = added(after_cross, out0, out_sent1, out_across)
    out_pieces = gather(after(out_rows, grad_rows))
    layer_output = assemble(ids, out_pieces, BF)

    part = model // shards
    square, turned_square = shaped((part, width), F32), shaped((width, part), F32)
    expand_grad, shrink_grad, pq_grad, pm_grad, merge_grad, wq_grad, wk_grad, wv_grad, norm_sum = run(
        arrived_kernel,
        None,
        (feed_sum, head_sum, *entry_sum.last(ids, grad_rows)),
        [shaped((part, hidden_units), F32), shaped((hidden_units, part), F32)]
        + [square, turned_square, turned_square, square, square, square, shaped((8, part), F32)],
        micros=3,
    )
    norm_sum = norm_sum + partner(norm_sum, 1)
    norm_sum = norm_sum + partner(norm_sum, 2)
    return (
        layer_output,
        tokens_grad,
        text_grad,
        norm_sum[0],
        norm_sum[1],
        norm_sum[4],
        norm_sum[5],
        norm_sum[2],
        norm_sum[3],
        wq_grad,
        wk_grad,
        wv_grad,
        merge_grad,
        pq_grad,
        key_prompt,
        value_prompt,
        pm_grad,
        expand_grad,
        shrink_grad,
    )


def solution(mesh):
    shards = mesh.shape["seq"]
    mesh = jax.sharding.Mesh(mesh.devices.reshape(shards // 2, 2, mesh.shape["mp"]), (*SEQ, "mp"))
    seq, mp, both = P(SEQ, None), P("mp", None), P(None, "mp")
    return jax.shard_map(
        body,
        mesh=mesh,
        in_specs=(seq,) + (P(),) * 9 + (both,) * 3 + (mp,) + (both,) * 3 + (mp, both, mp, seq),
        out_specs=(
            (seq, seq, P(None, None, "mp"))
            + (P(SEQ),) * 6
            + (P(SEQ, "mp"),) * 3
            + (P("mp", SEQ), P(SEQ, "mp"), both, both, P("mp", SEQ), P(SEQ, "mp"), P("mp", SEQ))
        ),
        check_vma=False,
    )
```

```python
import functools

import jax
import jax.numpy as jnp
from jax import lax
from jax.experimental import pallas as pl
from jax.experimental.pallas import tpu as pltpu
from jax.sharding import PartitionSpec as P

HD = 64
ITEM_LEN = 1024
EPS = 1e-06
NEGATIVE = -1e30
BF = jnp.bfloat16
F32 = jnp.float32
BLOCK = 256
SCALE = HD**-0.5
MIB = 1 << 20


def dot(left, right, ld, rd):
    return lax.dot_general(left, right, (((ld,), (rd,)), ((), ())), preferred_element_type=F32)


def nn(left, right):
    return dot(left, right, 1, 0)


def nt(left, right):
    return dot(left, right, 1, 1)


def tn(left, right):
    return dot(left, right, 0, 0)


def partner(value, step):
    count = lax.axis_size("mp")
    return lax.ppermute(value, "mp", [(rank, rank ^ step) for rank in range(count)])


SEQ = ("far", "near")


def from_behind(value, steps):
    count = lax.axis_size("far") * lax.axis_size("near")
    leading, last = (max(0, -steps), min(count, count - steps))
    return lax.ppermute(value, SEQ, [(source, source + steps) for source in range(leading, last)])


def shard_bits():
    return (lax.axis_size("far") * lax.axis_size("near")).bit_length() - 1


def across_bit(value, bit):
    return lax.ppermute(value, SEQ, [(shard, shard ^ (1 << bit)) for shard in range(1 << shard_bits())])


def own_bit(bit):
    return lax.axis_index(SEQ) // (1 << bit) % 2


def step_kernel(bit, ids, kept, sent, kept_o, send_o):
    own = lax.shift_right_logical(ids[0], bit) % 2
    kept_o[0] = (kept[own].astype(F32) + sent[own].astype(F32)).astype(BF)
    send_o[0] = (kept[1 - own].astype(F32) + sent[1 - own].astype(F32)).astype(BF)


class ShardSum:
    def __init__(self, kept, send):
        self.left = list(range(1, shard_bits()))
        self.kept, self.sent = kept, across_bit(send, 0)

    def step(self, ids, *others):
        blocks, part, columns = self.kept.shape
        half = pl.BlockSpec((1, part, columns), lambda j, s: (j, 0, 0))
        self.kept, send = run(
            functools.partial(step_kernel, self.left[0]),
            ids,
            (self.kept, after(self.sent, *others)),
            [shaped((blocks // 2, part, columns), BF)] * 2,
            grid=(blocks // 2,),
            in_specs=[pl.BlockSpec((2, part, columns), lambda j, s: (j, 0, 0))] * 2,
            out_specs=[half, half],
            micros=2,
        )
        self.sent = across_bit(send, self.left[0])
        self.left = self.left[1:]

    def last(self, ids, *others):
        while self.left:
            self.step(ids, *others)
        rows = lambda value: value.reshape(-1, value.shape[-1])
        return rows(self.kept), rows(after(self.sent, *others))


def double(value, have, bit):
    other = across_bit(value, bit)
    dim = sorted([*have, bit], reverse=True).index(bit)
    low = own_bit(bit) == 0
    return jnp.stack([jnp.where(low, value, other), jnp.where(low, other, value)], axis=dim)


def to_all(own):
    have = []
    value = own
    for bit in reversed(range(shard_bits())):
        value = double(value, have, bit)
        have.append(bit)
    return value.reshape(-1, own.shape[-1])


def added(*terms):
    total = terms[0].astype(F32)
    for term in terms[1:]:
        total = total + term.astype(F32)
    return total.astype(BF)


def whole(array):
    rank = len(array.shape)
    return pl.BlockSpec(array.shape, lambda *_: (0,) * rank)


def shaped(shape, dtype):
    return jax.ShapeDtypeStruct(shape, dtype)


def run(kernel, ids, args, outs, grid=(1,), in_specs=None, out_specs=None, scratch=(), micros=1, vmem=40):
    in_specs = in_specs or [None] * len(args)
    out_specs = out_specs or [None] * len(outs)
    in_specs = [whole(a) if s is None else s for a, s in zip(args, in_specs)]
    out_specs = [whole(a) if s is None else s for a, s in zip(outs, out_specs)]
    prefetch = () if ids is None else (ids,)
    return pl.pallas_call(
        functools.partial(kernel, None) if ids is None else kernel,
        out_shape=outs,
        grid_spec=pltpu.PrefetchScalarGridSpec(
            num_scalar_prefetch=len(prefetch),
            grid=grid,
            in_specs=in_specs,
            out_specs=out_specs,
            scratch_shapes=list(scratch),
        ),
        compiler_params=pltpu.CompilerParams(vmem_limit_bytes=vmem * MIB),
        cost_estimate=pl.CostEstimate(flops=int(micros * 0.5e9), transcendentals=0, bytes_accessed=1000),
    )(*prefetch, *args)


def after(value, *others):
    return lax.optimization_barrier((value, *others))[0]


def ln_rows(values):
    centred = values - jnp.mean(values, axis=-1, keepdims=True)
    spread = jnp.mean(centred * centred, axis=-1, keepdims=True)
    inverse = lax.rsqrt(spread + EPS)
    return centred * inverse, inverse


def ln_back(grad, gain, normed, inverse):
    scaled = grad * gain
    first = jnp.mean(scaled, axis=-1, keepdims=True)
    second = jnp.mean(scaled * normed, axis=-1, keepdims=True)
    return inverse * (scaled - first - normed * second)


def head_mask(head, heads):
    lanes = lax.broadcasted_iota(jnp.int32, (1, heads * HD), 1)
    return jnp.where(lanes // HD == head, 1.0, 0.0).astype(BF)


def by_head(rows, heads):
    return [rows * head_mask(head, heads) for head in range(heads)]


def layout_kernel(rows, lens, prompts, place, ids, begin):
    items = lens.shape[0]
    offset = place[0] * rows
    own_first = offset + place[1] * (rows // 4)
    reach = begin.shape[1]
    positions = offset + lax.broadcasted_iota(jnp.int32, (1, reach), 1)
    found = jnp.zeros((1, reach), jnp.int32)
    lows = [jnp.int32(0)] * (reach // BLOCK)
    begun = base = own_base = jnp.int32(0)
    for item in range(items):
        found = jnp.where(positions >= begun, begun, found)
        lows = [jnp.where(offset + block * BLOCK >= begun, begun, low) for block, low in enumerate(lows)]
        begun = begun + lens[item]
        base = base + jnp.where(begun <= offset, 1, 0)
        own_base = own_base + jnp.where(begun <= own_first, 1, 0)
    begin[...] = jnp.where(positions >= begun, begun, found) - offset
    lows = [jnp.where(offset + block * BLOCK >= begun, begun, low) for block, low in enumerate(lows)]
    base = jnp.minimum(base, items - 3)
    own_base = jnp.minimum(own_base, items - 2)
    begun = bound = jnp.int32(0)
    for item in range(items):
        begun = begun + lens[item]
        bound = jnp.where(own_base == item, begun, bound)
    ids[0] = place[0]
    ids[1] = place[1]
    ids[2] = base
    ids[3] = (own_base - base) * 128
    ids[4] = bound - own_first
    ids[5] = prompts[own_base]
    ids[6] = prompts[own_base + 1]
    ids[7] = 0
    for block, low in enumerate(lows):
        ids[8 + block] = low - offset


def pack_kernel(ids, merge, pq, pm, pack):
    width = pq.shape[1]
    pack[:width, :] = merge[...]
    pack[width : 2 * width, :] = pq[...].T
    pack[2 * width :, :] = pm[...]


def entry_kernel(ids, tok, gain, bias, wq, wk, wv, hid, q, kv, tail):
    width = wq.shape[1]
    normed, _ = ln_rows(tok[...].astype(F32))
    hidden = (normed * gain[...] + bias[...]).astype(BF)
    hid[...] = hidden
    kv[:, :width] = nn(hidden, wk[...]).astype(BF)
    kv[:, width:] = nn(hidden, wv[...]).astype(BF)
    q[...] = (nn(hidden, wq[...]).astype(BF) * SCALE).astype(BF)

    @pl.when(pl.program_id(0) == pl.num_programs(0) - 1)
    def _():
        tail[...] = kv[...]


def prompt_kernel(ids, text, pk, pv, out):
    width = pk.shape[1]
    out[:, :width] = nn(text[0], pk[...]).astype(BF)
    out[:, width:] = nn(text[0], pv[...]).astype(BF)


def window_bias(key_base, query_base, begin):
    shape = (BLOCK, BLOCK)
    key = key_base + lax.broadcasted_iota(jnp.int32, shape, 0)
    query = query_base + lax.broadcasted_iota(jnp.int32, shape, 1)
    return jnp.where((key <= query) & (key >= begin), 0.0, NEGATIVE).astype(F32)


def attend_block(keys, values_t, queries, bias, top, total, acc):
    heads = range(len(queries))
    before, sums, held = top[...], total[...], [acc[head] for head in heads]
    scores = [nt(keys, query) + bias for query in queries]
    after = [jnp.maximum(before[h : h + 1, :], jnp.max(scores[h], axis=0, keepdims=True)) for h in heads]
    unnorm = [jnp.exp(scores[h] - after[h]) for h in heads]
    fade = [jnp.exp(before[h : h + 1, :] - after[h]) for h in heads]
    parts = [nn(values_t[h * HD : (h + 1) * HD, :], unnorm[h].astype(BF)) for h in heads]
    added_up = [sums[h : h + 1, :] * fade[h] + jnp.sum(unnorm[h], axis=0, keepdims=True) for h in heads]
    for h in heads:
        acc[h] = held[h] * fade[h] + parts[h]
    top[...] = jnp.concatenate(after, axis=0)
    total[...] = jnp.concatenate(added_up, axis=0)


def attend_local_kernel(ids, q, kv, begin, acc_o, top_o, total_o, vt, acc, top, total):
    step = pl.program_id(0)
    width = q.shape[1]
    heads = width // HD
    blocks = kv.shape[0] // BLOCK

    @pl.when(step == 0)
    def _():
        for b in range(blocks):
            vt[b] = kv[b * BLOCK : (b + 1) * BLOCK, width:].T

    queries = by_head(q[...], heads)
    top[...] = jnp.full_like(top, NEGATIVE)
    total[...] = jnp.zeros_like(total)
    acc[...] = jnp.zeros_like(acc)
    low = lax.shift_right_logical(jnp.maximum(ids[8 + step], 0), 8)

    @pl.loop(low, step + 1)
    def _(b):
        row = pl.multiple_of(b * BLOCK, BLOCK)
        bias = window_bias(row, step * BLOCK, begin[...])
        attend_block(kv[pl.ds(row, BLOCK), :width], vt[b], queries, bias, top, total, acc)

    acc_o[0] = acc[...]
    top_o[0] = top[...]
    total_o[0] = total[...]


def attend_remote_kernel(ids, q, kv, tail, begin, acc_i, top_i, total_i, out, low_out, lse, ship_a, ship_b, ship0, vt, acc, top, total):
    step = pl.program_id(0)
    width = q.shape[1]
    heads = width // HD
    blocks = kv.shape[0] // BLOCK

    @pl.when(step == 0)
    def _():
        vt[0] = tail[:, width:].T
        for b in range(blocks):
            vt[b + 1] = kv[b * BLOCK : (b + 1) * BLOCK, width:].T

    queries = by_head(q[...], heads)
    acc[...] = acc_i[0]
    top[...] = top_i[0]
    total[...] = total_i[0]
    span = (blocks + 1) * BLOCK
    low = lax.shift_right_logical(jnp.maximum(ids[8 + step] + span, 0), 8)

    def bias_of(b):
        return window_bias(b * BLOCK - span, step * BLOCK, begin[...])

    @pl.when(low == 0)
    def _():
        attend_block(tail[:, :width], vt[0], queries, bias_of(0), top, total, acc)

    @pl.loop(jnp.maximum(low, 1), blocks + 1)
    def _(b):
        row = pl.multiple_of((b - 1) * BLOCK, BLOCK)
        attend_block(kv[pl.ds(row, BLOCK), :width], vt[b], queries, bias_of(b), top, total, acc)

    sums = top[...] + jnp.log(total[...])
    lse[0] = sums
    high = sums.astype(BF).astype(F32)
    both = jnp.concatenate([high, sums - high], axis=1)
    stacked = jnp.concatenate([acc[h] * (1.0 / total[h : h + 1, :]) for h in range(heads)], axis=0)
    rows = stacked.T
    out[0] = rows
    low_out[0] = rows.astype(BF)
    half = pl.num_programs(0) // 2

    def put(ship):
        ship[:BLOCK, :width] = q[...]
        ship[:BLOCK, width:] = rows.astype(BF)
        ship[BLOCK:, :] = jnp.concatenate([both, jnp.zeros((16 - heads, 2 * BLOCK), F32)], axis=0).astype(BF)

    @pl.when(step < half)
    def _():
        put(ship_a.at[0])

    @pl.when(step >= half)
    def _():
        put(ship_b.at[0])

    @pl.when(step == 0)
    def _():
        ship0[0] = ship_a[0]


def back_block(keys, values, keys_t, queries, grads, bias, lse, delta, dq, dkv):
    width = keys.shape[1]
    heads = range(len(queries))
    logs, deltas = lse[...], delta[...]
    probs = [jnp.exp(nt(keys, queries[h]) + bias - logs[h : h + 1, :]) for h in heads]
    prob_grads = [nt(values, grads[h]) for h in heads]
    score_grads = [(probs[h] * (prob_grads[h] - deltas[h : h + 1, :])).astype(BF) for h in heads]
    if dkv is not None:
        stack = lambda parts: jnp.concatenate(parts, axis=1)
        low = stack([prob.astype(BF) for prob in probs])
        dkv[:, :width] += nn(stack(score_grads), jnp.concatenate(queries, axis=0))
        dkv[:, width:] += nn(low, jnp.concatenate(grads, axis=0))
    if dq is not None:
        parts = [nn(keys_t[h * HD : (h + 1) * HD, :], score_grads[h]) for h in heads]
        for h in heads:
            dq[h] += parts[h]


def put_delta(delta, grad, out):
    products = (grad.astype(F32) * out.astype(F32)).T
    for head in range(delta.shape[0]):
        delta[head : head + 1, :] = jnp.sum(products[head * HD : (head + 1) * HD, :], axis=0, keepdims=True)


def back_local_kernel(ids, q, kv, begin, grad, out, lse, dkv_o, dq_o, delta_o, kt, dkv):
    step = pl.program_id(0)
    width = q.shape[1]
    heads = width // HD
    blocks = kv.shape[0] // BLOCK

    @pl.when(step == 0)
    def _():
        dkv[...] = jnp.zeros_like(dkv)
        for b in range(blocks):
            kt[b] = kv[b * BLOCK : (b + 1) * BLOCK, :width].T

    put_delta(delta_o.at[0], grad[0], out[0])
    dq_o[...] = jnp.zeros_like(dq_o)
    queries = by_head(q[...], heads)
    grads = by_head(grad[0], heads)
    low = lax.shift_right_logical(jnp.maximum(ids[8 + step], 0), 8)

    @pl.loop(low, step + 1)
    def _(b):
        row = pl.multiple_of(b * BLOCK, BLOCK)
        pair = kv[pl.ds(row, BLOCK), :]
        bias = window_bias(row, step * BLOCK, begin[...])
        back_block(
            pair[:, :width], pair[:, width:], kt[b], queries, grads, bias, lse.at[0], delta_o.at[0], dq_o.at[0], dkv.at[b]
        )

    @pl.when(step == pl.num_programs(0) - 1)
    def _():
        for b in range(blocks):
            dkv_o[b * BLOCK : (b + 1) * BLOCK, :] = dkv[b]


def back_query_kernel(ids, q, kv, tail, begin, grad, lse, delta, dq_i, dq_o, kt, dq):
    step = pl.program_id(0)
    width = q.shape[1]
    heads = width // HD
    blocks = kv.shape[0] // BLOCK

    @pl.when(step == 0)
    def _():
        kt[0] = tail[:, :width].T
        for b in range(blocks):
            kt[b + 1] = kv[b * BLOCK : (b + 1) * BLOCK, :width].T

    dq[...] = dq_i[0]
    span = (blocks + 1) * BLOCK
    low = lax.shift_right_logical(jnp.maximum(ids[8 + step] + span, 0), 8)

    @pl.when(low <= blocks)
    def _():
        queries = by_head(q[...], heads)
        grads = by_head(grad[0], heads)

        def one(b, pair):
            bias = window_bias(b * BLOCK - span, step * BLOCK, begin[...])
            back_block(pair[:, :width], pair[:, width:], kt[b], queries, grads, bias, lse.at[0], delta.at[0], dq, None)

        @pl.when(low == 0)
        def _():
            one(0, tail[...])

        @pl.loop(jnp.maximum(low, 1), blocks + 1)
        def _(b):
            row = pl.multiple_of((b - 1) * BLOCK, BLOCK)
            one(b, kv[pl.ds(row, BLOCK), :])

    stacked = jnp.concatenate([dq[h] for h in range(heads)], axis=0)
    dq_o[...] = (stacked.T * SCALE).astype(BF)


def back_key_kernel(ids, kv, begin, ship_low, ship_high, grad_n, ship_f, grad_f, dkv_i, dkv_o, delta, lse, dkv):
    step = pl.program_id(0)
    width = kv.shape[1] // 2
    heads = width // HD
    blocks = kv.shape[0] // BLOCK

    @pl.when(step == 0)
    def _():
        for b in range(blocks):
            dkv[b] = dkv_i[b * BLOCK : (b + 1) * BLOCK, :]

    low = lax.shift_right_logical(jnp.maximum(ids[8 + blocks + step], 0), 8)

    def all_keys(ship, grad):
        put_delta(delta, grad, ship[:BLOCK, width:])
        parts = ship[BLOCK:, :].astype(F32)
        lse[...] = parts[:heads, :BLOCK] + parts[:heads, BLOCK:]
        queries, grads = by_head(ship[:BLOCK, :width], heads), by_head(grad, heads)

        @pl.loop(low, blocks)
        def _(b):
            row = pl.multiple_of(b * BLOCK, BLOCK)
            pair = kv[pl.ds(row, BLOCK), :]
            bias = window_bias(row, blocks * BLOCK + step * BLOCK, begin[...])
            back_block(pair[:, :width], pair[:, width:], None, queries, grads, bias, lse, delta, None, dkv.at[b])

    @pl.when((low < blocks) & (step < blocks // 2))
    def _():
        all_keys(ship_low.at[0], grad_n[0])

    @pl.when((low < blocks) & (step >= blocks // 2) & (step < blocks))
    def _():
        all_keys(ship_high.at[0], grad_n[0])

    @pl.when((low < blocks) & (step == blocks))
    def _():
        all_keys(ship_f.at[0], grad_f[0])

    @pl.when(step == blocks)
    def _():
        for b in range(blocks):
            dkv_o[b * BLOCK : (b + 1) * BLOCK, :] = dkv[b].astype(BF)


def cross_bias(ids, prompt_rows, rows):
    shape = (2 * prompt_rows, rows)
    key = lax.broadcasted_iota(jnp.int32, shape, 0)
    query = lax.broadcasted_iota(jnp.int32, shape, 1)
    key_slot = lax.shift_right_logical(key, prompt_rows.bit_length() - 1)
    query_slot = jnp.where(query >= ids[4], 1, 0)
    limit = jnp.where(key_slot == 1, prompt_rows + ids[6], ids[5])
    return jnp.where((key_slot == query_slot) & (key < limit), 0.0, NEGATIVE).astype(F32)


def cross_kernel(ids, tok, low, *refs):
    packs, pairs = refs[:4], refs[4:8]
    gain2, bias2, gain3, bias3 = refs[8:12]
    after_self_o, two_o, q_o, stat_o, out_o, after_o, three_o = refs[12:]
    rows = tok.shape[0]
    width = packs[0].shape[0] // 3
    heads = width // HD
    rank = ids[1]
    prompt_rows = pairs[0].shape[0] // 3
    after = tok[...].astype(F32)
    for d in range(4):
        after = after + nn(low[rank ^ d], packs[d][:width, :])
    after_self_o[...] = after
    normed, _ = ln_rows(after)
    hidden = (normed * gain2[...] + bias2[...]).astype(BF)
    two_o[...] = hidden
    bias = cross_bias(ids, prompt_rows, rows)
    first = pl.multiple_of(ids[3], prompt_rows)
    for d in range(4):
        columns = slice(d * width, (d + 1) * width)
        query_rows = (nt(hidden, packs[d][width : 2 * width, :]).astype(BF) * SCALE).astype(BF)
        q_o[:, columns] = query_rows
        keys = pairs[d][pl.ds(first, 2 * prompt_rows), :width]
        values_t = pairs[d][pl.ds(first, 2 * prompt_rows), width:].T
        each = range(heads)
        scores = [nt(keys, query) + bias for query in by_head(query_rows, heads)]
        tops = [jnp.max(score, axis=0, keepdims=True) for score in scores]
        unnorm = [jnp.exp(scores[h] - tops[h]) for h in each]
        totals = [jnp.sum(value, axis=0, keepdims=True) for value in unnorm]
        stat_o[d * heads : (d + 1) * heads, :] = jnp.concatenate([tops[h] + jnp.log(totals[h]) for h in each], axis=0)
        parts = [nn(values_t[h * HD : (h + 1) * HD, :], unnorm[h].astype(BF)) * (1.0 / totals[h]) for h in each]
        out_o[:, columns] = jnp.concatenate(parts, axis=0).T.astype(BF)
    after = after_self_o[...]
    for d in range(4):
        after = after + nn(out_o[:, d * width : (d + 1) * width], packs[d][2 * width :, :])
    after_o[...] = after
    normed, _ = ln_rows(after)
    three_o[...] = (normed * gain3[...] + bias3[...]).astype(BF)


def cross_back_kernel(ids, kept, sent, crossed, og, after, after_self, q, stat, *refs):
    packs, pairs = refs[:4], refs[4:8]
    gain2, gain3 = refs[8:10]
    cog_o, cqg_o, slg_o, resid_o, shg_o, keep0_o, keep1_o, send_o, norms_o = refs[10:]
    rows, model = after.shape
    width = packs[0].shape[0] // 3
    heads = width // HD
    rank = ids[1]
    prompt_rows = pairs[0].shape[0] // 3
    grad = kept[...].astype(F32) + sent[...].astype(F32) + crossed[...].astype(F32)
    normed, inverse = ln_rows(after[...])
    norms_o[0:1, :] = jnp.sum(grad * normed, axis=0, keepdims=True)
    norms_o[1:2, :] = jnp.sum(grad, axis=0, keepdims=True)
    resid = og[...].astype(F32) + ln_back(grad, gain3[...], normed, inverse)
    low_resid = resid.astype(BF)
    cog_o[...] = low_resid
    bias = cross_bias(ids, prompt_rows, rows)
    first = pl.multiple_of(ids[3], prompt_rows)
    keep0_o[...] = jnp.zeros_like(keep0_o)
    keep1_o[...] = jnp.zeros_like(keep1_o)
    send_o[...] = jnp.zeros_like(send_o)
    for d in range(4):
        columns = slice(d * width, (d + 1) * width)
        head_grad = nt(low_resid, packs[d][2 * width :, :]).astype(BF)
        keys = pairs[d][pl.ds(first, 2 * prompt_rows), :width]
        values = pairs[d][pl.ds(first, 2 * prompt_rows), width:]
        keys_t = keys.T
        each = range(heads)
        queries, grads = by_head(q[:, columns], heads), by_head(head_grad, heads)
        logs = stat[d * heads : (d + 1) * heads, :]
        probs = [jnp.exp(nt(keys, queries[h]) + bias - logs[h : h + 1, :]) for h in each]
        prob_grads = [nt(values, grads[h]) for h in each]
        deltas = [jnp.sum(probs[h] * prob_grads[h], axis=0, keepdims=True) for h in each]
        score_grads = [(probs[h] * (prob_grads[h] - deltas[h])).astype(BF) for h in each]
        key_sum = nn(jnp.concatenate(score_grads, axis=1), jnp.concatenate(queries, axis=0))
        value_sum = nn(jnp.concatenate([prob.astype(BF) for prob in probs], axis=1), jnp.concatenate(grads, axis=0))
        parts = [nn(keys_t[h * HD : (h + 1) * HD, :], score_grads[h]) for h in each]
        cqg_o[:, columns] = (jnp.concatenate(parts, axis=0).T * SCALE).astype(BF)
        target = (keep0_o, send_o.at[0], keep1_o, send_o.at[1])[d]
        target[pl.ds(first, 2 * prompt_rows), :width] = key_sum.astype(BF)
        target[pl.ds(first, 2 * prompt_rows), width:] = value_sum.astype(BF)
    two_grad = None
    for d in range(4):
        term = nn(cqg_o[:, d * width : (d + 1) * width], packs[d][width : 2 * width, :])
        two_grad = term if two_grad is None else two_grad + term
    normed, inverse = ln_rows(after_self[...])
    norms_o[2:3, :] = jnp.sum(two_grad * normed, axis=0, keepdims=True)
    norms_o[3:4, :] = jnp.sum(two_grad, axis=0, keepdims=True)
    resid = resid + ln_back(two_grad, gain2[...], normed, inverse)
    resid_o[...] = resid
    low_resid = resid.astype(BF)
    slg_o[...] = low_resid
    for d in range(4):
        shg_o[rank ^ d] = nt(low_resid, packs[d][:width, :]).astype(BF)


def feed_kernel(ids, h_a, h_b, dh_a, dh_b, expand, shrink, *outs):
    c = 0.7978845608028654

    def rows(h, dh, low_o, pre_o, out_o, three_o):
        v = nn(h[...], expand[...])
        square = v * v
        t = jnp.tanh(v * (c + (c * 0.044715) * square))
        half = 0.5 * (1.0 + t)
        low = (v * half).astype(BF)
        slope = half + (v * (1.0 - t * t)) * (0.5 * c + (1.5 * c * 0.044715) * square)
        pre = (dh[...].astype(F32) * slope).astype(BF)
        low_o[...] = low
        pre_o[...] = pre
        out_o[...] = nn(low, shrink[...]).astype(BF)
        three_o[...] = nt(pre, expand[...]).astype(BF)

    half = pl.num_programs(0) // 2

    @pl.when(pl.program_id(0) < half)
    def _():
        rows(h_a, dh_a, *outs[:4])

    @pl.when(pl.program_id(0) >= half)
    def _():
        rows(h_b, dh_b, *outs[4:])


def feed(ids, base, h_a, h_b, dh, expand, shrink):
    rows, model = h_a.shape
    hidden = expand.shape[1]
    tile = 128
    tiles = rows // tile
    first, second = lambda j: jnp.minimum(j, tiles - 1), lambda j: jnp.maximum(j - tiles, 0)
    spec = lambda columns, at: pl.BlockSpec((tile, columns), lambda j, s: (at(j), 0))
    own = lambda d, at: pl.BlockSpec((tile, hidden), lambda j, s: ((s[1] ^ d) * tiles + at(j), 0))
    outs = lambda at: [spec(hidden, at), spec(hidden, at), spec(model, at), spec(model, at)]
    return run(
        feed_kernel,
        ids,
        (h_a, h_b, dh, dh, expand, shrink),
        [shaped((rows, hidden), BF), shaped((rows, hidden), BF), shaped((rows, model), BF), shaped((rows, model), BF)] * 2,
        grid=(2 * tiles,),
        in_specs=[spec(model, first), spec(model, second), own(base, first), own(base + 1, second), None, None],
        out_specs=outs(first) + outs(second),
        micros=12,
    )


def spread(ids, rows, kept, send):
    far, part, _ = kept.shape
    own = ids[0] % 2
    for block in range(far):
        kept[block] = rows[pl.ds(pl.multiple_of((2 * block + own) * part, part), part), :]
        send[block] = rows[pl.ds(pl.multiple_of((2 * block + 1 - own) * part, part), part), :]


def feed_weights_kernel(ids, *refs):
    threes, pres, lows = refs[:4], refs[4:8], refs[8:12]
    og, out, turned = refs[12:]
    step = pl.program_id(0)
    half = pl.num_programs(0) // 2
    rank = ids[1]
    rows = threes[0].shape[0]

    @pl.when(step == 0)
    def _():
        for d in range(4):
            turned[:, d * rows : (d + 1) * rows] = threes[d][...].T

    @pl.when(step == half)
    def _():
        for d in range(4):
            turned[:, d * rows : (d + 1) * rows] = og[pl.ds(pl.multiple_of((rank ^ d) * rows, rows), rows), :].T

    @pl.when(step < half)
    def _():
        out[...] = nn(turned[...], jnp.concatenate([p[...] for p in pres], axis=0)).astype(BF)

    @pl.when(step >= half)
    def _():
        out[...] = nn(turned[...], jnp.concatenate([p[...] for p in lows], axis=0)).astype(BF)


def feed_weights(ids, threes, pres, lows, og):
    rows, model = threes[0].shape
    hidden = pres[0].shape[1]
    chunk = 256
    half = hidden // chunk
    front = pl.BlockSpec((rows, chunk), lambda j, s: (0, jnp.minimum(j, half - 1)))
    back = pl.BlockSpec((rows, chunk), lambda j, s: (0, jnp.maximum(j - half, 0)))
    return run(
        feed_weights_kernel,
        ids,
        (*threes, *pres, *lows, og),
        [shaped((model, 2 * hidden), BF)],
        grid=(2 * half,),
        in_specs=[None] * 4 + [front] * 4 + [back] * 4 + [None],
        out_specs=[pl.BlockSpec((model, chunk), lambda j, s: (0, j))],
        scratch=[pltpu.VMEM((model, 4 * rows), BF)],
        micros=9,
        vmem=60,
    )[0]


def head_weights_kernel(ids, two, cqg, cog, crossed, slg, low, keep0, keep1, send):
    rank = ids[1]
    width = low.shape[2]
    two_t, cog_t, slg_t = two[...].T, cog[...].T, slg[...].T
    for d, out in enumerate((keep0, send.at[0], keep1, send.at[1])):
        columns = slice(d * width, (d + 1) * width)
        out[:, :width] = nn(two_t, cqg[:, columns]).astype(BF)
        out[:, width : 2 * width] = nn(cog_t, crossed[:, columns]).astype(BF)
        out[:, 2 * width :] = nn(slg_t, low[rank ^ d]).astype(BF)


def one_grad_kernel(ids, kvg, hid, dq, wq, wk, wv, gain, bias, keep0, keep1, send, norms):
    rows, width2 = kvg.shape
    width = width2 // 2
    quarter = rows // 4
    rank = ids[1]
    product = total = None
    for d in (1, 3, 2, 0):
        own = pl.ds(pl.multiple_of((rank ^ d) * quarter, quarter), quarter)
        part = (
            nt(dq[own, :], wq[...]) + nt(kvg[own, :width], wk[...]) + nt(kvg[own, width:], wv[...])
        )
        hidden = hid[own, :].astype(F32)
        term = jnp.sum(part * hidden, axis=0, keepdims=True)
        plain = jnp.sum(part, axis=0, keepdims=True)
        product = term if product is None else product + term
        total = plain if total is None else total + plain
        (keep0, send.at[0], keep1, send.at[1])[d][...] = part.astype(BF)
    norms[0:1, :] = (product - bias[...] * total) / gain[...]
    norms[1:2, :] = total


def text_kernel(ids, own, pk, pv, keep0, keep1, send):
    width = own.shape[1] // 2
    rank = ids[1]
    for d, out in enumerate((keep0, send.at[0], keep1, send.at[1])):
        columns = pl.ds(pl.multiple_of((rank ^ d) * width, width), width)
        out[...] = (nt(own[:, :width], pk[columns, :]) + nt(own[:, width:], pv[columns, :])).astype(BF)


def entry_weights_kernel(ids, hid, dq, kvg, entry_norms, norms, kept, send, rows):
    width = dq.shape[1]
    model = hid.shape[1]
    turned = hid[...].T
    rows[:, :width] = nn(turned, dq[...]).astype(BF)
    rows[:, width : 3 * width] = nn(turned, kvg[...]).astype(BF)
    sums = jnp.concatenate([entry_norms[...], norms[...], jnp.zeros((122, model), F32)], axis=0)
    rows[:, 3 * width :] = sums.T.astype(BF)
    spread(ids, rows, kept, send)


def arrived_kernel(ids, *refs):
    feed, head, entry, (expand, shrink, pq, pm, merge, wq, wk, wv, norms) = refs[:1], refs[1:2], refs[2:4], refs[4:]

    def total(terms, width, index):
        columns = slice(index * width, (index + 1) * width)
        value = terms[0][:, columns].astype(F32)
        for term in terms[1:]:
            value = value + term[:, columns].astype(F32)
        return value

    hidden, width = expand.shape[1], pq.shape[1]
    expand[...] = total(feed, hidden, 0)
    shrink[...] = total(feed, hidden, 1).T
    pq[...] = total(head, width, 0)
    pm[...] = total(head, width, 1).T
    merge[...] = total(head, width, 2).T
    wq[...] = total(entry, width, 0)
    wk[...] = total(entry, width, 1)
    wv[...] = total(entry, width, 2)
    norms[...] = total(entry, 128, 3 * width // 128).T[:8, :]


def prompt_kernel_back(ids, text, grads, key, value, text_grad):
    width = key.shape[1]

    @pl.when(pl.program_id(0) == 0)
    def _():
        key[...] = jnp.zeros_like(key)
        value[...] = jnp.zeros_like(value)

    turned = text[...].T
    key[...] += nn(turned, grads[:, :width])
    value[...] += nn(turned, grads[:, width : 2 * width])
    text_grad[...] = grads[:, 2 * width :].astype(F32)


def entry_back_kernel(ids, keep, sent, crossed, tok, gain, resid, out):
    grad = keep[...].astype(F32) + sent[0].astype(F32) + crossed[...].astype(F32)
    normed, inverse = ln_rows(tok[...].astype(F32))
    out[...] = (resid[...] + ln_back(grad, gain[...], normed, inverse)).astype(BF)


def assemble_kernel(ids, *refs):
    out = refs[4]
    for d in range(4):

        @pl.when(pl.program_id(0) == ids[1] ^ d)
        def _():
            out[...] = refs[d][...].astype(out.dtype)


def assemble(ids, pieces, dtype):
    rows, model = pieces[0].shape
    return run(
        assemble_kernel,
        ids,
        pieces,
        [shaped((4 * rows, model), dtype)],
        grid=(4,),
        out_specs=[pl.BlockSpec((rows, model), lambda i, s: (i, 0))],
        micros=3,
    )[0]


def gather(own):
    across = partner(own, 2)
    near = partner(own, 1)
    return own, near, across, partner(across, 1)


def body(
    tokens,
    text_states,
    item_lengths,
    prompt_lengths,
    entry_gain,
    entry_bias,
    cross_gain,
    cross_bias_,
    mixer_gain,
    mixer_bias,
    query_weight,
    key_weight,
    value_weight,
    merge_weight,
    prompt_query,
    prompt_key,
    prompt_value,
    prompt_merge,
    expand_weight,
    shrink_weight,
    output_grad,
):
    rows, model = tokens.shape
    ranks = lax.axis_size("mp")
    width = query_weight.shape[1]
    heads = width // HD
    items, prompt_rows = text_states.shape[:2]
    quarter = rows // ranks
    steps = rows // BLOCK
    hidden_units = expand_weight.shape[1]
    shards = lax.axis_size("far") * lax.axis_size("near")
    assert ranks == 4 and quarter == BLOCK and prompt_rows == 128 and items % shards == 0

    place = jnp.stack([lax.axis_index(SEQ), lax.axis_index("mp")]).astype(jnp.int32)
    scalars = pl.BlockSpec(memory_space=pltpu.SMEM)
    ids, begin = pl.pallas_call(
        functools.partial(layout_kernel, rows),
        out_shape=[shaped((9 + 2 * steps + 7,), jnp.int32), shaped((1, 2 * rows + BLOCK), jnp.int32)],
        in_specs=[scalars] * 3,
        out_specs=[scalars, pl.BlockSpec(memory_space=pltpu.VMEM)],
    )(item_lengths, prompt_lengths, place)
    base = ids[2]

    row = lambda vector: vector.reshape(1, -1)
    own_rows = lambda columns: pl.BlockSpec((quarter, columns), lambda *g: (g[-1][1], 0))

    block_rows = lambda columns: pl.BlockSpec((BLOCK, columns), lambda i, *s: (i, 0))
    pack = run(pack_kernel, None, (merge_weight, prompt_query, prompt_merge), [shaped((3 * width, model), BF)], vmem=60)[0]
    pack_near, pack_across = partner(pack, 1), partner(pack, 2)
    hidden_one, q, kv, kv_tail = run(
        entry_kernel,
        None,
        (after(tokens, pack), row(entry_gain), row(entry_bias), query_weight, key_weight, value_weight),
        [
            shaped((rows, model), BF),
            shaped((rows, width), BF),
            shaped((rows, 2 * width), BF),
            shaped((BLOCK, 2 * width), BF),
        ],
        grid=(steps,),
        in_specs=[block_rows(model)] + [None] * 5,
        out_specs=[block_rows(model), block_rows(width), block_rows(2 * width), None],
        micros=2,
        vmem=60,
    )
    kv_near = from_behind(kv, 1)
    kv_far = from_behind(kv_tail, 2)

    pair = run(
        prompt_kernel,
        ids,
        (after(text_states, kv, pack_near), prompt_key, prompt_value),
        [shaped((3 * prompt_rows, 2 * width), BF)],
        grid=(3,),
        in_specs=[pl.BlockSpec((1, prompt_rows, model), lambda i, s: (s[2] + i, 0, 0)), None, None],
        out_specs=[pl.BlockSpec((prompt_rows, 2 * width), lambda i, s: (i, 0))],
        micros=1.5,
    )[0]
    pair_near, pair_across = partner(pair, 1), partner(pair, 2)
    hidden_grad = nt(after(output_grad, kv, pair), shrink_weight).astype(BF)

    state = [shaped((steps, heads, HD, BLOCK), F32), shaped((steps, heads, BLOCK), F32), shaped((steps, heads, BLOCK), F32)]
    state_specs = [
        pl.BlockSpec((1, heads, HD, BLOCK), lambda i, s: (i, 0, 0, 0)),
        pl.BlockSpec((1, heads, BLOCK), lambda i, s: (i, 0, 0)),
        pl.BlockSpec((1, heads, BLOCK), lambda i, s: (i, 0, 0)),
    ]
    state_scratch = [pltpu.VMEM((heads, HD, BLOCK), F32), pltpu.VMEM((heads, BLOCK), F32), pltpu.VMEM((heads, BLOCK), F32)]
    q_spec = block_rows(width)
    begin_spec = pl.BlockSpec((1, BLOCK), lambda i, s: (0, i))
    piece_spec = pl.BlockSpec((1, BLOCK, width), lambda i, s: (i, 0, 0))
    turned = lambda blocks: pltpu.VMEM((blocks, width, BLOCK), BF)
    acc, top, total = run(
        attend_local_kernel,
        ids,
        (after(q, pair_near), kv, begin),
        state,
        grid=(steps,),
        in_specs=[q_spec, None, begin_spec],
        out_specs=state_specs,
        scratch=[turned(steps)] + state_scratch,
        micros=13,
    )
    kv_near, kv_far = lax.optimization_barrier((kv_near, kv_far, acc, hidden_grad))[:2]
    def ship_spec(side):
        half = steps // 2
        index = (lambda i: jnp.maximum(i - half, 0)) if side else (lambda i: jnp.minimum(i, half - 1))
        return pl.BlockSpec((1, BLOCK + 16, 2 * width), lambda i, s: (index(jnp.minimum(i, steps - 1)), 0, 0))

    self_out, self_low, lse, ship_low, ship_high, ship_first = run(
        attend_remote_kernel,
        ids,
        (q, kv_near, kv_far, begin, acc, top, total),
        [shaped((steps, BLOCK, width), F32), shaped((steps, BLOCK, width), BF), shaped((steps, heads, BLOCK), F32)]
        + [shaped((blocks, BLOCK + 16, 2 * width), BF) for blocks in (steps // 2, steps // 2, 1)],
        grid=(steps,),
        in_specs=[q_spec, None, None, begin_spec] + state_specs,
        out_specs=[piece_spec, piece_spec, state_specs[1], ship_spec(0), ship_spec(1), None],
        scratch=[turned(steps + 1)] + state_scratch,
        micros=9,
    )
    low_rows = lax.all_to_all(self_low, "mp", 0, 0)
    pack_across, pair_across = lax.optimization_barrier((pack_across, pair_across, self_low))[:2]
    packs = (pack, pack_near, pack_across, partner(pack_across, 1))
    pairs = (pair, pair_near, pair_across, partner(pair_across, 1))

    wide = lambda dtype: shaped((quarter, model), dtype)
    stat_shape = shaped((ranks * heads, quarter), F32)
    norms = (row(cross_gain), row(cross_bias_), row(mixer_gain), row(mixer_bias))
    after_self, hidden_two, cross_q, stat, cross_out, after_cross, hidden_three = run(
        cross_kernel,
        ids,
        (tokens, low_rows, *packs, *pairs, *norms),
        [wide(F32), wide(BF), wide(BF), stat_shape, wide(BF), wide(F32), wide(BF)],
        in_specs=[own_rows(model)] + [None] * 13,
        micros=11,
    )

    ship_low, ship_high, ship_f = after((ship_low, ship_high, ship_first), hidden_three)
    ship_low, ship_f = from_behind(ship_low, -1), from_behind(ship_f, -2)

    three_near, three_across = partner(hidden_three, 1), partner(hidden_three, 2)
    low0, pre0, out0, part0, low1, pre1, out1, part1 = feed(
        ids, 0, hidden_three, three_near, hidden_grad, expand_weight, shrink_weight
    )
    three_across, ship_low, ship_f = after((three_across, ship_low, ship_f), part1)
    threes = (hidden_three, three_near, three_across, partner(three_across, 1))
    sent1, out_sent1 = partner(part1, 1), partner(out1, 1)
    low2, pre2, out2, part2, low3, pre3, out3, part3 = feed(
        ids, 2, threes[2], threes[3], hidden_grad, expand_weight, shrink_weight
    )
    part3, sent1, out_sent1, ship_high = after((part3, sent1, out_sent1, ship_high), part2)
    ship_high = from_behind(ship_high, -1)
    partial = (part2.astype(F32) + partner(part3, 1).astype(F32)).astype(BF)
    across = partner(partial, 2)
    out_partial = (out2.astype(F32) + partner(after(out3, partial), 1).astype(F32)).astype(BF)
    feed_grads = feed_weights(ids, threes, after((pre0, pre1, pre2, pre3), partial), (low0, low1, low2, low3), output_grad)
    feed_sum = lax.psum_scatter(feed_grads, SEQ, scatter_dimension=0, tiled=True)
    across, ship_high = after((across, ship_high), feed_grads, out_partial)
    out_across = partner(after(out_partial, across), 2)

    pair_out = shaped((3 * prompt_rows, 2 * width), BF)
    cog, cqg, slg, resid, shg, pair_keep0, pair_keep1, pair_send, norm_grads = run(
        cross_back_kernel,
        ids,
        (part0, sent1, across, output_grad, after_cross, after_self, cross_q, stat, *packs, *pairs, norms[0], norms[2]),
        [wide(BF), wide(BF), wide(BF), wide(F32), shaped((ranks, quarter, width), BF)]
        + [pair_out, pair_out, shaped((2, *pair_out.shape), BF), shaped((4, model), F32)],
        in_specs=[None] * 3 + [own_rows(model)] + [None] * 14,
        micros=15,
        vmem=48,
    )
    self_grad = lax.all_to_all(shg, "mp", 0, 0)

    pair_sent = partner(pair_send, 1)
    pieces = shaped((model, 3 * width), BF)
    head_keep0, head_keep1, head_send = run(
        head_weights_kernel,
        ids,
        (hidden_two, cqg, cog, cross_out, slg, low_rows),
        [pieces, pieces, shaped((2, *pieces.shape), BF)],
        micros=5,
        vmem=60,
    )
    head_sent = partner(head_send, 1)
    head_half = added(head_keep1, head_sent[1])
    self_grad, out_across, pair_sent, head_half = after((self_grad, out_across, pair_sent, head_half), head_keep0)
    head_across = partner(head_half, 2)
    grad_n, grad_f = from_behind(self_grad, -1), from_behind(self_grad[:1], -2)
    pair_half = added(pair_keep1, pair_sent[1])
    pair_across = partner(pair_half, 2)

    lse_spec = state_specs[1]
    stat4 = shaped((steps, heads, BLOCK), F32)
    dkv, dq_part, delta = run(
        back_local_kernel,
        ids,
        (q, kv, begin, after(self_grad, pair_half), self_out, lse),
        [shaped((rows, 2 * width), F32), state[0], stat4],
        grid=(steps,),
        in_specs=[q_spec, None, begin_spec, piece_spec, piece_spec, lse_spec],
        out_specs=[None, state_specs[0], lse_spec],
        scratch=[turned(steps), pltpu.VMEM((steps, BLOCK, 2 * width), F32)],
        micros=15,
    )
    pair_across, grad_n, grad_f = after((pair_across, grad_n, grad_f), dq_part)
    pair_sum = added(pair_keep0, pair_sent[0], pair_across).reshape(3, prompt_rows, 2 * width)
    placed = lax.dynamic_update_slice_in_dim(jnp.zeros((items, prompt_rows, 2 * width), BF), pair_sum, base, 0)
    placed = placed.reshape(shards // 2, 2, -1, 2 * width)
    own = own_bit(0)
    text_sum = ShardSum(
        lax.dynamic_index_in_dim(placed, own, 1, keepdims=False), lax.dynamic_index_in_dim(placed, 1 - own, 1, keepdims=False)
    )
    dq = run(
        back_query_kernel,
        ids,
        (q, kv_near, kv_far, begin, self_grad, lse, delta, after(dq_part, text_sum.kept)),
        [shaped((rows, width), BF)],
        grid=(steps,),
        in_specs=[q_spec, None, None, begin_spec, piece_spec, lse_spec, lse_spec, state_specs[0]],
        out_specs=[q_spec],
        scratch=[turned(steps + 1), state_scratch[0]],
        micros=7,
    )[0]
    far = shards // 2
    spread_out = [shaped((far, model // shards, 3 * width + 128), BF)] * 2
    text_sum.step(ids, dq)
    grad_n, grad_f = after((grad_n, grad_f), dq, text_sum.kept)
    held = lambda i: jnp.minimum(i, steps - 1)
    near_piece = pl.BlockSpec((1, BLOCK, width), lambda i, s: (held(i), 0, 0))
    kvg = run(
        back_key_kernel,
        ids,
        (kv, begin, ship_low, ship_high, grad_n, ship_f, grad_f, dkv),
        [shaped((rows, 2 * width), BF)],
        grid=(steps + 1,),
        in_specs=[None, pl.BlockSpec((1, BLOCK), lambda i, s: (0, steps + i)), ship_spec(0), ship_spec(1), near_piece] + [None] * 3,
        scratch=[pltpu.VMEM((heads, BLOCK), F32)] * 2 + [pltpu.VMEM((steps, BLOCK, 2 * width), F32)],
        micros=8,
    )[0]

    quarter_out = shaped((quarter, model), BF)
    one_keep0, one_keep1, one_send, entry_norms = run(
        one_grad_kernel,
        ids,
        (kvg, hidden_one, dq, query_weight, key_weight, value_weight, row(entry_gain), row(entry_bias)),
        [quarter_out, quarter_out, shaped((2, *quarter_out.shape), BF), shaped((2, model), F32)],
        micros=3,
    )
    one_sent = partner(one_send, 1)
    entry_rows = run(
        entry_weights_kernel,
        ids,
        (hidden_one, after(dq, one_send), kvg, entry_norms, norm_grads),
        spread_out,
        scratch=[pltpu.VMEM((model, 3 * width + 128), BF)],
        micros=4,
    )
    entry_sum = ShardSum(*entry_rows)
    head_rows = added(head_keep0, head_sent[0], after(head_across, kvg))
    one_half = added(one_keep1, after(one_sent, entry_rows[0])[1])
    one_across = partner(one_half, 2)
    own_pair = added(*text_sum.last(ids, one_half))
    text_out = shaped((prompt_rows * items // shards, width), BF)
    text_keep0, text_keep1, text_send = run(
        text_kernel, ids, (own_pair, prompt_key, prompt_value), [text_out, text_out, shaped((2, *text_out.shape), BF)], micros=1
    )
    text_sent = partner(text_send, 1)
    text_half = added(text_keep1, text_sent[1])
    text_across = partner(text_half, 2)
    one_across = after(one_across, text_half, head_rows, feed_sum)
    head_sum = lax.psum_scatter(after(head_rows, feed_sum), SEQ, scatter_dimension=0, tiled=True)
    grad_rows = run(
        entry_back_kernel,
        ids,
        (one_keep0, one_sent, one_across, tokens, row(entry_gain), resid),
        [wide(BF)],
        in_specs=[None] * 3 + [own_rows(model)] + [None] * 2,
        micros=2,
        vmem=60,
    )[0]
    grad_pieces = gather(grad_rows)

    text_own = added(text_keep0, text_sent[0], after(text_across, grad_rows))
    entry_sum.step(ids, grad_rows)
    prompt_all = to_all(jnp.concatenate([own_pair, text_own], axis=1))
    all_text = items * prompt_rows
    some = min(all_text, 1024)
    key_prompt, value_prompt, text_grad = run(
        prompt_kernel_back,
        None,
        (text_states.reshape(all_text, model), prompt_all),
        [shaped((model, width), F32), shaped((model, width), F32), shaped((all_text, width), F32)],
        grid=(all_text // some,),
        in_specs=[pl.BlockSpec((some, model), lambda i: (i, 0)), pl.BlockSpec((some, 3 * width), lambda i: (i, 0))],
        out_specs=[None, None, pl.BlockSpec((some, width), lambda i: (i, 0))],
        micros=3,
    )
    text_grad = text_grad.reshape(items, prompt_rows, width)

    tokens_grad = assemble(ids, grad_pieces, F32)
    out_rows = added(after_cross, out0, out_sent1, out_across)
    out_pieces = gather(after(out_rows, grad_rows))
    layer_output = assemble(ids, out_pieces, BF)

    part = model // shards
    square, turned_square = shaped((part, width), F32), shaped((width, part), F32)
    expand_grad, shrink_grad, pq_grad, pm_grad, merge_grad, wq_grad, wk_grad, wv_grad, norm_sum = run(
        arrived_kernel,
        None,
        (feed_sum, head_sum, *entry_sum.last(ids, grad_rows)),
        [shaped((part, hidden_units), F32), shaped((hidden_units, part), F32)]
        + [square, turned_square, turned_square, square, square, square, shaped((8, part), F32)],
        micros=3,
    )
    norm_sum = norm_sum + partner(norm_sum, 1)
    norm_sum = norm_sum + partner(norm_sum, 2)
    return (
        layer_output,
        tokens_grad,
        text_grad,
        norm_sum[0],
        norm_sum[1],
        norm_sum[4],
        norm_sum[5],
        norm_sum[2],
        norm_sum[3],
        wq_grad,
        wk_grad,
        wv_grad,
        merge_grad,
        pq_grad,
        key_prompt,
        value_prompt,
        pm_grad,
        expand_grad,
        shrink_grad,
    )


def solution(mesh):
    shards = mesh.shape["seq"]
    mesh = jax.sharding.Mesh(mesh.devices.reshape(shards // 2, 2, mesh.shape["mp"]), (*SEQ, "mp"))
    seq, mp, both = P(SEQ, None), P("mp", None), P(None, "mp")
    return jax.shard_map(
        body,
        mesh=mesh,
        in_specs=(seq,) + (P(),) * 9 + (both,) * 3 + (mp,) + (both,) * 3 + (mp, both, mp, seq),
        out_specs=(
            (seq, seq, P(None, None, "mp"))
            + (P(SEQ),) * 6
            + (P(SEQ, "mp"),) * 3
            + (P("mp", SEQ), P(SEQ, "mp"), both, both, P("mp", SEQ), P(SEQ, "mp"), P("mp", SEQ))
        ),
        check_vma=False,
    )
```
